128 devices in a mesh: ctx: 32 (over z, y, x_hi), head: 4 (over x_lo, core).
Axes of the slice: x: 4 (x_hi: 2, x_lo: 2; x = x_hi * 2 + x_lo), y: 4, z: 4, core: 2. Of those that a mesh axis runs over, the one named last changes fastest.
Arguments:
- q_proj: bfloat16 [8192, 3072], P('ctx', 'head'), may hold values from -6 to 6
- k_proj: bfloat16 [8192, 3072], P('ctx', 'head'), may hold values from -6 to 6
- v_proj: bfloat16 [8192, 3072], P('ctx', 'head'), may hold values from -6 to 6
- out_weight: bfloat16 [3072, 6144], P('head'), may hold values from -1.5 to 1.5
- out_grad: bfloat16 [8192, 6144], P('ctx', 'head'), may hold values from -1.1953125 to 1.1953125
Outputs:
- mixed_out: bfloat16 [8192, 6144], P('ctx', 'head')
- q_grad: bfloat16 [8192, 3072], P('ctx', 'head')
- k_grad: bfloat16 [8192, 3072], P('ctx', 'head')
- v_grad: bfloat16 [8192, 3072], P('ctx', 'head')
The draws below stay inside these ranges and needn't reach their ends.
All inputs are finite; a program needn't handle non-finite values.
Results may differ from the reference program's by a relative error of at most 0.014.
The reference program's roundings to bfloat16 on the way count: a program that leaves them out, or rounds other values in their place, can miss the bound.
Values may be sent and summed in bfloat16 or wider, within the bound.
No kernel may reach another device: no remote copies, remote signals or barrier semaphores. Data moves between devices by JAX's collectives and lax.ppermute only.
A program may use at most 192 MiB of HBM per device.

```python
import math
import jax
import jax.numpy as jnp
from jax import lax

D = 6144
HEADS = 24
HEAD_DIM = 128
SHORT = 4
WINDOW = 1024
TOK_DEV = 256
TOKENS = 8192
COARSE = 2048
N_CTX = 32
N_HEAD = 4


def row_scales(key):
    return jnp.exp(jax.random.uniform(key, (TOKENS, 1), minval=math.log(0.3), maxval=math.log(3.0)))


def draw_q_proj(key, part):
    key = jax.random.fold_in(key, 5)
    key_row, key_value = jax.random.split(key)
    scales = row_scales(key_row)
    values = jnp.clip(jax.random.normal(key_value, (TOKENS, HEADS * HEAD_DIM)), -2.0, 2.0) * scales
    return values.astype(jnp.bfloat16)


def draw_k_proj(key, part):
    key = jax.random.fold_in(key, 7)
    key_row, key_value = jax.random.split(key)
    scales = row_scales(key_row)
    values = jnp.clip(jax.random.normal(key_value, (TOKENS, HEADS * HEAD_DIM)), -2.0, 2.0) * scales
    return values.astype(jnp.bfloat16)


def steps_of(own_key, shape, shards, least, top_value):
    factor_of, own = 1.0, jax.random.fold_in(own_key, 6)
    for axis_at, blocks in shards:
        heights = jnp.exp(jax.random.uniform(jax.random.fold_in(own, axis_at), (blocks,), jnp.float32, least / len(shards), top_value / len(shards)))
        factor_of = factor_of * jnp.repeat(heights, shape[axis_at] // blocks).reshape([-1 if axis == axis_at else 1 for axis in range(len(shape))])
    return factor_of


def normal_values(key, shape, deviation, limit, shards=(), kind=jnp.bfloat16):
    entries = jax.random.normal(key, shape, jnp.float32) * deviation
    if len(shards) > 0:
        entries = steps_of(key, shape, shards, -0.22, 0.18) * entries
    return jnp.clip(entries, min=-limit, max=limit).astype(kind)


def setup_inputs(seed: int = 0) -> dict:
    seeds = jax.random.split(jax.random.key(seed), 6)
    q_proj = draw_q_proj(jax.random.fold_in(seeds[5], 71), 0)
    k_proj = draw_k_proj(jax.random.fold_in(seeds[5], 71), 0)
    v_proj = normal_values(seeds[2], (TOKENS, HEADS * HEAD_DIM), 1.0, 6.0, ((0, 32), (1, 4)))
    out_weight = normal_values(seeds[3], (HEADS * HEAD_DIM, D), 16 ** -0.5, 1.5, ((0, 4),))
    out_grad = normal_values(seeds[4], (TOKENS, D), 0.2, 1.1953125, ((0, 32), (1, 4)))
    return {"q_proj": q_proj, "k_proj": k_proj, "v_proj": v_proj, "out_weight": out_weight, "out_grad": out_grad}


def to_heads(matrix):
    return matrix.reshape(matrix.shape[0], HEADS, HEAD_DIM)

def rounded(matrix):
    return lax.optimization_barrier(matrix.astype(jnp.bfloat16)).astype(jnp.float32)

def pool_rows(matrix):
    padding = jnp.zeros((SHORT - 1, matrix.shape[1]), jnp.float32)
    padded = jnp.concatenate([padding, matrix.astype(jnp.float32)], 0)[:TOKENS]
    return (padded.reshape(COARSE, SHORT, matrix.shape[1]).sum(1) / SHORT).astype(jnp.bfloat16)

def spread_rows(gradient):
    extended = jnp.concatenate([gradient, jnp.zeros((1, gradient.shape[1]), jnp.float32)], 0)
    return jnp.repeat(extended, SHORT, axis=0)[SHORT - 1:SHORT - 1 + TOKENS] / SHORT

def log_totals(scores):
    row_max = lax.optimization_barrier(jnp.max(scores, -1, keepdims=True))
    return row_max + jnp.log(lax.optimization_barrier(jnp.sum(jnp.exp(scores - row_max), -1, keepdims=True)))

def window_block(q_proj, key_padded, value_padded, block):
    start = block * TOK_DEV
    q_block = to_heads(lax.dynamic_slice_in_dim(q_proj, start, TOK_DEV, 0)).astype(jnp.float32)
    k_block = to_heads(lax.dynamic_slice_in_dim(key_padded, start, WINDOW + TOK_DEV, 0)).astype(jnp.float32)
    v_block = to_heads(lax.dynamic_slice_in_dim(value_padded, start, WINDOW + TOK_DEV, 0)).astype(jnp.float32)
    scores = jnp.einsum('thd,shd->hts', q_block, k_block) * (1.0 / math.sqrt(HEAD_DIM))
    query_pos = start + jnp.arange(TOK_DEV, dtype=jnp.int32)[:, None]
    key_pos = start - WINDOW + jnp.arange(WINDOW + TOK_DEV, dtype=jnp.int32)[None, :]
    allowed = (key_pos > query_pos - WINDOW) & (key_pos <= query_pos) & (key_pos >= 0)
    return (q_block, k_block, v_block, jnp.where(allowed[None], scores, -jnp.inf))

def coarse_head(operands):
    q_head, k_head, v_head, grad_head = operands
    coarse_scale = 2.0 / math.sqrt(HEAD_DIM)
    scores = jnp.dot(q_head, k_head.T, preferred_element_type=jnp.float32) * coarse_scale
    positions = jnp.arange(COARSE, dtype=jnp.int32)
    allowed = positions[None, :] <= positions[:, None]
    scores = jnp.where(allowed, scores, -jnp.inf)
    exp_weights = jnp.exp(scores - log_totals(scores))
    weights = exp_weights.astype(jnp.bfloat16)
    output = jnp.dot(weights, v_head, preferred_element_type=jnp.float32)
    delta = lax.optimization_barrier(jnp.sum(grad_head.astype(jnp.float32) * output, -1, keepdims=True))
    grad_prob = jnp.dot(grad_head, v_head.T, preferred_element_type=jnp.float32)
    grad_score = (exp_weights * (grad_prob - delta)).astype(jnp.bfloat16)
    grad_q = jnp.dot(grad_score, k_head, preferred_element_type=jnp.float32) * coarse_scale
    grad_k = jnp.dot(grad_score.T, q_head, preferred_element_type=jnp.float32) * coarse_scale
    grad_v = jnp.dot(weights.T, grad_head, preferred_element_type=jnp.float32)
    return (output, grad_q, grad_k, grad_v)

def reference(q_proj, k_proj, v_proj, out_weight, out_grad):
    head_cols = HEADS * HEAD_DIM
    score_scale = 1.0 / math.sqrt(HEAD_DIM)
    grad_attn = jnp.dot(out_grad, out_weight.T, preferred_element_type=jnp.float32).astype(jnp.bfloat16)
    pooled_q = pool_rows(q_proj)
    pooled_k = pool_rows(k_proj)
    pooled_v = pool_rows(v_proj)
    grad_pooled = grad_attn.astype(jnp.float32).reshape(COARSE, SHORT, head_cols).sum(1).astype(jnp.bfloat16)

    def heads_first(matrix):
        return matrix.reshape(COARSE, HEADS, HEAD_DIM).transpose(1, 0, 2)

    def heads_last(matrix):
        return matrix.transpose(1, 0, 2).reshape(COARSE, head_cols)
    coarse_out, coarse_dq, coarse_dk, coarse_dv = lax.map(coarse_head, (heads_first(pooled_q), heads_first(pooled_k), heads_first(pooled_v), heads_first(grad_pooled)))
    coarse_out = heads_last(coarse_out)
    zero_rows = jnp.zeros((WINDOW, head_cols), jnp.bfloat16)
    key_padded = jnp.concatenate([zero_rows, k_proj], 0)
    value_padded = jnp.concatenate([zero_rows, v_proj], 0)
    blocks = jnp.arange(N_CTX, dtype=jnp.int32)

    def fine_forward(block):
        q_block, k_block, v_block, scores = window_block(q_proj, key_padded, value_padded, block)
        log_total = log_totals(scores)
        weights = rounded(jnp.exp(scores - log_total))
        return (jnp.einsum('hts,shd->thd', weights, v_block), log_total)
    fine_out, fine_lse = lax.map(fine_forward, blocks)
    fine_out = fine_out.reshape(TOKENS, HEADS, HEAD_DIM)
    attn = (fine_out.reshape(TOKENS, head_cols) + jnp.repeat(coarse_out, SHORT, axis=0)).astype(jnp.bfloat16)
    group_cols = head_cols // N_HEAD
    total = jnp.zeros((TOKENS, D), jnp.float32)
    for group in range(N_HEAD):
        lower = group * group_cols
        product = jnp.dot(attn[:, lower:lower + group_cols], out_weight[lower:lower + group_cols], preferred_element_type=jnp.float32)
        total = total + rounded(product)
    mixed_out = total.astype(jnp.bfloat16)
    fine_delta = lax.optimization_barrier(jnp.sum(to_heads(grad_attn).astype(jnp.float32) * fine_out, -1))

    def fine_backward(carry, block):
        key_acc, value_acc = carry
        start = block * TOK_DEV
        q_block, k_block, v_block, scores = window_block(q_proj, key_padded, value_padded, block)
        exp_weights = jnp.exp(scores - fine_lse[block])
        weights = rounded(exp_weights)
        grad_block = to_heads(lax.dynamic_slice_in_dim(grad_attn, start, TOK_DEV, 0)).astype(jnp.float32)
        delta_block = lax.dynamic_slice_in_dim(fine_delta, start, TOK_DEV, 0).T[:, :, None]
        grad_prob = jnp.einsum('thd,shd->hts', grad_block, v_block)
        grad_score = rounded(exp_weights * (grad_prob - delta_block))
        grad_q = jnp.einsum('hts,shd->thd', grad_score, k_block) * score_scale
        grad_k = jnp.einsum('hts,thd->shd', grad_score, q_block) * score_scale
        grad_v = jnp.einsum('hts,thd->shd', weights, grad_block)
        reach = WINDOW + TOK_DEV
        key_acc = lax.dynamic_update_slice_in_dim(key_acc, lax.dynamic_slice_in_dim(key_acc, start, reach, 0) + grad_k, start, 0)
        value_acc = lax.dynamic_update_slice_in_dim(value_acc, lax.dynamic_slice_in_dim(value_acc, start, reach, 0) + grad_v, start, 0)
        return ((key_acc, value_acc), grad_q)
    zero_acc = jnp.zeros((WINDOW + TOKENS, HEADS, HEAD_DIM), jnp.float32)
    (key_acc, value_acc), fine_dq = lax.scan(fine_backward, (zero_acc, zero_acc), blocks)
    fine_dq = fine_dq.reshape(TOKENS, head_cols)
    fine_dk = key_acc[WINDOW:].reshape(TOKENS, head_cols)
    fine_dv = value_acc[WINDOW:].reshape(TOKENS, head_cols)
    q_grad = (fine_dq + spread_rows(heads_last(coarse_dq))).astype(jnp.bfloat16)
    k_grad = (fine_dk + spread_rows(heads_last(coarse_dk))).astype(jnp.bfloat16)
    v_grad = (fine_dv + spread_rows(heads_last(coarse_dv))).astype(jnp.bfloat16)
    return (mixed_out, q_grad, k_grad, v_grad)
```

```python
import functools
import math

import jax
import jax.numpy as jnp
import numpy as np
from jax import lax
from jax.experimental import pallas as pl
from jax.experimental.pallas import tpu as pltpu
from jax.sharding import Mesh, PartitionSpec as P

HEAD_DIM = 128
SHORT = 4
WINDOW = 1024
PLANES = 4
PLANE_DEVS = 8
BLOCK = 256
TAIL = 16
LOG2E = math.log2(math.e)
SCALE = 1.0 / math.sqrt(HEAD_DIM)
COARSE_SCALE = 2.0 * SCALE
FAR = -1e30
PLANE = ("y", "xh")
bf16 = jnp.bfloat16
f32 = jnp.float32


def call(kernel, out_shape, vmem_mib, **rest):
    return pl.pallas_call(
        kernel,
        out_shape=out_shape,
        compiler_params=pltpu.CompilerParams(vmem_limit_bytes=vmem_mib * 1024 * 1024),
        **rest,
    )


def dot(a, b):
    return jnp.dot(a, b, preferred_element_type=f32)


def dot_nt(a, b):
    return lax.dot_general(a, b, (((1,), (1,)), ((), ())), preferred_element_type=f32)


def iota(shape, dim):
    return lax.broadcasted_iota(jnp.int32, shape, dim)


def split(x):
    high = x.astype(bf16)
    return high, (x - high.astype(f32)).astype(bf16)


def ones_where(mask):
    return jnp.where(mask, 1.0, 0.0).astype(bf16)


def pack_kernel(q_ref, k_ref, v_ref, out_ref, sems):
    tokens = q_ref.shape[0]
    last = q_ref.shape[1] // HEAD_DIM - 1
    copies = []
    for slot in range(PLANE_DEVS):
        cols = pl.ds(min(slot, last) * HEAD_DIM, HEAD_DIM)
        tail = q_ref.at[tokens - TAIL :, cols]
        pieces = (
            (k_ref.at[:, cols], out_ref.at[slot, 0:tokens, 0:128]),
            (v_ref.at[:, cols], out_ref.at[slot, 0:tokens, 128:256]),
            (tail, out_ref.at[slot, tokens:, 0:128]),
            (tail, out_ref.at[slot, tokens:, 128:256]),
        )
        for at, (source, target) in enumerate(pieces):
            copies.append(pltpu.make_async_copy(source, target, sems.at[slot, at]))
    for copy in copies:
        copy.start()
    for copy in copies:
        copy.wait()


def pooling(lead):
    shape = (BLOCK // SHORT, BLOCK + lead)
    back = iota(shape, 1) - lead - SHORT * iota(shape, 0)
    return ones_where((back <= 0) & (back > -SHORT))


def spreading():
    shape = (BLOCK, BLOCK // SHORT + TAIL)
    return ones_where((iota(shape, 0) + (SHORT - 1)) // SHORT == iota(shape, 1))


def pooled_rows(block, lead=None):
    rows = block if lead is None else jnp.concatenate([lead, block], 0)
    taken = pooling(0 if lead is None else TAIL)
    return (dot(taken, rows) * (1.0 / SHORT)).astype(bf16)


def pool_kernel(x_ref, after_ref, near_ref, far_ref):
    del after_ref
    devs, tokens = x_ref.shape[0], x_ref.shape[1] - TAIL
    step = tokens // SHORT
    half = WINDOW // SHORT
    coarse = devs * step
    for slot in range(devs):
        block = x_ref[slot, 0:tokens, :]
        lead = x_ref[slot - 1, tokens - TAIL : tokens, :] if slot else None
        far_ref[slot * step : (slot + 1) * step, :] = pooled_rows(block, lead)
        late = slot * tokens - (devs * tokens - WINDOW)
        if late >= 0:
            near_ref[late : late + tokens, :] = block
    far_ref[coarse : coarse + TAIL, :] = x_ref[devs - 1, tokens - TAIL : tokens, :]
    near_ref[WINDOW : WINDOW + TAIL, :] = x_ref[devs - 1, tokens:, :]
    near_ref[WINDOW + TAIL :, :] = far_ref[0 : half + TAIL, :]


def first_row_fixed(pooled, tail):
    kept = jnp.where(iota(tail.shape, 0) > TAIL - SHORT, tail.astype(f32), 0.0)
    lacking = jnp.sum(kept, 0, keepdims=True) * (1.0 / SHORT)
    head = pooled[0:TAIL, :].astype(f32)
    return jnp.where(iota(head.shape, 0) == 0, head + lacking, head).astype(bf16)


def attention_kernel(
    z_ref,
    x_ref,
    own_ref,
    near_ref,
    far2_ref,
    far3_ref,
    pair_ref,
    attn_ref,
    fine_ref,
    coarse_ref,
    back1_ref,
    back2_ref,
    back3_ref,
    kx,
    vx,
    kxt,
    vxt,
    kc,
    vc,
    kct,
    vct,
    pq,
    gp,
    dkx,
    dvx,
    dkc,
    dvc,
    high_t,
    low_t,
    high,
    low,
    query_high,
    query_low,
):
    z = z_ref[0]
    rows = pair_ref.shape[0]
    tokens = rows // PLANE_DEVS
    coarse = rows // SHORT
    half = WINDOW // SHORT
    step = BLOCK // SHORT
    span = WINDOW + BLOCK
    reach = WINDOW // BLOCK

    kx[0:WINDOW, :] = near_ref[0:WINDOW, 0:128]
    vx[0:WINDOW, :] = near_ref[0:WINDOW, 128:256]
    for slot in range(PLANE_DEVS):
        at = WINDOW + slot * tokens
        kx[at : at + tokens, :] = x_ref[slot, 0:tokens, 0:128]
        vx[at : at + tokens, :] = x_ref[slot, 0:tokens, 128:256]

    def transposed(ref, out, count):
        def body(i, carry):
            at = pl.multiple_of(i * BLOCK, BLOCK)
            out[:, pl.ds(at, BLOCK)] = ref[pl.ds(at, BLOCK), :].T
            return carry

        lax.fori_loop(0, count, body, 0)

    transposed(kx, kxt, (WINDOW + rows) // BLOCK)
    transposed(vx, vxt, (WINDOW + rows) // BLOCK)

    tails = [
        near_ref[WINDOW - TAIL : WINDOW, :],
        far2_ref[coarse : coarse + TAIL, :],
        far3_ref[coarse : coarse + TAIL, :],
    ]
    base = WINDOW + TAIL
    for piece in range(reach):
        at = coarse + half + piece * step
        block = near_ref[piece * BLOCK : (piece + 1) * BLOCK, :]
        lead = near_ref[piece * BLOCK - TAIL : piece * BLOCK, :] if piece else None
        rest = pooled_rows(block, lead)
        kc[at : at + step, :] = rest[:, 0:128]
        vc[at : at + step, :] = rest[:, 128:256]
    sources = ((own_ref, coarse), (near_ref.at[base:], half + TAIL), (far2_ref, coarse), (far3_ref, coarse))
    for slot, (source, count) in enumerate(sources):
        at = slot * coarse
        kc[at : at + count, :] = source[0:count, 0:128]
        vc[at : at + count, :] = source[0:count, 128:256]
        if slot + 1 < PLANES:
            fixed = first_row_fixed(source[0:TAIL, :], tails[slot])
            kc[at : at + TAIL, :] = fixed[:, 0:128]
            vc[at : at + TAIL, :] = fixed[:, 128:256]
    transposed(kc, kct, PLANES * coarse // BLOCK)
    transposed(vc, vct, PLANES * coarse // BLOCK)

    shape = (step, BLOCK)
    offset = iota(shape, 1) - SHORT * iota(shape, 0)
    taken = ones_where((offset >= 0) & (offset < SHORT))
    for block in range(rows // BLOCK):
        at = block * BLOCK
        lead = pair_ref[at - TAIL : at, 0:128] if block else near_ref[WINDOW : WINDOW + TAIL, 0:128]
        pq[block * step : (block + 1) * step, :] = pooled_rows(pair_ref[at : at + BLOCK, 0:128], lead)
        gp[block * step : (block + 1) * step, :] = dot(
            taken, pair_ref[at : at + BLOCK, 128:256]
        ).astype(bf16)

    def weights(scores, biases, factor):
        tops = [jnp.max(s, 0, keepdims=True) + b for s, b in zip(scores, biases)]
        top = functools.reduce(jnp.maximum, tops)
        exps = [jnp.exp2((s - (top - b)) * factor) for s, b in zip(scores, biases)]
        total = functools.reduce(jnp.add, [jnp.sum(e, 0, keepdims=True) for e in exps])
        inverse = 1.0 / total
        return jnp.concatenate([e * inverse for e in exps], 0)

    row_at, col_at = iota((BLOCK, BLOCK), 0), iota((BLOCK, BLOCK), 1)
    diagonal = row_at <= col_at
    for block in range(coarse // BLOCK):
        at = block * BLOCK
        query = pq[at : at + BLOCK, :]
        grad = gp[at : at + BLOCK, :]
        scores, biases, keys, values = [], [], [], []
        for piece in range(block + 1):
            s = dot_nt(kc[piece * BLOCK : (piece + 1) * BLOCK, :], query)
            scores.append(jnp.where(diagonal, s, FAR) if piece == block else s)
            biases.append(0.0)
        for slot in range(1, PLANES):
            s = dot_nt(kc[slot * coarse : (slot + 1) * coarse, :], query)
            scores.append(s)
            biases.append(jnp.where(z >= slot, 0.0, FAR))
        probs = weights(scores, biases, COARSE_SCALE * LOG2E)
        rounded = probs.astype(bf16)
        own = at + BLOCK
        parts = ((0, own, 0), (coarse, PLANES * coarse, own))
        out_t = functools.reduce(
            jnp.add, [dot(vct[:, a:b], rounded[c : c + b - a]) for a, b, c in parts]
        )
        grad_t = grad.astype(f32).T
        delta = jnp.sum(grad_t * out_t, 0, keepdims=True)
        high_t[:, at : at + BLOCK], low_t[:, at : at + BLOCK] = split(out_t)
        query_grad_t = jnp.zeros((HEAD_DIM, BLOCK), f32)
        for a, b, c in parts:
            grad_probs = dot_nt(vc[a:b, :], grad)
            grad_scores = (probs[c : c + b - a] * (grad_probs - delta)).astype(bf16)
            query_grad_t += dot(kct[:, a:b], grad_scores)
            dk = dot(grad_scores, query) * COARSE_SCALE
            dv = dot(rounded[c : c + b - a], grad)
            if block == 0:
                dkc[a:b, :] = dk
                dvc[a:b, :] = dv
                if a == 0:
                    dkc[b:coarse, :] = jnp.zeros((coarse - b, HEAD_DIM), f32)
                    dvc[b:coarse, :] = jnp.zeros((coarse - b, HEAD_DIM), f32)
            else:
                dkc[a:b, :] += dk
                dvc[a:b, :] += dv
        query_grad = query_grad_t.T * COARSE_SCALE
        query_high[at : at + BLOCK, :], query_low[at : at + BLOCK, :] = split(query_grad)
    query_high[coarse:, :] = jnp.zeros((TAIL, HEAD_DIM), bf16)
    query_low[coarse:, :] = jnp.zeros((TAIL, HEAD_DIM), bf16)
    coarse_ref[:, 0:128] = dkc[0:coarse, :]
    coarse_ref[:, 128:256] = dvc[0:coarse, :]

    dkx[...] = jnp.zeros_like(dkx)
    dvx[...] = jnp.zeros_like(dvx)

    def window(block, carry):
        at = pl.multiple_of(block * BLOCK, BLOCK)
        query = pair_ref[pl.ds(at, BLOCK), 0:128]
        grad = pair_ref[pl.ds(at, BLOCK), 128:256]
        scores, biases = [], []
        for piece in range(reach + 1):
            key = kx[pl.ds(pl.multiple_of(at + piece * BLOCK, BLOCK), BLOCK), :]
            s = dot_nt(key, query)
            if piece == 0:
                s = jnp.where(row_at > col_at, s, FAR)
            if piece == reach:
                s = jnp.where(diagonal, s, FAR)
            scores.append(s)
            biases.append(jnp.where((z == 0) & (block + piece < reach), FAR, 0.0))
        probs = weights(scores, biases, SCALE * LOG2E)
        rounded = probs.astype(bf16)
        out_t = dot(vxt[:, pl.ds(at, span)], rounded)
        grad_t = grad.astype(f32).T
        delta = jnp.sum(grad_t * out_t, 0, keepdims=True)
        pair = pl.multiple_of(block // 2 * (2 * step), 2 * step)
        shape = (2 * step, BLOCK)
        spread = ones_where(iota(shape, 0) == block % 2 * step + iota(shape, 1) // SHORT)
        short_t = dot(high_t[:, pl.ds(pair, 2 * step)], spread)
        short_t += dot(low_t[:, pl.ds(pair, 2 * step)], spread)
        attn_ref[pl.ds(at, BLOCK), 0:128] = (out_t + short_t).T.astype(bf16)
        grad_probs = dot_nt(vx[pl.ds(at, span), :], grad)
        grad_scores = (probs * (grad_probs - delta)).astype(bf16)
        query_grad = dot(kxt[:, pl.ds(at, span)], grad_scores).T * SCALE
        below = pl.ds(pl.multiple_of(block * step, step), step + TAIL)
        spread = dot(spreading(), query_high[below, :]) + dot(spreading(), query_low[below, :])
        query_grad += spread * (1.0 / SHORT)
        attn_ref[pl.ds(at, BLOCK), 128:256] = query_grad.astype(bf16)
        dkx[pl.ds(at, span), :] += dot(grad_scores, query)
        dvx[pl.ds(at, span), :] += dot(rounded, grad)
        return carry

    lax.fori_loop(0, rows // BLOCK, window, 0, unroll=8)
    fine_ref[:, 0:128] = dkx[WINDOW:, :] * SCALE
    fine_ref[:, 128:256] = dvx[WINDOW:, :]

    first = iota((TAIL, HEAD_DIM), 0) == 0
    for cols, short in ((slice(0, 128), dkc), (slice(128, 256), dvc)):
        high[0:half, cols], low[0:half, cols] = split(short[2 * coarse - half : 2 * coarse, :])
        above = jnp.where(first, short[0:TAIL, :], 0.0)
        high[half:, cols], low[half:, cols] = split(above)
    taken = spreading()
    for piece in range(reach):
        at = piece * BLOCK
        below = piece * step
        spread = dot(taken, high[below : below + step + TAIL, :])
        spread += dot(taken, low[below : below + step + TAIL, :])
        spread = spread * (1.0 / SHORT)
        back1_ref[at : at + BLOCK, 0:128] = (
            dkx[at : at + BLOCK, :] * SCALE + spread[:, 0:128]
        ).astype(bf16)
        back1_ref[at : at + BLOCK, 128:256] = (
            dvx[at : at + BLOCK, :] + spread[:, 128:256]
        ).astype(bf16)
    query_row = jnp.where(first, query_high[0:TAIL, :].astype(f32), 0.0).astype(bf16)
    back1_ref[WINDOW:base, 0:128] = query_row
    back1_ref[WINDOW:base, 128:256] = query_row
    back1_ref[base:, 0:128] = dkc[coarse : coarse + half + TAIL, :].astype(bf16)
    back1_ref[base:, 128:256] = dvc[coarse : coarse + half + TAIL, :].astype(bf16)
    for slot, ref in ((2, back2_ref), (3, back3_ref)):
        at = slot * coarse
        above = at - coarse
        for cols, short in ((slice(0, 128), dkc), (slice(128, 256), dvc)):
            ref[0:coarse, cols] = short[at : at + coarse, :].astype(bf16)
            row = jnp.where(first, short[above : above + TAIL, :], 0.0)
            ref[coarse : coarse + TAIL, cols] = row.astype(bf16)


def finish_kernel(fine_ref, coarse_ref, back1_ref, back2_ref, back3_ref, out_ref, high, low):
    rows = fine_ref.shape[0]
    tokens = rows // PLANE_DEVS
    coarse = rows // SHORT
    half = coarse - WINDOW // SHORT
    step = BLOCK // SHORT
    base = WINDOW + TAIL
    part = half + TAIL
    ups = (back2_ref, back3_ref)
    total = coarse_ref[...]
    for up in ups:
        total += up[0:coarse, :].astype(f32)
    near = total[0:part, :] + back1_ref[base:, :].astype(f32)
    high[0:part, :], low[0:part, :] = split(near)
    high[part : part + half, :], low[part : part + half, :] = split(total[half:, :])
    extra = functools.reduce(jnp.add, [up[coarse : coarse + TAIL, :].astype(f32) for up in ups])
    high[part + half :, :], low[part + half :, :] = split(extra)
    taken = spreading()
    for block in range(rows // BLOCK):
        at = block * BLOCK
        late = at - (rows - WINDOW)
        below = block * step if late < 0 else part + late // SHORT
        spread = dot(taken, high[below : below + step + TAIL, :])
        spread += dot(taken, low[below : below + step + TAIL, :])
        result = fine_ref[at : at + BLOCK, :] + spread * (1.0 / SHORT)
        if late >= 0:
            result = result + back1_ref[late : late + BLOCK, :].astype(f32)
        out_ref[block, 0:tokens, :] = result.astype(bf16)
        out_ref[block, tokens:, :] = jnp.zeros((TAIL, 256), bf16)
    out_ref[PLANE_DEVS - 1, tokens:, :] = back1_ref[WINDOW:base, :]


def unpack_kernel(pair_ref, x_ref, q_ref, k_ref, v_ref):
    tokens = q_ref.shape[0]
    last = iota((TAIL, HEAD_DIM), 0) > TAIL - SHORT
    for slot in range(q_ref.shape[1] // HEAD_DIM):
        cols = pl.ds(slot * HEAD_DIM, HEAD_DIM)
        k_ref[:, cols] = x_ref[slot, 0:tokens, 0:128]
        v_ref[:, cols] = x_ref[slot, 0:tokens, 128:256]
        q_ref[0 : tokens - TAIL, cols] = pair_ref[slot, 0 : tokens - TAIL, 128:256]
        above = jnp.sum(x_ref[slot, tokens:, 0:128].astype(f32), 0, keepdims=True) * (1.0 / SHORT)
        rest = pair_ref[slot, tokens - TAIL :, 128:256].astype(f32)
        q_ref[tokens - TAIL :, cols] = (rest + jnp.where(last, above, 0.0)).astype(bf16)


def grad_product(halves, a_ref, b_ref, w_ref, total, start):
    at = pl.program_id(0)
    depth = w_ref.shape[1]
    for piece, ref in enumerate((a_ref, b_ref)):
        for half in range(halves):

            @pl.when(at == piece * halves + half)
            def _():
                product = dot_nt(w_ref[...], ref[:, half * depth : (half + 1) * depth])
                if piece + half > 0:
                    total[...] += product
                elif start is None:
                    total[...] = product
                else:
                    total[...] = start[...] + product


def grad_near_kernel(halves, order_ref, a_ref, b_ref, w_ref, total):
    grad_product(halves, a_ref, b_ref, w_ref, total, None)


def grad_far_kernel(halves, order_ref, a_ref, b_ref, w_ref, start, q_ref, out_ref, total):
    grad_product(halves, a_ref, b_ref, w_ref, total, start)

    @pl.when(pl.program_id(0) == pl.num_programs(0) - 1)
    def _():
        last = total.shape[0] // HEAD_DIM - 1
        for slot in range(PLANE_DEVS):
            head = slice(min(slot, last) * HEAD_DIM, (min(slot, last) + 1) * HEAD_DIM)
            out_ref[slot, :, 0:128] = q_ref[:, head]
            out_ref[slot, :, 128:256] = total[head, :].T.astype(bf16)


def grad_part(pieces, order, weight, rest=()):
    rows, width = pieces[0].shape
    depth = weight.shape[0]
    halves = 1
    tile = width // halves

    first = 2 if rest else 0

    def whole(shape):
        return pl.BlockSpec(shape, lambda i, o: (0,) * len(shape))

    packed = (PLANE_DEVS, rows, 2 * HEAD_DIM)
    return pl.pallas_call(
        functools.partial(grad_far_kernel if rest else grad_near_kernel, halves),
        out_shape=jax.ShapeDtypeStruct(packed, bf16) if rest else jax.ShapeDtypeStruct((depth, rows), f32),
        grid_spec=pltpu.PrefetchScalarGridSpec(
            num_scalar_prefetch=1,
            grid=(2 * halves,),
            in_specs=[whole((rows, width))] * 2
            + [pl.BlockSpec((depth, tile), lambda i, o: (0, o[first + i // halves] * halves + i % halves))]
            + [whole(x.shape) for x in rest],
            out_specs=whole(packed if rest else (depth, rows)),
            scratch_shapes=[pltpu.VMEM((depth, rows), f32)] if rest else [],
        ),
        compiler_params=pltpu.CompilerParams(vmem_limit_bytes=62 * 1024 * 1024),
    )(order, *pieces, weight, *rest)


def project_kernel(halves, order_ref, attn_ref, w_ref, *refs):
    send_ref, keep_ref, rows_ref = refs[-3:]
    at = pl.program_id(0)
    heads = w_ref.shape[0] // HEAD_DIM
    tile = w_ref.shape[1]

    @pl.when(at == 0)
    def _():
        for slot in range(heads):
            rows_ref[:, slot * HEAD_DIM : (slot + 1) * HEAD_DIM] = attn_ref[slot, :, 0:128]

    product = dot(rows_ref[...], w_ref[...]).astype(bf16)
    for half in range(halves):

        @pl.when(at == half)
        def _():
            send_ref[:, half * tile : (half + 1) * tile] = product

        @pl.when(at == halves + half)
        def _():
            keep_ref[:, half * tile : (half + 1) * tile] = product


def project(attn, order, last, weight, width, after):
    rows = attn.shape[1]
    depth = weight.shape[0]
    halves = 1
    tile = width // halves
    out = jax.ShapeDtypeStruct((rows, width), bf16)
    return pl.pallas_call(
        functools.partial(project_kernel, halves),
        out_shape=(out, out),
        grid_spec=pltpu.PrefetchScalarGridSpec(
            num_scalar_prefetch=1,
            grid=(2 * halves,),
            in_specs=[
                pl.BlockSpec(attn.shape, lambda i, o: (0, 0, 0)),
                pl.BlockSpec((depth, tile), lambda i, o: (0, o[last - i // halves] * halves + i % halves)),
            ]
            + [pl.BlockSpec(memory_space=pltpu.HBM)] * len(after),
            out_specs=[pl.BlockSpec((rows, width), lambda i, o: (0, 0))] * 2,
            scratch_shapes=[pltpu.VMEM((rows, depth), bf16)],
        ),
        compiler_params=pltpu.CompilerParams(vmem_limit_bytes=62 * 1024 * 1024),
    )(order, attn, weight, *after)


def swap(x, axis):
    return lax.ppermute(x, axis, [(0, 1), (1, 0)])


def planes_up(x, by):
    return lax.ppermute(x, "z", [(i, i + by) for i in range(PLANES) if 0 <= i + by < PLANES])


def in_plane(x):
    return lax.all_to_all(x, PLANE, 0, 0, tiled=True)


def column_blocks():
    xl, core = lax.axis_index("xl"), lax.axis_index("c")
    own, other = 2 * xl, 2 * (1 - xl)
    return jnp.stack([own + core, own + 1 - core, other + core, other + 1 - core]).astype(jnp.int32)


def gathered_grad(out_grad, out_weight, q_proj, blocks):
    far = swap(out_grad, "xl")
    near = swap(out_grad, "c")
    start = grad_part((out_grad, near), blocks, out_weight)
    far, start = lax.optimization_barrier((far, start))
    both = swap(far, "c")
    return start, grad_part((far, both), blocks, out_weight, (start, q_proj))


def projected(attn, out_weight, width, blocks, after):
    def share(last, attn):
        send, keep = project(attn, blocks, last, out_weight, width, after)
        return keep.astype(f32) + swap(send, "c").astype(f32)

    part = share(3, attn).astype(bf16)
    part, attn = lax.optimization_barrier((part, attn))
    far = swap(part, "xl")
    return (share(1, attn) + far.astype(f32)).astype(bf16)


def shards(q_proj, k_proj, v_proj, out_weight, out_grad):
    tokens, cols = q_proj.shape
    rows = tokens * PLANE_DEVS
    coarse = rows // SHORT
    total = PLANES * coarse
    z = lax.axis_index("z").astype(jnp.int32).reshape(1)

    def array(*shape, dtype=bf16):
        return jax.ShapeDtypeStruct(shape, dtype)

    in_place = pl.BlockSpec(memory_space=pltpu.HBM)
    whole = pl.BlockSpec(memory_space=pltpu.VMEM)
    packed = call(
        pack_kernel,
        array(PLANE_DEVS, tokens + TAIL, 2 * HEAD_DIM),
        62,
        in_specs=[in_place] * 3,
        out_specs=whole,
        scratch_shapes=[pltpu.SemaphoreType.DMA((PLANE_DEVS, 4))],
    )(q_proj, k_proj, v_proj)
    own = in_plane(packed)
    blocks = column_blocks()
    early, pair_packed = gathered_grad(out_grad, out_weight, q_proj, blocks)
    near_rows = WINDOW + 2 * TAIL + WINDOW // SHORT
    near, far = call(
        pool_kernel,
        (array(near_rows, 256), array(coarse + TAIL, 256)),
        16,
        in_specs=[whole, in_place],
    )(own, early)
    near_in = planes_up(near, 1)
    far3_in = lax.ppermute(far, "z", [(0, 3), (1, 0)])
    far2_in = lax.ppermute(far3_in, "z", [(3, 2), (0, 3)])
    pair = in_plane(pair_packed).reshape(rows, 2 * HEAD_DIM)

    attn, fine, short, back1, back2, back3 = call(
        attention_kernel,
        (
            array(rows, 256),
            array(rows, 256, dtype=f32),
            array(coarse, 256, dtype=f32),
            array(near_rows, 256),
            array(coarse + TAIL, 256),
            array(coarse + TAIL, 256),
        ),
        62,
        in_specs=[pl.BlockSpec(memory_space=pltpu.SMEM)] + [whole] * 6,
        out_specs=[whole] * 6,
        scratch_shapes=[
            pltpu.VMEM((WINDOW + rows, HEAD_DIM), bf16),
            pltpu.VMEM((WINDOW + rows, HEAD_DIM), bf16),
            pltpu.VMEM((HEAD_DIM, WINDOW + rows), bf16),
            pltpu.VMEM((HEAD_DIM, WINDOW + rows), bf16),
            pltpu.VMEM((total, HEAD_DIM), bf16),
            pltpu.VMEM((total, HEAD_DIM), bf16),
            pltpu.VMEM((HEAD_DIM, total), bf16),
            pltpu.VMEM((HEAD_DIM, total), bf16),
            pltpu.VMEM((coarse, HEAD_DIM), bf16),
            pltpu.VMEM((coarse, HEAD_DIM), bf16),
            pltpu.VMEM((WINDOW + rows, HEAD_DIM), f32),
            pltpu.VMEM((WINDOW + rows, HEAD_DIM), f32),
            pltpu.VMEM((total, HEAD_DIM), f32),
            pltpu.VMEM((total, HEAD_DIM), f32),
            pltpu.VMEM((HEAD_DIM, coarse), bf16),
            pltpu.VMEM((HEAD_DIM, coarse), bf16),
            pltpu.VMEM((WINDOW // SHORT + TAIL, 256), bf16),
            pltpu.VMEM((WINDOW // SHORT + TAIL, 256), bf16),
            pltpu.VMEM((coarse + TAIL, HEAD_DIM), bf16),
            pltpu.VMEM((coarse + TAIL, HEAD_DIM), bf16),
        ],
    )(z, own, far, near_in, far2_in, far3_in, pair)

    back1_in = planes_up(back1, -1)
    halfway = lax.ppermute(back2, "z", [(3, 0), (2, 3)])
    back3_in = lax.ppermute(back3, "z", [(3, 0)])
    back2_in = lax.ppermute(halfway, "z", [(0, 1), (3, 0)])
    attn_in = in_plane(attn.reshape(PLANE_DEVS, tokens, 256))
    finished = call(
        finish_kernel,
        array(PLANE_DEVS, tokens + TAIL, 256),
        32,
        scratch_shapes=[
            pltpu.VMEM((coarse + 2 * TAIL, 256), bf16),
            pltpu.VMEM((coarse + 2 * TAIL, 256), bf16),
        ],
    )(fine, short, back1_in, back2_in, back3_in)
    mixed_out = projected(
        attn_in, out_weight, out_grad.shape[1], blocks, (finished,)
    )
    returned = in_plane(finished)
    grads = call(unpack_kernel, (array(tokens, cols),) * 3, 16)(attn_in, returned)
    return (mixed_out, *grads)


def solution(mesh):
    fine_mesh = Mesh(np.asarray(mesh.devices).reshape(4, 4, 2, 2, 2), ("z", "y", "xh", "xl", "c"))
    both = P(("z", "y", "xh"), ("xl", "c"))
    in_specs = (both, both, both, P(("xl", "c"), None), both)
    return jax.shard_map(
        shards, mesh=fine_mesh, in_specs=in_specs, out_specs=(both,) * 4, check_vma=False
    )
```

```python
import functools
import math

import jax
import jax.numpy as jnp
import numpy as np
from jax import lax
from jax.experimental import pallas as pl
from jax.experimental.pallas import tpu as pltpu
from jax.sharding import Mesh, PartitionSpec as P

HEAD_DIM = 128
SHORT = 4
WINDOW = 1024
PLANES = 4
PLANE_DEVS = 8
BLOCK = 256
TAIL = 16
LOG2E = math.log2(math.e)
SCALE = 1.0 / math.sqrt(HEAD_DIM)
COARSE_SCALE = 2.0 * SCALE
FAR = -1e30
PLANE = ("y", "xh")
bf16 = jnp.bfloat16
f32 = jnp.float32


def call(kernel, out_shape, vmem_mib, **rest):
    return pl.pallas_call(
        kernel,
        out_shape=out_shape,
        compiler_params=pltpu.CompilerParams(vmem_limit_bytes=vmem_mib * 1024 * 1024),
        **rest,
    )


def dot(a, b):
    return jnp.dot(a, b, preferred_element_type=f32)


def dot_nt(a, b):
    return lax.dot_general(a, b, (((1,), (1,)), ((), ())), preferred_element_type=f32)


def iota(shape, dim):
    return lax.broadcasted_iota(jnp.int32, shape, dim)


def split(x):
    high = x.astype(bf16)
    return high, (x - high.astype(f32)).astype(bf16)


def ones_where(mask):
    return jnp.where(mask, 1.0, 0.0).astype(bf16)


def pack_kernel(q_ref, k_ref, v_ref, out_ref, sems):
    tokens = q_ref.shape[0]
    last = q_ref.shape[1] // HEAD_DIM - 1
    copies = []
    for slot in range(PLANE_DEVS):
        cols = pl.ds(min(slot, last) * HEAD_DIM, HEAD_DIM)
        tail = q_ref.at[tokens - TAIL :, cols]
        pieces = (
            (k_ref.at[:, cols], out_ref.at[slot, 0:tokens, 0:128]),
            (v_ref.at[:, cols], out_ref.at[slot, 0:tokens, 128:256]),
            (tail, out_ref.at[slot, tokens:, 0:128]),
            (tail, out_ref.at[slot, tokens:, 128:256]),
        )
        for at, (source, target) in enumerate(pieces):
            copies.append(pltpu.make_async_copy(source, target, sems.at[slot, at]))
    for copy in copies:
        copy.start()
    for copy in copies:
        copy.wait()


def pooling(lead):
    shape = (BLOCK // SHORT, BLOCK + lead)
    back = iota(shape, 1) - lead - SHORT * iota(shape, 0)
    return ones_where((back <= 0) & (back > -SHORT))


def spreading():
    shape = (BLOCK, BLOCK // SHORT + TAIL)
    return ones_where((iota(shape, 0) + (SHORT - 1)) // SHORT == iota(shape, 1))


def pooled_rows(block, lead=None):
    rows = block if lead is None else jnp.concatenate([lead, block], 0)
    taken = pooling(0 if lead is None else TAIL)
    return (dot(taken, rows) * (1.0 / SHORT)).astype(bf16)


def pool_kernel(x_ref, after_ref, near_ref, far_ref):
    del after_ref
    devs, tokens = x_ref.shape[0], x_ref.shape[1] - TAIL
    step = tokens // SHORT
    half = WINDOW // SHORT
    coarse = devs * step
    for slot in range(devs):
        block = x_ref[slot, 0:tokens, :]
        lead = x_ref[slot - 1, tokens - TAIL : tokens, :] if slot else None
        far_ref[slot * step : (slot + 1) * step, :] = pooled_rows(block, lead)
        late = slot * tokens - (devs * tokens - WINDOW)
        if late >= 0:
            near_ref[late : late + tokens, :] = block
    far_ref[coarse : coarse + TAIL, :] = x_ref[devs - 1, tokens - TAIL : tokens, :]
    near_ref[WINDOW : WINDOW + TAIL, :] = x_ref[devs - 1, tokens:, :]
    near_ref[WINDOW + TAIL :, :] = far_ref[0 : half + TAIL, :]


def first_row_fixed(pooled, tail):
    kept = jnp.where(iota(tail.shape, 0) > TAIL - SHORT, tail.astype(f32), 0.0)
    lacking = jnp.sum(kept, 0, keepdims=True) * (1.0 / SHORT)
    head = pooled[0:TAIL, :].astype(f32)
    return jnp.where(iota(head.shape, 0) == 0, head + lacking, head).astype(bf16)


def transposed(ref, out, count):
    def body(i, carry):
        at = pl.multiple_of(i * BLOCK, BLOCK)
        out[:, pl.ds(at, BLOCK)] = ref[pl.ds(at, BLOCK), :].T
        return carry

    lax.fori_loop(0, count, body, 0)


def weights(scores, biases, factor):
    tops = [jnp.max(s, 0, keepdims=True) + b for s, b in zip(scores, biases)]
    top = functools.reduce(jnp.maximum, tops)
    exps = [jnp.exp2((s - (top - b)) * factor) for s, b in zip(scores, biases)]
    total = functools.reduce(jnp.add, [jnp.sum(e, 0, keepdims=True) for e in exps])
    inverse = 1.0 / total
    return jnp.concatenate([e * inverse for e in exps], 0)


def window_block(at, query, grad, biases, kx, vx, kxt, vxt, dk, dv):
    span = WINDOW + BLOCK
    reach = WINDOW // BLOCK
    row_at, col_at = iota((BLOCK, BLOCK), 0), iota((BLOCK, BLOCK), 1)
    scores = []
    for piece in range(reach + 1):
        s = dot_nt(kx[pl.ds(pl.multiple_of(at + piece * BLOCK, BLOCK), BLOCK), :], query)
        if piece == 0:
            s = jnp.where(row_at > col_at, s, FAR)
        if piece == reach:
            s = jnp.where(row_at <= col_at, s, FAR)
        scores.append(s)
    probs = weights(scores, biases, SCALE * LOG2E)
    rounded = probs.astype(bf16)
    out_t = dot(vxt[:, pl.ds(at, span)], rounded)
    delta = jnp.sum(grad.astype(f32).T * out_t, 0, keepdims=True)
    grad_probs = dot_nt(vx[pl.ds(at, span), :], grad)
    grad_scores = (probs * (grad_probs - delta)).astype(bf16)
    dk[pl.ds(at, span), :] += dot(grad_scores, query)
    dv[pl.ds(at, span), :] += dot(rounded, grad)
    return out_t, dot(kxt[:, pl.ds(at, span)], grad_scores).T * SCALE


def own_kernel(x_ref, pair_ref, part_ref, sums_ref, kx, vx, kxt, vxt, dk, dv):
    rows = pair_ref.shape[0]
    tokens = rows // PLANE_DEVS
    for slot in range(PLANE_DEVS):
        at = slot * tokens
        kx[at : at + tokens, :] = x_ref[slot, 0:tokens, 0:128]
        vx[at : at + tokens, :] = x_ref[slot, 0:tokens, 128:256]
    transposed(kx, kxt, rows // BLOCK)
    transposed(vx, vxt, rows // BLOCK)
    dk[...] = jnp.zeros_like(dk)
    dv[...] = jnp.zeros_like(dv)

    def body(block, carry):
        at = pl.multiple_of(block * BLOCK, BLOCK)
        own = pl.ds(pl.multiple_of(WINDOW + at, BLOCK), BLOCK)
        biases = [0.0] * (WINDOW // BLOCK + 1)
        out_t, query_grad = window_block(
            at, pair_ref[own, 0:128], pair_ref[own, 128:256], biases, kx, vx, kxt, vxt, dk, dv
        )
        part_ref[pl.ds(at, BLOCK), 0:128] = out_t.T
        part_ref[pl.ds(at, BLOCK), 128:256] = query_grad
        return carry

    lax.fori_loop(0, (rows - WINDOW) // BLOCK, body, 0, unroll=4)
    sums_ref[:, 0:128] = dk[...] * SCALE
    sums_ref[:, 128:256] = dv[...]


def attention_kernel(
    z_ref,
    x_ref,
    own_ref,
    near_ref,
    far2_ref,
    far3_ref,
    pair_ref,
    part_ref,
    attn_ref,
    fine_ref,
    coarse_ref,
    back1_ref,
    back2_ref,
    back3_ref,
    kx,
    vx,
    kxt,
    vxt,
    kc,
    vc,
    kct,
    vct,
    pq,
    gp,
    dkx,
    dvx,
    dkc,
    dvc,
    high_t,
    low_t,
    high,
    low,
    query_high,
    query_low,
):
    z = z_ref[0]
    rows = pair_ref.shape[0]
    tokens = rows // PLANE_DEVS
    coarse = rows // SHORT
    half = WINDOW // SHORT
    step = BLOCK // SHORT
    reach = WINDOW // BLOCK

    kx[0:WINDOW, :] = near_ref[0:WINDOW, 0:128]
    vx[0:WINDOW, :] = near_ref[0:WINDOW, 128:256]
    for slot in range((rows - WINDOW) // tokens):
        at = WINDOW + slot * tokens
        kx[at : at + tokens, :] = x_ref[slot, 0:tokens, 0:128]
        vx[at : at + tokens, :] = x_ref[slot, 0:tokens, 128:256]

    transposed(kx, kxt, rows // BLOCK)
    transposed(vx, vxt, rows // BLOCK)

    tails = [
        near_ref[WINDOW - TAIL : WINDOW, :],
        far2_ref[coarse : coarse + TAIL, :],
        far3_ref[coarse : coarse + TAIL, :],
    ]
    base = WINDOW + TAIL
    for piece in range(reach):
        at = coarse + half + piece * step
        block = near_ref[piece * BLOCK : (piece + 1) * BLOCK, :]
        lead = near_ref[piece * BLOCK - TAIL : piece * BLOCK, :] if piece else None
        rest = pooled_rows(block, lead)
        kc[at : at + step, :] = rest[:, 0:128]
        vc[at : at + step, :] = rest[:, 128:256]
    sources = ((own_ref, coarse), (near_ref.at[base:], half + TAIL), (far2_ref, coarse), (far3_ref, coarse))
    for slot, (source, count) in enumerate(sources):
        at = slot * coarse
        kc[at : at + count, :] = source[0:count, 0:128]
        vc[at : at + count, :] = source[0:count, 128:256]
        if slot + 1 < PLANES:
            fixed = first_row_fixed(source[0:TAIL, :], tails[slot])
            kc[at : at + TAIL, :] = fixed[:, 0:128]
            vc[at : at + TAIL, :] = fixed[:, 128:256]
    transposed(kc, kct, PLANES * coarse // BLOCK)
    transposed(vc, vct, PLANES * coarse // BLOCK)

    shape = (step, BLOCK)
    offset = iota(shape, 1) - SHORT * iota(shape, 0)
    taken = ones_where((offset >= 0) & (offset < SHORT))
    for block in range(rows // BLOCK):
        at = block * BLOCK
        lead = pair_ref[at - TAIL : at, 0:128] if block else near_ref[WINDOW : WINDOW + TAIL, 0:128]
        pq[block * step : (block + 1) * step, :] = pooled_rows(pair_ref[at : at + BLOCK, 0:128], lead)
        gp[block * step : (block + 1) * step, :] = dot(
            taken, pair_ref[at : at + BLOCK, 128:256]
        ).astype(bf16)

    row_at, col_at = iota((BLOCK, BLOCK), 0), iota((BLOCK, BLOCK), 1)
    diagonal = row_at <= col_at
    for block in range(coarse // BLOCK):
        at = block * BLOCK
        query = pq[at : at + BLOCK, :]
        grad = gp[at : at + BLOCK, :]
        scores, biases, keys, values = [], [], [], []
        for piece in range(block + 1):
            s = dot_nt(kc[piece * BLOCK : (piece + 1) * BLOCK, :], query)
            scores.append(jnp.where(diagonal, s, FAR) if piece == block else s)
            biases.append(0.0)
        for slot in range(1, PLANES):
            s = dot_nt(kc[slot * coarse : (slot + 1) * coarse, :], query)
            scores.append(s)
            biases.append(jnp.where(z >= slot, 0.0, FAR))
        probs = weights(scores, biases, COARSE_SCALE * LOG2E)
        rounded = probs.astype(bf16)
        own = at + BLOCK
        parts = ((0, own, 0), (coarse, PLANES * coarse, own))
        out_t = functools.reduce(
            jnp.add, [dot(vct[:, a:b], rounded[c : c + b - a]) for a, b, c in parts]
        )
        grad_t = grad.astype(f32).T
        delta = jnp.sum(grad_t * out_t, 0, keepdims=True)
        high_t[:, at : at + BLOCK], low_t[:, at : at + BLOCK] = split(out_t)
        query_grad_t = jnp.zeros((HEAD_DIM, BLOCK), f32)
        for a, b, c in parts:
            grad_probs = dot_nt(vc[a:b, :], grad)
            grad_scores = (probs[c : c + b - a] * (grad_probs - delta)).astype(bf16)
            query_grad_t += dot(kct[:, a:b], grad_scores)
            dk = dot(grad_scores, query) * COARSE_SCALE
            dv = dot(rounded[c : c + b - a], grad)
            if block == 0:
                dkc[a:b, :] = dk
                dvc[a:b, :] = dv
                if a == 0:
                    dkc[b:coarse, :] = jnp.zeros((coarse - b, HEAD_DIM), f32)
                    dvc[b:coarse, :] = jnp.zeros((coarse - b, HEAD_DIM), f32)
            else:
                dkc[a:b, :] += dk
                dvc[a:b, :] += dv
        query_grad = query_grad_t.T * COARSE_SCALE
        query_high[at : at + BLOCK, :], query_low[at : at + BLOCK, :] = split(query_grad)
    query_high[coarse:, :] = jnp.zeros((TAIL, HEAD_DIM), bf16)
    query_low[coarse:, :] = jnp.zeros((TAIL, HEAD_DIM), bf16)
    coarse_ref[:, 0:128] = dkc[0:coarse, :]
    coarse_ref[:, 128:256] = dvc[0:coarse, :]

    dkx[...] = jnp.zeros_like(dkx)
    dvx[...] = jnp.zeros_like(dvx)

    def short_out(block):
        pair = pl.multiple_of(block // 2 * (2 * step), 2 * step)
        shape = (2 * step, BLOCK)
        spread = ones_where(iota(shape, 0) == block % 2 * step + iota(shape, 1) // SHORT)
        short_t = dot(high_t[:, pl.ds(pair, 2 * step)], spread)
        return short_t + dot(low_t[:, pl.ds(pair, 2 * step)], spread)

    def short_query_grad(block):
        below = pl.ds(pl.multiple_of(block * step, step), step + TAIL)
        spread = dot(spreading(), query_high[below, :]) + dot(spreading(), query_low[below, :])
        return spread * (1.0 / SHORT)

    def window(block, carry):
        at = pl.multiple_of(block * BLOCK, BLOCK)
        here = pl.ds(at, BLOCK)
        biases = [jnp.where((z == 0) & (block + piece < reach), FAR, 0.0) for piece in range(reach + 1)]
        out_t, query_grad = window_block(
            at, pair_ref[here, 0:128], pair_ref[here, 128:256], biases, kx, vx, kxt, vxt, dkx, dvx
        )
        attn_ref[here, 0:128] = (out_t + short_out(block)).T.astype(bf16)
        attn_ref[here, 128:256] = (query_grad + short_query_grad(block)).astype(bf16)
        late = pl.ds(pl.multiple_of(WINDOW + at, BLOCK), BLOCK)
        attn_ref[late, 0:128] = (part_ref[here, 0:128] + short_out(block + reach).T).astype(bf16)
        attn_ref[late, 128:256] = (part_ref[here, 128:256] + short_query_grad(block + reach)).astype(bf16)
        return carry

    lax.fori_loop(0, reach, window, 0, unroll=4)
    fine_ref[:, 0:128] = dkx[WINDOW:, :] * SCALE
    fine_ref[:, 128:256] = dvx[WINDOW:, :]

    first = iota((TAIL, HEAD_DIM), 0) == 0
    for cols, short in ((slice(0, 128), dkc), (slice(128, 256), dvc)):
        high[0:half, cols], low[0:half, cols] = split(short[2 * coarse - half : 2 * coarse, :])
        above = jnp.where(first, short[0:TAIL, :], 0.0)
        high[half:, cols], low[half:, cols] = split(above)
    taken = spreading()
    for piece in range(reach):
        at = piece * BLOCK
        below = piece * step
        spread = dot(taken, high[below : below + step + TAIL, :])
        spread += dot(taken, low[below : below + step + TAIL, :])
        spread = spread * (1.0 / SHORT)
        back1_ref[at : at + BLOCK, 0:128] = (
            dkx[at : at + BLOCK, :] * SCALE + spread[:, 0:128]
        ).astype(bf16)
        back1_ref[at : at + BLOCK, 128:256] = (
            dvx[at : at + BLOCK, :] + spread[:, 128:256]
        ).astype(bf16)
    query_row = jnp.where(first, query_high[0:TAIL, :].astype(f32), 0.0).astype(bf16)
    back1_ref[WINDOW:base, 0:128] = query_row
    back1_ref[WINDOW:base, 128:256] = query_row
    back1_ref[base:, 0:128] = dkc[coarse : coarse + half + TAIL, :].astype(bf16)
    back1_ref[base:, 128:256] = dvc[coarse : coarse + half + TAIL, :].astype(bf16)
    for slot, ref in ((2, back2_ref), (3, back3_ref)):
        at = slot * coarse
        above = at - coarse
        for cols, short in ((slice(0, 128), dkc), (slice(128, 256), dvc)):
            ref[0:coarse, cols] = short[at : at + coarse, :].astype(bf16)
            row = jnp.where(first, short[above : above + TAIL, :], 0.0)
            ref[coarse : coarse + TAIL, cols] = row.astype(bf16)


def finish_kernel(
    sums_ref, fine_ref, coarse_ref, back1_ref, back2_ref, back3_ref, out_ref, high, low
):
    rows = sums_ref.shape[0]
    tokens = rows // PLANE_DEVS
    coarse = rows // SHORT
    half = coarse - WINDOW // SHORT
    step = BLOCK // SHORT
    base = WINDOW + TAIL
    part = half + TAIL
    ups = (back2_ref, back3_ref)
    total = coarse_ref[...]
    for up in ups:
        total += up[0:coarse, :].astype(f32)
    near = total[0:part, :] + back1_ref[base:, :].astype(f32)
    high[0:part, :], low[0:part, :] = split(near)
    high[part : part + half, :], low[part : part + half, :] = split(total[half:, :])
    extra = functools.reduce(jnp.add, [up[coarse : coarse + TAIL, :].astype(f32) for up in ups])
    high[part + half :, :], low[part + half :, :] = split(extra)
    taken = spreading()
    for block in range(rows // BLOCK):
        at = block * BLOCK
        late = at - (rows - WINDOW)
        below = block * step if late < 0 else part + late // SHORT
        spread = dot(taken, high[below : below + step + TAIL, :])
        spread += dot(taken, low[below : below + step + TAIL, :])
        result = sums_ref[at : at + BLOCK, :] + spread * (1.0 / SHORT)
        if late < 0:
            result = result + fine_ref[at : at + BLOCK, :]
        else:
            result = result + back1_ref[late : late + BLOCK, :].astype(f32)
        out_ref[block, 0:tokens, :] = result.astype(bf16)
        out_ref[block, tokens:, :] = jnp.zeros((TAIL, 256), bf16)
    out_ref[PLANE_DEVS - 1, tokens:, :] = back1_ref[WINDOW:base, :]


def unpack_kernel(pair_ref, x_ref, q_ref, k_ref, v_ref):
    tokens = q_ref.shape[0]
    last = iota((TAIL, HEAD_DIM), 0) > TAIL - SHORT
    for slot in range(q_ref.shape[1] // HEAD_DIM):
        cols = pl.ds(slot * HEAD_DIM, HEAD_DIM)
        k_ref[:, cols] = x_ref[slot, 0:tokens, 0:128]
        v_ref[:, cols] = x_ref[slot, 0:tokens, 128:256]
        q_ref[0 : tokens - TAIL, cols] = pair_ref[slot, 0 : tokens - TAIL, 128:256]
        above = jnp.sum(x_ref[slot, tokens:, 0:128].astype(f32), 0, keepdims=True) * (1.0 / SHORT)
        rest = pair_ref[slot, tokens - TAIL :, 128:256].astype(f32)
        q_ref[tokens - TAIL :, cols] = (rest + jnp.where(last, above, 0.0)).astype(bf16)


def grad_product(halves, a_ref, b_ref, w_ref, total, start):
    at = pl.program_id(0)
    depth = w_ref.shape[1]
    for piece, ref in enumerate((a_ref, b_ref)):
        for half in range(halves):

            @pl.when(at == piece * halves + half)
            def _():
                product = dot_nt(w_ref[...], ref[:, half * depth : (half + 1) * depth])
                if piece + half > 0:
                    total[...] += product
                elif start is None:
                    total[...] = product
                else:
                    total[...] = start[...] + product


def grad_near_kernel(halves, order_ref, a_ref, b_ref, w_ref, total):
    grad_product(halves, a_ref, b_ref, w_ref, total, None)


def grad_far_kernel(halves, order_ref, a_ref, b_ref, w_ref, start, q_ref, out_ref, total):
    grad_product(halves, a_ref, b_ref, w_ref, total, start)

    @pl.when(pl.program_id(0) == pl.num_programs(0) - 1)
    def _():
        last = total.shape[0] // HEAD_DIM - 1
        for slot in range(PLANE_DEVS):
            head = slice(min(slot, last) * HEAD_DIM, (min(slot, last) + 1) * HEAD_DIM)
            out_ref[slot, :, 0:128] = q_ref[:, head]
            out_ref[slot, :, 128:256] = total[head, :].T.astype(bf16)


def grad_part(pieces, order, weight, rest=()):
    rows, width = pieces[0].shape
    depth = weight.shape[0]
    halves = 1
    tile = width // halves

    first = 2 if rest else 0

    def whole(shape):
        return pl.BlockSpec(shape, lambda i, o: (0,) * len(shape))

    packed = (PLANE_DEVS, rows, 2 * HEAD_DIM)
    return pl.pallas_call(
        functools.partial(grad_far_kernel if rest else grad_near_kernel, halves),
        out_shape=jax.ShapeDtypeStruct(packed, bf16) if rest else jax.ShapeDtypeStruct((depth, rows), f32),
        grid_spec=pltpu.PrefetchScalarGridSpec(
            num_scalar_prefetch=1,
            grid=(2 * halves,),
            in_specs=[whole((rows, width))] * 2
            + [pl.BlockSpec((depth, tile), lambda i, o: (0, o[first + i // halves] * halves + i % halves))]
            + [whole(x.shape) for x in rest],
            out_specs=whole(packed if rest else (depth, rows)),
            scratch_shapes=[pltpu.VMEM((depth, rows), f32)] if rest else [],
        ),
        compiler_params=pltpu.CompilerParams(vmem_limit_bytes=62 * 1024 * 1024),
    )(order, *pieces, weight, *rest)


def project_kernel(halves, order_ref, attn_ref, w_ref, *refs):
    send_ref, keep_ref, rows_ref = refs[-3:]
    at = pl.program_id(0)
    heads = w_ref.shape[0] // HEAD_DIM
    tile = w_ref.shape[1]

    @pl.when(at == 0)
    def _():
        for slot in range(heads):
            rows_ref[:, slot * HEAD_DIM : (slot + 1) * HEAD_DIM] = attn_ref[slot, :, 0:128]

    product = dot(rows_ref[...], w_ref[...]).astype(bf16)
    for half in range(halves):

        @pl.when(at == half)
        def _():
            send_ref[:, half * tile : (half + 1) * tile] = product

        @pl.when(at == halves + half)
        def _():
            keep_ref[:, half * tile : (half + 1) * tile] = product


def project(attn, order, last, weight, width, after):
    rows = attn.shape[1]
    depth = weight.shape[0]
    halves = 1
    tile = width // halves
    out = jax.ShapeDtypeStruct((rows, width), bf16)
    return pl.pallas_call(
        functools.partial(project_kernel, halves),
        out_shape=(out, out),
        grid_spec=pltpu.PrefetchScalarGridSpec(
            num_scalar_prefetch=1,
            grid=(2 * halves,),
            in_specs=[
                pl.BlockSpec(attn.shape, lambda i, o: (0, 0, 0)),
                pl.BlockSpec((depth, tile), lambda i, o: (0, o[last - i // halves] * halves + i % halves)),
            ]
            + [pl.BlockSpec(memory_space=pltpu.HBM)] * len(after),
            out_specs=[pl.BlockSpec((rows, width), lambda i, o: (0, 0))] * 2,
            scratch_shapes=[pltpu.VMEM((rows, depth), bf16)],
        ),
        compiler_params=pltpu.CompilerParams(vmem_limit_bytes=62 * 1024 * 1024),
    )(order, attn, weight, *after)


def swap(x, axis):
    return lax.ppermute(x, axis, [(0, 1), (1, 0)])


def planes_up(x, by):
    return lax.ppermute(x, "z", [(i, i + by) for i in range(PLANES) if 0 <= i + by < PLANES])


def in_plane(x):
    return lax.all_to_all(x, PLANE, 0, 0, tiled=True)


def column_blocks():
    xl, core = lax.axis_index("xl"), lax.axis_index("c")
    own, other = 2 * xl, 2 * (1 - xl)
    return jnp.stack([own + core, own + 1 - core, other + core, other + 1 - core]).astype(jnp.int32)


def gathered_grad(out_grad, out_weight, q_proj, blocks):
    far = swap(out_grad, "xl")
    near = swap(out_grad, "c")
    start = grad_part((out_grad, near), blocks, out_weight)
    far, start = lax.optimization_barrier((far, start))
    both = swap(far, "c")
    return start, grad_part((far, both), blocks, out_weight, (start, q_proj))


def projected(attn, out_weight, width, blocks, after):
    def share(last, attn):
        send, keep = project(attn, blocks, last, out_weight, width, after)
        return keep.astype(f32) + swap(send, "c").astype(f32)

    part = share(3, attn).astype(bf16)
    part, attn = lax.optimization_barrier((part, attn))
    far = swap(part, "xl")
    return (share(1, attn) + far.astype(f32)).astype(bf16)


def shards(q_proj, k_proj, v_proj, out_weight, out_grad):
    tokens, cols = q_proj.shape
    rows = tokens * PLANE_DEVS
    coarse = rows // SHORT
    total = PLANES * coarse
    z = lax.axis_index("z").astype(jnp.int32).reshape(1)

    def array(*shape, dtype=bf16):
        return jax.ShapeDtypeStruct(shape, dtype)

    in_place = pl.BlockSpec(memory_space=pltpu.HBM)
    whole = pl.BlockSpec(memory_space=pltpu.VMEM)
    packed = call(
        pack_kernel,
        array(PLANE_DEVS, tokens + TAIL, 2 * HEAD_DIM),
        62,
        in_specs=[in_place] * 3,
        out_specs=whole,
        scratch_shapes=[pltpu.SemaphoreType.DMA((PLANE_DEVS, 4))],
    )(q_proj, k_proj, v_proj)
    own = in_plane(packed)
    blocks = column_blocks()
    early, pair_packed = gathered_grad(out_grad, out_weight, q_proj, blocks)
    near_rows = WINDOW + 2 * TAIL + WINDOW // SHORT
    near, far = call(
        pool_kernel,
        (array(near_rows, 256), array(coarse + TAIL, 256)),
        16,
        in_specs=[whole, in_place],
    )(own, early)
    near_in = planes_up(near, 1)
    far3_in = lax.ppermute(far, "z", [(0, 3), (1, 0)])
    far2_in = lax.ppermute(far3_in, "z", [(3, 2), (0, 3)])
    pair = in_plane(pair_packed).reshape(rows, 2 * HEAD_DIM)

    part, sums = call(
        own_kernel,
        (array(rows - WINDOW, 256, dtype=f32), array(rows, 256, dtype=f32)),
        56,
        in_specs=[whole] * 2,
        out_specs=[whole] * 2,
        scratch_shapes=[pltpu.VMEM((rows, HEAD_DIM), bf16)] * 2
        + [pltpu.VMEM((HEAD_DIM, rows), bf16)] * 2
        + [pltpu.VMEM((rows, HEAD_DIM), f32)] * 2,
    )(own, pair)
    attn, fine, short, back1, back2, back3 = call(
        attention_kernel,
        (
            array(rows, 256),
            array(rows - WINDOW, 256, dtype=f32),
            array(coarse, 256, dtype=f32),
            array(near_rows, 256),
            array(coarse + TAIL, 256),
            array(coarse + TAIL, 256),
        ),
        62,
        in_specs=[pl.BlockSpec(memory_space=pltpu.SMEM)] + [whole] * 7,
        out_specs=[whole] * 6,
        scratch_shapes=[
            pltpu.VMEM((rows, HEAD_DIM), bf16),
            pltpu.VMEM((rows, HEAD_DIM), bf16),
            pltpu.VMEM((HEAD_DIM, rows), bf16),
            pltpu.VMEM((HEAD_DIM, rows), bf16),
            pltpu.VMEM((total, HEAD_DIM), bf16),
            pltpu.VMEM((total, HEAD_DIM), bf16),
            pltpu.VMEM((HEAD_DIM, total), bf16),
            pltpu.VMEM((HEAD_DIM, total), bf16),
            pltpu.VMEM((coarse, HEAD_DIM), bf16),
            pltpu.VMEM((coarse, HEAD_DIM), bf16),
            pltpu.VMEM((rows, HEAD_DIM), f32),
            pltpu.VMEM((rows, HEAD_DIM), f32),
            pltpu.VMEM((total, HEAD_DIM), f32),
            pltpu.VMEM((total, HEAD_DIM), f32),
            pltpu.VMEM((HEAD_DIM, coarse), bf16),
            pltpu.VMEM((HEAD_DIM, coarse), bf16),
            pltpu.VMEM((WINDOW // SHORT + TAIL, 256), bf16),
            pltpu.VMEM((WINDOW // SHORT + TAIL, 256), bf16),
            pltpu.VMEM((coarse + TAIL, HEAD_DIM), bf16),
            pltpu.VMEM((coarse + TAIL, HEAD_DIM), bf16),
        ],
    )(z, own, far, near_in, far2_in, far3_in, pair, part)

    back1_in = planes_up(back1, -1)
    halfway = lax.ppermute(back2, "z", [(3, 0), (2, 3)])
    back3_in = lax.ppermute(back3, "z", [(3, 0)])
    back2_in = lax.ppermute(halfway, "z", [(0, 1), (3, 0)])
    attn_in = in_plane(attn.reshape(PLANE_DEVS, tokens, 256))
    finished = call(
        finish_kernel,
        array(PLANE_DEVS, tokens + TAIL, 256),
        32,
        scratch_shapes=[
            pltpu.VMEM((coarse + 2 * TAIL, 256), bf16),
            pltpu.VMEM((coarse + 2 * TAIL, 256), bf16),
        ],
    )(sums, fine, short, back1_in, back2_in, back3_in)
    mixed_out = projected(
        attn_in, out_weight, out_grad.shape[1], blocks, (finished,)
    )
    returned = in_plane(finished)
    grads = call(unpack_kernel, (array(tokens, cols),) * 3, 16)(attn_in, returned)
    return (mixed_out, *grads)


def solution(mesh):
    fine_mesh = Mesh(np.asarray(mesh.devices).reshape(4, 4, 2, 2, 2), ("z", "y", "xh", "xl", "c"))
    both = P(("z", "y", "xh"), ("xl", "c"))
    in_specs = (both, both, both, P(("xl", "c"), None), both)
    return jax.shard_map(
        shards, mesh=fine_mesh, in_specs=in_specs, out_specs=(both,) * 4, check_vma=False
    )
```

```python
import functools
import math

import jax
import jax.numpy as jnp
import numpy as np
from jax import lax
from jax.experimental import pallas as pl
from jax.experimental.pallas import tpu as pltpu
from jax.sharding import Mesh, PartitionSpec as P

HEAD_DIM = 128
SHORT = 4
WINDOW = 1024
PLANES = 4
PLANE_DEVS = 8
BLOCK = 256
TAIL = 16
LOG2E = math.log2(math.e)
SCALE = 1.0 / math.sqrt(HEAD_DIM)
COARSE_SCALE = 2.0 * SCALE
FAR = -1e30
PLANE = ("y", "xh")
bf16 = jnp.bfloat16
f32 = jnp.float32


def call(kernel, out_shape, vmem_mib, **rest):
    return pl.pallas_call(
        kernel,
        out_shape=out_shape,
        compiler_params=pltpu.CompilerParams(vmem_limit_bytes=vmem_mib * 1024 * 1024),
        **rest,
    )


def dot(a, b):
    return jnp.dot(a, b, preferred_element_type=f32)


def dot_nt(a, b):
    return lax.dot_general(a, b, (((1,), (1,)), ((), ())), preferred_element_type=f32)


def iota(shape, dim):
    return lax.broadcasted_iota(jnp.int32, shape, dim)


def split(x):
    high = x.astype(bf16)
    return high, (x - high.astype(f32)).astype(bf16)


def ones_where(mask):
    return jnp.where(mask, 1.0, 0.0).astype(bf16)


def pack_kernel(q_ref, k_ref, v_ref, out_ref, sems):
    tokens = q_ref.shape[0]
    last = q_ref.shape[1] // HEAD_DIM - 1
    copies = []
    for slot in range(PLANE_DEVS):
        cols = pl.ds(min(slot, last) * HEAD_DIM, HEAD_DIM)
        tail = q_ref.at[tokens - TAIL :, cols]
        pieces = (
            (k_ref.at[:, cols], out_ref.at[slot, 0:tokens, 0:128]),
            (v_ref.at[:, cols], out_ref.at[slot, 0:tokens, 128:256]),
            (tail, out_ref.at[slot, tokens:, 0:128]),
            (tail, out_ref.at[slot, tokens:, 128:256]),
        )
        for at, (source, target) in enumerate(pieces):
            copies.append(pltpu.make_async_copy(source, target, sems.at[slot, at]))
    for copy in copies:
        copy.start()
    for copy in copies:
        copy.wait()


def pooling(lead):
    shape = (BLOCK // SHORT, BLOCK + lead)
    back = iota(shape, 1) - lead - SHORT * iota(shape, 0)
    return ones_where((back <= 0) & (back > -SHORT))


def spreading():
    shape = (BLOCK, BLOCK // SHORT + TAIL)
    return ones_where((iota(shape, 0) + (SHORT - 1)) // SHORT == iota(shape, 1))


def pooled_rows(block, lead=None):
    rows = block if lead is None else jnp.concatenate([lead, block], 0)
    taken = pooling(0 if lead is None else TAIL)
    return (dot(taken, rows) * (1.0 / SHORT)).astype(bf16)


def pool_kernel(x_ref, after_ref, near_ref, far_ref):
    del after_ref
    devs, tokens = x_ref.shape[0], x_ref.shape[1] - TAIL
    step = tokens // SHORT
    half = WINDOW // SHORT
    coarse = devs * step
    for slot in range(devs):
        block = x_ref[slot, 0:tokens, :]
        lead = x_ref[slot - 1, tokens - TAIL : tokens, :] if slot else None
        far_ref[slot * step : (slot + 1) * step, :] = pooled_rows(block, lead)
        late = slot * tokens - (devs * tokens - WINDOW)
        if late >= 0:
            near_ref[late : late + tokens, :] = block
    far_ref[coarse : coarse + TAIL, :] = x_ref[devs - 1, tokens - TAIL : tokens, :]
    near_ref[WINDOW : WINDOW + TAIL, :] = x_ref[devs - 1, tokens:, :]
    near_ref[WINDOW + TAIL :, :] = far_ref[0 : half + TAIL, :]


def first_row_fixed(pooled, tail):
    kept = jnp.where(iota(tail.shape, 0) > TAIL - SHORT, tail.astype(f32), 0.0)
    lacking = jnp.sum(kept, 0, keepdims=True) * (1.0 / SHORT)
    head = pooled[0:TAIL, :].astype(f32)
    return jnp.where(iota(head.shape, 0) == 0, head + lacking, head).astype(bf16)


def transposed(ref, out, count):
    def body(i, carry):
        at = pl.multiple_of(i * BLOCK, BLOCK)
        out[:, pl.ds(at, BLOCK)] = ref[pl.ds(at, BLOCK), :].T
        return carry

    lax.fori_loop(0, count, body, 0)


def weights(scores, biases, factor):
    tops = [jnp.max(s, 0, keepdims=True) + b for s, b in zip(scores, biases)]
    top = functools.reduce(jnp.maximum, tops)
    exps = [jnp.exp2((s - (top - b)) * factor) for s, b in zip(scores, biases)]
    total = functools.reduce(jnp.add, [jnp.sum(e, 0, keepdims=True) for e in exps])
    inverse = 1.0 / total
    return jnp.concatenate([e * inverse for e in exps], 0)


def window_block(at, query, grad, biases, kx, vx, kxt, vxt, dk, dv):
    span = WINDOW + BLOCK
    reach = WINDOW // BLOCK
    row_at, col_at = iota((BLOCK, BLOCK), 0), iota((BLOCK, BLOCK), 1)
    scores = []
    for piece in range(reach + 1):
        s = dot_nt(kx[pl.ds(pl.multiple_of(at + piece * BLOCK, BLOCK), BLOCK), :], query)
        if piece == 0:
            s = jnp.where(row_at > col_at, s, FAR)
        if piece == reach:
            s = jnp.where(row_at <= col_at, s, FAR)
        scores.append(s)
    probs = weights(scores, biases, SCALE * LOG2E)
    rounded = probs.astype(bf16)
    out_t = dot(vxt[:, pl.ds(at, span)], rounded)
    delta = jnp.sum(grad.astype(f32).T * out_t, 0, keepdims=True)
    grad_probs = dot_nt(vx[pl.ds(at, span), :], grad)
    grad_scores = (probs * (grad_probs - delta)).astype(bf16)
    dk[pl.ds(at, span), :] += dot(grad_scores, query)
    dv[pl.ds(at, span), :] += dot(rounded, grad)
    return out_t, dot(kxt[:, pl.ds(at, span)], grad_scores).T * SCALE


def own_kernel(x_ref, pair_ref, part_ref, sums_ref, kx, vx, kxt, vxt, dk, dv):
    rows = pair_ref.shape[0]
    tokens = rows // PLANE_DEVS
    for slot in range(PLANE_DEVS):
        at = slot * tokens
        kx[at : at + tokens, :] = x_ref[slot, 0:tokens, 0:128]
        vx[at : at + tokens, :] = x_ref[slot, 0:tokens, 128:256]
    transposed(kx, kxt, rows // BLOCK)
    transposed(vx, vxt, rows // BLOCK)
    dk[...] = jnp.zeros_like(dk)
    dv[...] = jnp.zeros_like(dv)

    def body(block, carry):
        at = pl.multiple_of(block * BLOCK, BLOCK)
        own = pl.ds(pl.multiple_of(WINDOW + at, BLOCK), BLOCK)
        biases = [0.0] * (WINDOW // BLOCK + 1)
        out_t, query_grad = window_block(
            at, pair_ref[own, 0:128], pair_ref[own, 128:256], biases, kx, vx, kxt, vxt, dk, dv
        )
        part_ref[pl.ds(at, BLOCK), 0:128] = out_t.T
        part_ref[pl.ds(at, BLOCK), 128:256] = query_grad
        return carry

    lax.fori_loop(0, (rows - WINDOW) // BLOCK, body, 0, unroll=4)
    sums_ref[:, 0:128] = dk[...] * SCALE
    sums_ref[:, 128:256] = dv[...]


def attention_kernel(
    z_ref,
    x_ref,
    own_ref,
    near_ref,
    far2_ref,
    far3_ref,
    pair_ref,
    part_ref,
    attn_ref,
    fine_ref,
    coarse_ref,
    back1_ref,
    back2_ref,
    back3_ref,
    kx,
    vx,
    kxt,
    vxt,
    kc,
    vc,
    kct,
    vct,
    pq,
    gp,
    dkx,
    dvx,
    dkc,
    dvc,
    high_t,
    low_t,
    high,
    low,
    query_high,
    query_low,
):
    z = z_ref[0]
    rows = pair_ref.shape[0]
    tokens = rows // PLANE_DEVS
    coarse = rows // SHORT
    half = WINDOW // SHORT
    step = BLOCK // SHORT
    reach = WINDOW // BLOCK

    kx[0:WINDOW, :] = near_ref[0:WINDOW, 0:128]
    vx[0:WINDOW, :] = near_ref[0:WINDOW, 128:256]
    for slot in range((rows - WINDOW) // tokens):
        at = WINDOW + slot * tokens
        kx[at : at + tokens, :] = x_ref[slot, 0:tokens, 0:128]
        vx[at : at + tokens, :] = x_ref[slot, 0:tokens, 128:256]

    transposed(kx, kxt, rows // BLOCK)
    transposed(vx, vxt, rows // BLOCK)

    tails = [
        near_ref[WINDOW - TAIL : WINDOW, :],
        far2_ref[coarse : coarse + TAIL, :],
        far3_ref[coarse : coarse + TAIL, :],
    ]
    base = WINDOW + TAIL
    for piece in range(reach):
        at = coarse + half + piece * step
        block = near_ref[piece * BLOCK : (piece + 1) * BLOCK, :]
        lead = near_ref[piece * BLOCK - TAIL : piece * BLOCK, :] if piece else None
        rest = pooled_rows(block, lead)
        kc[at : at + step, :] = rest[:, 0:128]
        vc[at : at + step, :] = rest[:, 128:256]
    sources = ((own_ref, coarse), (near_ref.at[base:], half + TAIL), (far2_ref, coarse), (far3_ref, coarse))
    for slot, (source, count) in enumerate(sources):
        at = slot * coarse
        kc[at : at + count, :] = source[0:count, 0:128]
        vc[at : at + count, :] = source[0:count, 128:256]
        if slot + 1 < PLANES:
            fixed = first_row_fixed(source[0:TAIL, :], tails[slot])
            kc[at : at + TAIL, :] = fixed[:, 0:128]
            vc[at : at + TAIL, :] = fixed[:, 128:256]
    transposed(kc, kct, PLANES * coarse // BLOCK)
    transposed(vc, vct, PLANES * coarse // BLOCK)

    shape = (step, BLOCK)
    offset = iota(shape, 1) - SHORT * iota(shape, 0)
    taken = ones_where((offset >= 0) & (offset < SHORT))
    for block in range(rows // BLOCK):
        at = block * BLOCK
        lead = pair_ref[at - TAIL : at, 0:128] if block else near_ref[WINDOW : WINDOW + TAIL, 0:128]
        pq[block * step : (block + 1) * step, :] = pooled_rows(pair_ref[at : at + BLOCK, 0:128], lead)
        gp[block * step : (block + 1) * step, :] = dot(
            taken, pair_ref[at : at + BLOCK, 128:256]
        ).astype(bf16)

    row_at, col_at = iota((BLOCK, BLOCK), 0), iota((BLOCK, BLOCK), 1)
    diagonal = row_at <= col_at
    for block in range(coarse // BLOCK):
        at = block * BLOCK
        query = pq[at : at + BLOCK, :]
        grad = gp[at : at + BLOCK, :]
        scores, biases, keys, values = [], [], [], []
        for piece in range(block + 1):
            s = dot_nt(kc[piece * BLOCK : (piece + 1) * BLOCK, :], query)
            scores.append(jnp.where(diagonal, s, FAR) if piece == block else s)
            biases.append(0.0)
        for slot in range(1, PLANES):
            s = dot_nt(kc[slot * coarse : (slot + 1) * coarse, :], query)
            scores.append(s)
            biases.append(jnp.where(z >= slot, 0.0, FAR))
        probs = weights(scores, biases, COARSE_SCALE * LOG2E)
        rounded = probs.astype(bf16)
        own = at + BLOCK
        parts = ((0, own, 0), (coarse, PLANES * coarse, own))
        out_t = functools.reduce(
            jnp.add, [dot(vct[:, a:b], rounded[c : c + b - a]) for a, b, c in parts]
        )
        grad_t = grad.astype(f32).T
        delta = jnp.sum(grad_t * out_t, 0, keepdims=True)
        high_t[:, at : at + BLOCK], low_t[:, at : at + BLOCK] = split(out_t)
        query_grad_t = jnp.zeros((HEAD_DIM, BLOCK), f32)
        for a, b, c in parts:
            grad_probs = dot_nt(vc[a:b, :], grad)
            grad_scores = (probs[c : c + b - a] * (grad_probs - delta)).astype(bf16)
            query_grad_t += dot(kct[:, a:b], grad_scores)
            dk = dot(grad_scores, query) * COARSE_SCALE
            dv = dot(rounded[c : c + b - a], grad)
            if block == 0:
                dkc[a:b, :] = dk
                dvc[a:b, :] = dv
                if a == 0:
                    dkc[b:coarse, :] = jnp.zeros((coarse - b, HEAD_DIM), f32)
                    dvc[b:coarse, :] = jnp.zeros((coarse - b, HEAD_DIM), f32)
            else:
                dkc[a:b, :] += dk
                dvc[a:b, :] += dv
        query_grad = query_grad_t.T * COARSE_SCALE
        query_high[at : at + BLOCK, :], query_low[at : at + BLOCK, :] = split(query_grad)
    query_high[coarse:, :] = jnp.zeros((TAIL, HEAD_DIM), bf16)
    query_low[coarse:, :] = jnp.zeros((TAIL, HEAD_DIM), bf16)
    coarse_ref[:, 0:128] = dkc[0:coarse, :]
    coarse_ref[:, 128:256] = dvc[0:coarse, :]

    dkx[...] = jnp.zeros_like(dkx)
    dvx[...] = jnp.zeros_like(dvx)

    def short_out(block):
        pair = pl.multiple_of(block // 2 * (2 * step), 2 * step)
        shape = (2 * step, BLOCK)
        spread = ones_where(iota(shape, 0) == block % 2 * step + iota(shape, 1) // SHORT)
        short_t = dot(high_t[:, pl.ds(pair, 2 * step)], spread)
        return short_t + dot(low_t[:, pl.ds(pair, 2 * step)], spread)

    def short_query_grad(block):
        below = pl.ds(pl.multiple_of(block * step, step), step + TAIL)
        spread = dot(spreading(), query_high[below, :]) + dot(spreading(), query_low[below, :])
        return spread * (1.0 / SHORT)

    def window(block, carry):
        at = pl.multiple_of(block * BLOCK, BLOCK)
        here = pl.ds(at, BLOCK)
        biases = [jnp.where((z == 0) & (block + piece < reach), FAR, 0.0) for piece in range(reach + 1)]
        out_t, query_grad = window_block(
            at, pair_ref[here, 0:128], pair_ref[here, 128:256], biases, kx, vx, kxt, vxt, dkx, dvx
        )
        attn_ref[here, 0:128] = (out_t + short_out(block)).T.astype(bf16)
        attn_ref[here, 128:256] = (query_grad + short_query_grad(block)).astype(bf16)
        late = pl.ds(pl.multiple_of(WINDOW + at, BLOCK), BLOCK)
        attn_ref[late, 0:128] = (part_ref[here, 0:128] + short_out(block + reach).T).astype(bf16)
        attn_ref[late, 128:256] = (part_ref[here, 128:256] + short_query_grad(block + reach)).astype(bf16)
        return carry

    lax.fori_loop(0, reach, window, 0, unroll=4)
    fine_ref[:, 0:128] = dkx[WINDOW:, :] * SCALE
    fine_ref[:, 128:256] = dvx[WINDOW:, :]

    first = iota((TAIL, HEAD_DIM), 0) == 0
    for cols, short in ((slice(0, 128), dkc), (slice(128, 256), dvc)):
        high[0:half, cols], low[0:half, cols] = split(short[2 * coarse - half : 2 * coarse, :])
        above = jnp.where(first, short[0:TAIL, :], 0.0)
        high[half:, cols], low[half:, cols] = split(above)
    taken = spreading()
    for piece in range(reach):
        at = piece * BLOCK
        below = piece * step
        spread = dot(taken, high[below : below + step + TAIL, :])
        spread += dot(taken, low[below : below + step + TAIL, :])
        spread = spread * (1.0 / SHORT)
        back1_ref[at : at + BLOCK, 0:128] = (
            dkx[at : at + BLOCK, :] * SCALE + spread[:, 0:128]
        ).astype(bf16)
        back1_ref[at : at + BLOCK, 128:256] = (
            dvx[at : at + BLOCK, :] + spread[:, 128:256]
        ).astype(bf16)
    query_row = jnp.where(first, query_high[0:TAIL, :].astype(f32), 0.0).astype(bf16)
    back1_ref[WINDOW:base, 0:128] = query_row
    back1_ref[WINDOW:base, 128:256] = query_row
    back1_ref[base:, 0:128] = dkc[coarse : coarse + half + TAIL, :].astype(bf16)
    back1_ref[base:, 128:256] = dvc[coarse : coarse + half + TAIL, :].astype(bf16)
    for slot, ref in ((2, back2_ref), (3, back3_ref)):
        at = slot * coarse
        above = at - coarse
        for cols, short in ((slice(0, 128), dkc), (slice(128, 256), dvc)):
            ref[0:coarse, cols] = short[at : at + coarse, :].astype(bf16)
            row = jnp.where(first, short[above : above + TAIL, :], 0.0)
            ref[coarse : coarse + TAIL, cols] = row.astype(bf16)


def finish_kernel(
    sums_ref, fine_ref, coarse_ref, back1_ref, back2_ref, back3_ref, out_ref, high, low
):
    rows = sums_ref.shape[0]
    tokens = rows // PLANE_DEVS
    coarse = rows // SHORT
    half = coarse - WINDOW // SHORT
    step = BLOCK // SHORT
    base = WINDOW + TAIL
    part = half + TAIL
    ups = (back2_ref, back3_ref)
    total = coarse_ref[...]
    for up in ups:
        total += up[0:coarse, :].astype(f32)
    near = total[0:part, :] + back1_ref[base:, :].astype(f32)
    high[0:part, :], low[0:part, :] = split(near)
    high[part : part + half, :], low[part : part + half, :] = split(total[half:, :])
    extra = functools.reduce(jnp.add, [up[coarse : coarse + TAIL, :].astype(f32) for up in ups])
    high[part + half :, :], low[part + half :, :] = split(extra)
    taken = spreading()
    for block in range(rows // BLOCK):
        at = block * BLOCK
        late = at - (rows - WINDOW)
        below = block * step if late < 0 else part + late // SHORT
        spread = dot(taken, high[below : below + step + TAIL, :])
        spread += dot(taken, low[below : below + step + TAIL, :])
        result = sums_ref[at : at + BLOCK, :] + spread * (1.0 / SHORT)
        if late < 0:
            result = result + fine_ref[at : at + BLOCK, :]
        else:
            result = result + back1_ref[late : late + BLOCK, :].astype(f32)
        out_ref[block, 0:tokens, :] = result.astype(bf16)
        out_ref[block, tokens:, :] = jnp.zeros((TAIL, 256), bf16)
    out_ref[PLANE_DEVS - 1, tokens:, :] = back1_ref[WINDOW:base, :]


def unpack_kernel(pair_ref, x_ref, q_ref, k_ref, v_ref):
    tokens = q_ref.shape[0]
    last = iota((TAIL, HEAD_DIM), 0) > TAIL - SHORT
    for slot in range(q_ref.shape[1] // HEAD_DIM):
        cols = pl.ds(slot * HEAD_DIM, HEAD_DIM)
        k_ref[:, cols] = x_ref[slot, 0:tokens, 0:128]
        v_ref[:, cols] = x_ref[slot, 0:tokens, 128:256]
        q_ref[0 : tokens - TAIL, cols] = pair_ref[slot, 0 : tokens - TAIL, 128:256]
        above = jnp.sum(x_ref[slot, tokens:, 0:128].astype(f32), 0, keepdims=True) * (1.0 / SHORT)
        rest = pair_ref[slot, tokens - TAIL :, 128:256].astype(f32)
        q_ref[tokens - TAIL :, cols] = (rest + jnp.where(last, above, 0.0)).astype(bf16)


def grad_product(halves, a_ref, b_ref, w_ref, total, start):
    at = pl.program_id(0)
    depth = w_ref.shape[1]
    for piece, ref in enumerate((a_ref, b_ref)):
        for half in range(halves):

            @pl.when(at == piece * halves + half)
            def _():
                product = dot_nt(w_ref[...], ref[:, half * depth : (half + 1) * depth])
                if piece + half > 0:
                    total[...] += product
                elif start is None:
                    total[...] = product
                else:
                    total[...] = start[...] + product


def grad_near_kernel(halves, order_ref, a_ref, b_ref, w_ref, total):
    grad_product(halves, a_ref, b_ref, w_ref, total, None)


def grad_far_kernel(halves, order_ref, a_ref, b_ref, w_ref, start, q_ref, out_ref, total):
    grad_product(halves, a_ref, b_ref, w_ref, total, start)

    @pl.when(pl.program_id(0) == pl.num_programs(0) - 1)
    def _():
        last = total.shape[0] // HEAD_DIM - 1
        for slot in range(PLANE_DEVS):
            head = slice(min(slot, last) * HEAD_DIM, (min(slot, last) + 1) * HEAD_DIM)
            out_ref[slot, :, 0:128] = q_ref[:, head]
            out_ref[slot, :, 128:256] = total[head, :].T.astype(bf16)


def grad_part(pieces, order, weight, rest=()):
    rows, width = pieces[0].shape
    depth = weight.shape[0]
    halves = 1
    tile = width // halves

    first = 2 if rest else 0

    def whole(shape):
        return pl.BlockSpec(shape, lambda i, o: (0,) * len(shape))

    packed = (PLANE_DEVS, rows, 2 * HEAD_DIM)
    return pl.pallas_call(
        functools.partial(grad_far_kernel if rest else grad_near_kernel, halves),
        out_shape=jax.ShapeDtypeStruct(packed, bf16) if rest else jax.ShapeDtypeStruct((depth, rows), f32),
        grid_spec=pltpu.PrefetchScalarGridSpec(
            num_scalar_prefetch=1,
            grid=(2 * halves,),
            in_specs=[whole((rows, width))] * 2
            + [pl.BlockSpec((depth, tile), lambda i, o: (0, o[first + i // halves] * halves + i % halves))]
            + [whole(x.shape) for x in rest],
            out_specs=whole(packed if rest else (depth, rows)),
            scratch_shapes=[pltpu.VMEM((depth, rows), f32)] if rest else [],
        ),
        compiler_params=pltpu.CompilerParams(vmem_limit_bytes=62 * 1024 * 1024),
    )(order, *pieces, weight, *rest)


def project_kernel(halves, order_ref, attn_ref, w_ref, *refs):
    send_ref, keep_ref, rows_ref = refs[-3:]
    at = pl.program_id(0)
    heads = w_ref.shape[0] // HEAD_DIM
    tile = w_ref.shape[1]

    @pl.when(at == 0)
    def _():
        for slot in range(heads):
            rows_ref[:, slot * HEAD_DIM : (slot + 1) * HEAD_DIM] = attn_ref[slot, :, 0:128]

    product = dot(rows_ref[...], w_ref[...]).astype(bf16)
    for half in range(halves):

        @pl.when(at == half)
        def _():
            send_ref[:, half * tile : (half + 1) * tile] = product

        @pl.when(at == halves + half)
        def _():
            keep_ref[:, half * tile : (half + 1) * tile] = product


def project(attn, order, last, weight, width, after):
    rows = attn.shape[1]
    depth = weight.shape[0]
    halves = 1
    tile = width // halves
    out = jax.ShapeDtypeStruct((rows, width), bf16)
    return pl.pallas_call(
        functools.partial(project_kernel, halves),
        out_shape=(out, out),
        grid_spec=pltpu.PrefetchScalarGridSpec(
            num_scalar_prefetch=1,
            grid=(2 * halves,),
            in_specs=[
                pl.BlockSpec(attn.shape, lambda i, o: (0, 0, 0)),
                pl.BlockSpec((depth, tile), lambda i, o: (0, o[last - i // halves] * halves + i % halves)),
            ]
            + [pl.BlockSpec(memory_space=pltpu.HBM)] * len(after),
            out_specs=[pl.BlockSpec((rows, width), lambda i, o: (0, 0))] * 2,
            scratch_shapes=[pltpu.VMEM((rows, depth), bf16)],
        ),
        compiler_params=pltpu.CompilerParams(vmem_limit_bytes=62 * 1024 * 1024),
    )(order, attn, weight, *after)


def swap(x, axis):
    return lax.ppermute(x, axis, [(0, 1), (1, 0)])


def planes_up(x, by):
    return lax.ppermute(x, "z", [(i, i + by) for i in range(PLANES) if 0 <= i + by < PLANES])


def in_plane(x):
    return lax.all_to_all(x, PLANE, 0, 0, tiled=True)


def column_blocks():
    xl, core = lax.axis_index("xl"), lax.axis_index("c")
    own, other = 2 * xl, 2 * (1 - xl)
    return jnp.stack([own + core, own + 1 - core, other + core, other + 1 - core]).astype(jnp.int32)


def gathered_grad(out_grad, out_weight, q_proj, blocks):
    far = swap(out_grad, "xl")
    near = swap(out_grad, "c")
    start = grad_part((out_grad, near), blocks, out_weight)
    far, start = lax.optimization_barrier((far, start))
    both = swap(far, "c")
    return start, grad_part((far, both), blocks, out_weight, (start, q_proj))


def projected(attn, out_weight, width, blocks, after):
    def share(last, attn):
        send, keep = project(attn, blocks, last, out_weight, width, after)
        return keep.astype(f32) + swap(send, "c").astype(f32)

    part = share(3, attn).astype(bf16)
    part, attn = lax.optimization_barrier((part, attn))
    far = swap(part, "xl")
    return (share(1, attn) + far.astype(f32)).astype(bf16)


def shards(q_proj, k_proj, v_proj, out_weight, out_grad):
    tokens, cols = q_proj.shape
    rows = tokens * PLANE_DEVS
    coarse = rows // SHORT
    total = PLANES * coarse
    z = lax.axis_index("z").astype(jnp.int32).reshape(1)

    def array(*shape, dtype=bf16):
        return jax.ShapeDtypeStruct(shape, dtype)

    in_place = pl.BlockSpec(memory_space=pltpu.HBM)
    whole = pl.BlockSpec(memory_space=pltpu.VMEM)
    packed = call(
        pack_kernel,
        array(PLANE_DEVS, tokens + TAIL, 2 * HEAD_DIM),
        62,
        in_specs=[in_place] * 3,
        out_specs=whole,
        scratch_shapes=[pltpu.SemaphoreType.DMA((PLANE_DEVS, 4))],
    )(q_proj, k_proj, v_proj)
    own = in_plane(packed)
    blocks = column_blocks()
    early, pair_packed = gathered_grad(out_grad, out_weight, q_proj, blocks)
    near_rows = WINDOW + 2 * TAIL + WINDOW // SHORT
    near, far = call(
        pool_kernel,
        (array(near_rows, 256), array(coarse + TAIL, 256)),
        16,
        in_specs=[whole, in_place],
    )(own, early)
    near_in = planes_up(near, 1)
    far2_in = planes_up(far, 2)
    far3_in = planes_up(far, 3)
    pair = in_plane(pair_packed).reshape(rows, 2 * HEAD_DIM)

    part, sums = call(
        own_kernel,
        (array(rows - WINDOW, 256, dtype=f32), array(rows, 256, dtype=f32)),
        56,
        in_specs=[whole] * 2,
        out_specs=[whole] * 2,
        scratch_shapes=[pltpu.VMEM((rows, HEAD_DIM), bf16)] * 2
        + [pltpu.VMEM((HEAD_DIM, rows), bf16)] * 2
        + [pltpu.VMEM((rows, HEAD_DIM), f32)] * 2,
    )(own, pair)
    attn, fine, short, back1, back2, back3 = call(
        attention_kernel,
        (
            array(rows, 256),
            array(rows - WINDOW, 256, dtype=f32),
            array(coarse, 256, dtype=f32),
            array(near_rows, 256),
            array(coarse + TAIL, 256),
            array(coarse + TAIL, 256),
        ),
        62,
        in_specs=[pl.BlockSpec(memory_space=pltpu.SMEM)] + [whole] * 7,
        out_specs=[whole] * 6,
        scratch_shapes=[
            pltpu.VMEM((rows, HEAD_DIM), bf16),
            pltpu.VMEM((rows, HEAD_DIM), bf16),
            pltpu.VMEM((HEAD_DIM, rows), bf16),
            pltpu.VMEM((HEAD_DIM, rows), bf16),
            pltpu.VMEM((total, HEAD_DIM), bf16),
            pltpu.VMEM((total, HEAD_DIM), bf16),
            pltpu.VMEM((HEAD_DIM, total), bf16),
            pltpu.VMEM((HEAD_DIM, total), bf16),
            pltpu.VMEM((coarse, HEAD_DIM), bf16),
            pltpu.VMEM((coarse, HEAD_DIM), bf16),
            pltpu.VMEM((rows, HEAD_DIM), f32),
            pltpu.VMEM((rows, HEAD_DIM), f32),
            pltpu.VMEM((total, HEAD_DIM), f32),
            pltpu.VMEM((total, HEAD_DIM), f32),
            pltpu.VMEM((HEAD_DIM, coarse), bf16),
            pltpu.VMEM((HEAD_DIM, coarse), bf16),
            pltpu.VMEM((WINDOW // SHORT + TAIL, 256), bf16),
            pltpu.VMEM((WINDOW // SHORT + TAIL, 256), bf16),
            pltpu.VMEM((coarse + TAIL, HEAD_DIM), bf16),
            pltpu.VMEM((coarse + TAIL, HEAD_DIM), bf16),
        ],
    )(z, own, far, near_in, far2_in, far3_in, pair, part)

    back1_in = planes_up(back1, -1)
    back2_in = planes_up(back2, -2)
    back3_in = planes_up(back3, -3)
    attn_in = in_plane(attn.reshape(PLANE_DEVS, tokens, 256))
    finished = call(
        finish_kernel,
        array(PLANE_DEVS, tokens + TAIL, 256),
        32,
        scratch_shapes=[
            pltpu.VMEM((coarse + 2 * TAIL, 256), bf16),
            pltpu.VMEM((coarse + 2 * TAIL, 256), bf16),
        ],
    )(sums, fine, short, back1_in, back2_in, back3_in)
    mixed_out = projected(
        attn_in, out_weight, out_grad.shape[1], blocks, (finished,)
    )
    returned = in_plane(finished)
    grads = call(unpack_kernel, (array(tokens, cols),) * 3, 16)(attn_in, returned)
    return (mixed_out, *grads)


def solution(mesh):
    fine_mesh = Mesh(np.asarray(mesh.devices).reshape(4, 4, 2, 2, 2), ("z", "y", "xh", "xl", "c"))
    both = P(("z", "y", "xh"), ("xl", "c"))
    in_specs = (both, both, both, P(("xl", "c"), None), both)
    return jax.shard_map(
        shards, mesh=fine_mesh, in_specs=in_specs, out_specs=(both,) * 4, check_vma=False
    )
```

```python
import functools
import math

import jax
import jax.numpy as jnp
import numpy as np
from jax import lax
from jax.experimental import pallas as pl
from jax.experimental.pallas import tpu as pltpu
from jax.sharding import Mesh, PartitionSpec as P

HEAD_DIM = 128
SHORT = 4
WINDOW = 1024
PLANES = 4
PLANE_DEVS = 8
BLOCK = 256
TAIL = 16
LOG2E = math.log2(math.e)
SCALE = 1.0 / math.sqrt(HEAD_DIM)
COARSE_SCALE = 2.0 * SCALE
FAR = -1e30
PLANE = ("y", "xh")
bf16 = jnp.bfloat16
f32 = jnp.float32


def call(kernel, out_shape, vmem_mib, **rest):
    return pl.pallas_call(
        kernel,
        out_shape=out_shape,
        compiler_params=pltpu.CompilerParams(vmem_limit_bytes=vmem_mib * 1024 * 1024),
        **rest,
    )


def dot(a, b):
    return jnp.dot(a, b, preferred_element_type=f32)


def dot_nt(a, b):
    return lax.dot_general(a, b, (((1,), (1,)), ((), ())), preferred_element_type=f32)


def iota(shape, dim):
    return lax.broadcasted_iota(jnp.int32, shape, dim)


def split(x):
    high = x.astype(bf16)
    return high, (x - high.astype(f32)).astype(bf16)


def ones_where(mask):
    return jnp.where(mask, 1.0, 0.0).astype(bf16)


def pack_kernel(q_ref, k_ref, v_ref, out_ref, sems):
    tokens = q_ref.shape[0]
    last = q_ref.shape[1] // HEAD_DIM - 1
    copies = []
    for slot in range(PLANE_DEVS):
        cols = pl.ds(min(slot, last) * HEAD_DIM, HEAD_DIM)
        tail = q_ref.at[tokens - TAIL :, cols]
        pieces = (
            (k_ref.at[:, cols], out_ref.at[slot, 0:tokens, 0:128]),
            (v_ref.at[:, cols], out_ref.at[slot, 0:tokens, 128:256]),
            (tail, out_ref.at[slot, tokens:, 0:128]),
            (tail, out_ref.at[slot, tokens:, 128:256]),
        )
        for at, (source, target) in enumerate(pieces):
            copies.append(pltpu.make_async_copy(source, target, sems.at[slot, at]))
    for copy in copies:
        copy.start()
    for copy in copies:
        copy.wait()


def pooling(lead):
    shape = (BLOCK // SHORT, BLOCK + lead)
    back = iota(shape, 1) - lead - SHORT * iota(shape, 0)
    return ones_where((back <= 0) & (back > -SHORT))


def spreading():
    shape = (BLOCK, BLOCK // SHORT + TAIL)
    return ones_where((iota(shape, 0) + (SHORT - 1)) // SHORT == iota(shape, 1))


def pooled_rows(block, lead=None):
    rows = block if lead is None else jnp.concatenate([lead, block], 0)
    taken = pooling(0 if lead is None else TAIL)
    return (dot(taken, rows) * (1.0 / SHORT)).astype(bf16)


def pool_kernel(x_ref, after_ref, near_ref, far_ref):
    del after_ref
    devs, tokens = x_ref.shape[0], x_ref.shape[1] - TAIL
    step = tokens // SHORT
    half = WINDOW // SHORT
    coarse = devs * step
    for slot in range(devs):
        block = x_ref[slot, 0:tokens, :]
        lead = x_ref[slot - 1, tokens - TAIL : tokens, :] if slot else None
        far_ref[slot * step : (slot + 1) * step, :] = pooled_rows(block, lead)
        late = slot * tokens - (devs * tokens - WINDOW)
        if late >= 0:
            near_ref[late : late + tokens, :] = block
    far_ref[coarse : coarse + TAIL, :] = x_ref[devs - 1, tokens - TAIL : tokens, :]
    near_ref[WINDOW : WINDOW + TAIL, :] = x_ref[devs - 1, tokens:, :]
    near_ref[WINDOW + TAIL :, :] = far_ref[0 : half + TAIL, :]


def first_row_fixed(pooled, tail):
    kept = jnp.where(iota(tail.shape, 0) > TAIL - SHORT, tail.astype(f32), 0.0)
    lacking = jnp.sum(kept, 0, keepdims=True) * (1.0 / SHORT)
    head = pooled[0:TAIL, :].astype(f32)
    return jnp.where(iota(head.shape, 0) == 0, head + lacking, head).astype(bf16)


def transposed(ref, out, count):
    def body(i, carry):
        at = pl.multiple_of(i * BLOCK, BLOCK)
        out[:, pl.ds(at, BLOCK)] = ref[pl.ds(at, BLOCK), :].T
        return carry

    lax.fori_loop(0, count, body, 0)


def weights(scores, biases, factor):
    tops = [jnp.max(s, 0, keepdims=True) + b for s, b in zip(scores, biases)]
    top = functools.reduce(jnp.maximum, tops)
    exps = [jnp.exp2((s - (top - b)) * factor) for s, b in zip(scores, biases)]
    total = functools.reduce(jnp.add, [jnp.sum(e, 0, keepdims=True) for e in exps])
    inverse = 1.0 / total
    return jnp.concatenate([e * inverse for e in exps], 0)


def window_block(at, query, grad, biases, kx, vx, kxt, vxt, dk, dv):
    span = WINDOW + BLOCK
    reach = WINDOW // BLOCK
    row_at, col_at = iota((BLOCK, BLOCK), 0), iota((BLOCK, BLOCK), 1)
    scores = []
    for piece in range(reach + 1):
        s = dot_nt(kx[pl.ds(pl.multiple_of(at + piece * BLOCK, BLOCK), BLOCK), :], query)
        if piece == 0:
            s = jnp.where(row_at > col_at, s, FAR)
        if piece == reach:
            s = jnp.where(row_at <= col_at, s, FAR)
        scores.append(s)
    probs = weights(scores, biases, SCALE * LOG2E)
    rounded = probs.astype(bf16)
    out_t = dot(vxt[:, pl.ds(at, span)], rounded)
    delta = jnp.sum(grad.astype(f32).T * out_t, 0, keepdims=True)
    grad_probs = dot_nt(vx[pl.ds(at, span), :], grad)
    grad_scores = (probs * (grad_probs - delta)).astype(bf16)
    dk[pl.ds(at, span), :] += dot(grad_scores, query)
    dv[pl.ds(at, span), :] += dot(rounded, grad)
    return out_t, dot(kxt[:, pl.ds(at, span)], grad_scores).T * SCALE


def own_kernel(x_ref, pair_ref, part_ref, sums_ref, kx, vx, kxt, vxt, dk, dv):
    rows = pair_ref.shape[0]
    tokens = rows // PLANE_DEVS
    for slot in range(PLANE_DEVS):
        at = slot * tokens
        kx[at : at + tokens, :] = x_ref[slot, 0:tokens, 0:128]
        vx[at : at + tokens, :] = x_ref[slot, 0:tokens, 128:256]
    transposed(kx, kxt, rows // BLOCK)
    transposed(vx, vxt, rows // BLOCK)
    dk[...] = jnp.zeros_like(dk)
    dv[...] = jnp.zeros_like(dv)

    def body(block, carry):
        at = pl.multiple_of(block * BLOCK, BLOCK)
        own = pl.ds(pl.multiple_of(WINDOW + at, BLOCK), BLOCK)
        biases = [0.0] * (WINDOW // BLOCK + 1)
        out_t, query_grad = window_block(
            at, pair_ref[own, 0:128], pair_ref[own, 128:256], biases, kx, vx, kxt, vxt, dk, dv
        )
        part_ref[pl.ds(at, BLOCK), 0:128] = out_t.T
        part_ref[pl.ds(at, BLOCK), 128:256] = query_grad
        return carry

    lax.fori_loop(0, (rows - WINDOW) // BLOCK, body, 0, unroll=4)
    sums_ref[:, 0:128] = dk[...] * SCALE
    sums_ref[:, 128:256] = dv[...]


def attention_kernel(
    z_ref,
    x_ref,
    own_ref,
    near_ref,
    far2_ref,
    far3_ref,
    pair_ref,
    part_ref,
    attn_ref,
    fine_ref,
    coarse_ref,
    back1_ref,
    back2_ref,
    back3_ref,
    kx,
    vx,
    kxt,
    vxt,
    kc,
    vc,
    kct,
    vct,
    pq,
    gp,
    dkx,
    dvx,
    dkc,
    dvc,
    high_t,
    low_t,
    high,
    low,
    query_high,
    query_low,
):
    z = z_ref[0]
    rows = pair_ref.shape[0]
    tokens = rows // PLANE_DEVS
    coarse = rows // SHORT
    half = WINDOW // SHORT
    step = BLOCK // SHORT
    reach = WINDOW // BLOCK

    kx[0:WINDOW, :] = near_ref[0:WINDOW, 0:128]
    vx[0:WINDOW, :] = near_ref[0:WINDOW, 128:256]
    for slot in range((rows - WINDOW) // tokens):
        at = WINDOW + slot * tokens
        kx[at : at + tokens, :] = x_ref[slot, 0:tokens, 0:128]
        vx[at : at + tokens, :] = x_ref[slot, 0:tokens, 128:256]

    transposed(kx, kxt, rows // BLOCK)
    transposed(vx, vxt, rows // BLOCK)

    tails = [
        near_ref[WINDOW - TAIL : WINDOW, :],
        far2_ref[coarse : coarse + TAIL, :],
        far3_ref[coarse : coarse + TAIL, :],
    ]
    base = WINDOW + TAIL
    for piece in range(reach):
        at = coarse + half + piece * step
        block = near_ref[piece * BLOCK : (piece + 1) * BLOCK, :]
        lead = near_ref[piece * BLOCK - TAIL : piece * BLOCK, :] if piece else None
        rest = pooled_rows(block, lead)
        kc[at : at + step, :] = rest[:, 0:128]
        vc[at : at + step, :] = rest[:, 128:256]
    sources = ((own_ref, coarse), (near_ref.at[base:], half + TAIL), (far2_ref, coarse), (far3_ref, coarse))
    for slot, (source, count) in enumerate(sources):
        at = slot * coarse
        kc[at : at + count, :] = source[0:count, 0:128]
        vc[at : at + count, :] = source[0:count, 128:256]
        if slot + 1 < PLANES:
            fixed = first_row_fixed(source[0:TAIL, :], tails[slot])
            kc[at : at + TAIL, :] = fixed[:, 0:128]
            vc[at : at + TAIL, :] = fixed[:, 128:256]
    transposed(kc, kct, PLANES * coarse // BLOCK)
    transposed(vc, vct, PLANES * coarse // BLOCK)

    shape = (step, BLOCK)
    offset = iota(shape, 1) - SHORT * iota(shape, 0)
    taken = ones_where((offset >= 0) & (offset < SHORT))
    for block in range(rows // BLOCK):
        at = block * BLOCK
        lead = pair_ref[at - TAIL : at, 0:128] if block else near_ref[WINDOW : WINDOW + TAIL, 0:128]
        pq[block * step : (block + 1) * step, :] = pooled_rows(pair_ref[at : at + BLOCK, 0:128], lead)
        gp[block * step : (block + 1) * step, :] = dot(
            taken, pair_ref[at : at + BLOCK, 128:256]
        ).astype(bf16)

    row_at, col_at = iota((BLOCK, BLOCK), 0), iota((BLOCK, BLOCK), 1)
    diagonal = row_at <= col_at
    for block in range(coarse // BLOCK):
        at = block * BLOCK
        query = pq[at : at + BLOCK, :]
        grad = gp[at : at + BLOCK, :]
        scores, biases, keys, values = [], [], [], []
        for piece in range(block + 1):
            s = dot_nt(kc[piece * BLOCK : (piece + 1) * BLOCK, :], query)
            scores.append(jnp.where(diagonal, s, FAR) if piece == block else s)
            biases.append(0.0)
        for slot in range(1, PLANES):
            s = dot_nt(kc[slot * coarse : (slot + 1) * coarse, :], query)
            scores.append(s)
            biases.append(jnp.where(z >= slot, 0.0, FAR))
        probs = weights(scores, biases, COARSE_SCALE * LOG2E)
        rounded = probs.astype(bf16)
        own = at + BLOCK
        parts = ((0, own, 0), (coarse, PLANES * coarse, own))
        out_t = functools.reduce(
            jnp.add, [dot(vct[:, a:b], rounded[c : c + b - a]) for a, b, c in parts]
        )
        grad_t = grad.astype(f32).T
        delta = jnp.sum(grad_t * out_t, 0, keepdims=True)
        high_t[:, at : at + BLOCK], low_t[:, at : at + BLOCK] = split(out_t)
        query_grad_t = jnp.zeros((HEAD_DIM, BLOCK), f32)
        for a, b, c in parts:
            grad_probs = dot_nt(vc[a:b, :], grad)
            grad_scores = (probs[c : c + b - a] * (grad_probs - delta)).astype(bf16)
            query_grad_t += dot(kct[:, a:b], grad_scores)
            dk = dot(grad_scores, query) * COARSE_SCALE
            dv = dot(rounded[c : c + b - a], grad)
            if block == 0:
                dkc[a:b, :] = dk
                dvc[a:b, :] = dv
                if a == 0:
                    dkc[b:coarse, :] = jnp.zeros((coarse - b, HEAD_DIM), f32)
                    dvc[b:coarse, :] = jnp.zeros((coarse - b, HEAD_DIM), f32)
            else:
                dkc[a:b, :] += dk
                dvc[a:b, :] += dv
        query_grad = query_grad_t.T * COARSE_SCALE
        query_high[at : at + BLOCK, :], query_low[at : at + BLOCK, :] = split(query_grad)
    query_high[coarse:, :] = jnp.zeros((TAIL, HEAD_DIM), bf16)
    query_low[coarse:, :] = jnp.zeros((TAIL, HEAD_DIM), bf16)
    coarse_ref[:, 0:128] = dkc[0:coarse, :]
    coarse_ref[:, 128:256] = dvc[0:coarse, :]

    dkx[...] = jnp.zeros_like(dkx)
    dvx[...] = jnp.zeros_like(dvx)

    def short_out(block):
        pair = pl.multiple_of(block // 2 * (2 * step), 2 * step)
        shape = (2 * step, BLOCK)
        spread = ones_where(iota(shape, 0) == block % 2 * step + iota(shape, 1) // SHORT)
        short_t = dot(high_t[:, pl.ds(pair, 2 * step)], spread)
        return short_t + dot(low_t[:, pl.ds(pair, 2 * step)], spread)

    def short_query_grad(block):
        below = pl.ds(pl.multiple_of(block * step, step), step + TAIL)
        spread = dot(spreading(), query_high[below, :]) + dot(spreading(), query_low[below, :])
        return spread * (1.0 / SHORT)

    def window(block, carry):
        at = pl.multiple_of(block * BLOCK, BLOCK)
        here = pl.ds(at, BLOCK)
        biases = [jnp.where((z == 0) & (block + piece < reach), FAR, 0.0) for piece in range(reach + 1)]
        out_t, query_grad = window_block(
            at, pair_ref[here, 0:128], pair_ref[here, 128:256], biases, kx, vx, kxt, vxt, dkx, dvx
        )
        attn_ref[here, 0:128] = (out_t + short_out(block)).T.astype(bf16)
        attn_ref[here, 128:256] = (query_grad + short_query_grad(block)).astype(bf16)
        late = pl.ds(pl.multiple_of(WINDOW + at, BLOCK), BLOCK)
        attn_ref[late, 0:128] = (part_ref[here, 0:128] + short_out(block + reach).T).astype(bf16)
        attn_ref[late, 128:256] = (part_ref[here, 128:256] + short_query_grad(block + reach)).astype(bf16)
        return carry

    lax.fori_loop(0, reach, window, 0, unroll=4)
    fine_ref[:, 0:128] = dkx[WINDOW:, :] * SCALE
    fine_ref[:, 128:256] = dvx[WINDOW:, :]

    first = iota((TAIL, HEAD_DIM), 0) == 0
    for cols, short in ((slice(0, 128), dkc), (slice(128, 256), dvc)):
        high[0:half, cols], low[0:half, cols] = split(short[2 * coarse - half : 2 * coarse, :])
        above = jnp.where(first, short[0:TAIL, :], 0.0)
        high[half:, cols], low[half:, cols] = split(above)
    taken = spreading()
    for piece in range(reach):
        at = piece * BLOCK
        below = piece * step
        spread = dot(taken, high[below : below + step + TAIL, :])
        spread += dot(taken, low[below : below + step + TAIL, :])
        spread = spread * (1.0 / SHORT)
        back1_ref[at : at + BLOCK, 0:128] = (
            dkx[at : at + BLOCK, :] * SCALE + spread[:, 0:128]
        ).astype(bf16)
        back1_ref[at : at + BLOCK, 128:256] = (
            dvx[at : at + BLOCK, :] + spread[:, 128:256]
        ).astype(bf16)
    query_row = jnp.where(first, query_high[0:TAIL, :].astype(f32), 0.0).astype(bf16)
    back1_ref[WINDOW:base, 0:128] = query_row
    back1_ref[WINDOW:base, 128:256] = query_row
    back1_ref[base:, 0:128] = dkc[coarse : coarse + half + TAIL, :].astype(bf16)
    back1_ref[base:, 128:256] = dvc[coarse : coarse + half + TAIL, :].astype(bf16)
    for slot, ref in ((2, back2_ref), (3, back3_ref)):
        at = slot * coarse
        above = at - coarse
        for cols, short in ((slice(0, 128), dkc), (slice(128, 256), dvc)):
            ref[0:coarse, cols] = short[at : at + coarse, :].astype(bf16)
            row = jnp.where(first, short[above : above + TAIL, :], 0.0)
            ref[coarse : coarse + TAIL, cols] = row.astype(bf16)


def finish_kernel(
    sums_ref, fine_ref, coarse_ref, back1_ref, back2_ref, back3_ref, round_ref, out_ref, high, low
):
    rows = sums_ref.shape[0]
    tokens = rows // PLANE_DEVS
    coarse = rows // SHORT
    half = coarse - WINDOW // SHORT
    step = BLOCK // SHORT
    base = WINDOW + TAIL
    part = half + TAIL
    ups = (back2_ref, back3_ref, round_ref)
    total = coarse_ref[...]
    for up in ups:
        total += up[0:coarse, :].astype(f32)
    near = total[0:part, :] + back1_ref[base:, :].astype(f32)
    high[0:part, :], low[0:part, :] = split(near)
    high[part : part + half, :], low[part : part + half, :] = split(total[half:, :])
    extra = functools.reduce(jnp.add, [up[coarse : coarse + TAIL, :].astype(f32) for up in ups])
    high[part + half :, :], low[part + half :, :] = split(extra)
    taken = spreading()
    for block in range(rows // BLOCK):
        at = block * BLOCK
        late = at - (rows - WINDOW)
        below = block * step if late < 0 else part + late // SHORT
        spread = dot(taken, high[below : below + step + TAIL, :])
        spread += dot(taken, low[below : below + step + TAIL, :])
        result = sums_ref[at : at + BLOCK, :] + spread * (1.0 / SHORT)
        if late < 0:
            result = result + fine_ref[at : at + BLOCK, :]
        else:
            result = result + back1_ref[late : late + BLOCK, :].astype(f32)
        out_ref[block, 0:tokens, :] = result.astype(bf16)
        out_ref[block, tokens:, :] = jnp.zeros((TAIL, 256), bf16)
    out_ref[PLANE_DEVS - 1, tokens:, :] = back1_ref[WINDOW:base, :]


def unpack_kernel(pair_ref, x_ref, q_ref, k_ref, v_ref):
    tokens = q_ref.shape[0]
    last = iota((TAIL, HEAD_DIM), 0) > TAIL - SHORT
    for slot in range(q_ref.shape[1] // HEAD_DIM):
        cols = pl.ds(slot * HEAD_DIM, HEAD_DIM)
        k_ref[:, cols] = x_ref[slot, 0:tokens, 0:128]
        v_ref[:, cols] = x_ref[slot, 0:tokens, 128:256]
        q_ref[0 : tokens - TAIL, cols] = pair_ref[slot, 0 : tokens - TAIL, 128:256]
        above = jnp.sum(x_ref[slot, tokens:, 0:128].astype(f32), 0, keepdims=True) * (1.0 / SHORT)
        rest = pair_ref[slot, tokens - TAIL :, 128:256].astype(f32)
        q_ref[tokens - TAIL :, cols] = (rest + jnp.where(last, above, 0.0)).astype(bf16)


def grad_product(halves, a_ref, b_ref, w_ref, total, start):
    at = pl.program_id(0)
    depth = w_ref.shape[1]
    for piece, ref in enumerate((a_ref, b_ref)):
        for half in range(halves):

            @pl.when(at == piece * halves + half)
            def _():
                product = dot_nt(w_ref[...], ref[:, half * depth : (half + 1) * depth])
                if piece + half > 0:
                    total[...] += product
                elif start is None:
                    total[...] = product
                else:
                    total[...] = start[...] + product


def grad_near_kernel(halves, order_ref, a_ref, b_ref, w_ref, total):
    grad_product(halves, a_ref, b_ref, w_ref, total, None)


def grad_far_kernel(halves, order_ref, a_ref, b_ref, w_ref, start, q_ref, out_ref, total):
    grad_product(halves, a_ref, b_ref, w_ref, total, start)

    @pl.when(pl.program_id(0) == pl.num_programs(0) - 1)
    def _():
        last = total.shape[0] // HEAD_DIM - 1
        for slot in range(PLANE_DEVS):
            head = slice(min(slot, last) * HEAD_DIM, (min(slot, last) + 1) * HEAD_DIM)
            out_ref[slot, :, 0:128] = q_ref[:, head]
            out_ref[slot, :, 128:256] = total[head, :].T.astype(bf16)


def grad_part(pieces, order, weight, rest=()):
    rows, width = pieces[0].shape
    depth = weight.shape[0]
    halves = 1
    tile = width // halves

    first = 2 if rest else 0

    def whole(shape):
        return pl.BlockSpec(shape, lambda i, o: (0,) * len(shape))

    packed = (PLANE_DEVS, rows, 2 * HEAD_DIM)
    return pl.pallas_call(
        functools.partial(grad_far_kernel if rest else grad_near_kernel, halves),
        out_shape=jax.ShapeDtypeStruct(packed, bf16) if rest else jax.ShapeDtypeStruct((depth, rows), f32),
        grid_spec=pltpu.PrefetchScalarGridSpec(
            num_scalar_prefetch=1,
            grid=(2 * halves,),
            in_specs=[whole((rows, width))] * 2
            + [pl.BlockSpec((depth, tile), lambda i, o: (0, o[first + i // halves] * halves + i % halves))]
            + [whole(x.shape) for x in rest],
            out_specs=whole(packed if rest else (depth, rows)),
            scratch_shapes=[pltpu.VMEM((depth, rows), f32)] if rest else [],
        ),
        compiler_params=pltpu.CompilerParams(vmem_limit_bytes=62 * 1024 * 1024),
    )(order, *pieces, weight, *rest)


def project_kernel(halves, order_ref, attn_ref, w_ref, *refs):
    send_ref, keep_ref, rows_ref = refs[-3:]
    at = pl.program_id(0)
    heads = w_ref.shape[0] // HEAD_DIM
    tile = w_ref.shape[1]

    @pl.when(at == 0)
    def _():
        for slot in range(heads):
            rows_ref[:, slot * HEAD_DIM : (slot + 1) * HEAD_DIM] = attn_ref[slot, :, 0:128]

    product = dot(rows_ref[...], w_ref[...]).astype(bf16)
    for half in range(halves):

        @pl.when(at == half)
        def _():
            send_ref[:, half * tile : (half + 1) * tile] = product

        @pl.when(at == halves + half)
        def _():
            keep_ref[:, half * tile : (half + 1) * tile] = product


def project(attn, order, last, weight, width, after):
    rows = attn.shape[1]
    depth = weight.shape[0]
    halves = 1
    tile = width // halves
    out = jax.ShapeDtypeStruct((rows, width), bf16)
    return pl.pallas_call(
        functools.partial(project_kernel, halves),
        out_shape=(out, out),
        grid_spec=pltpu.PrefetchScalarGridSpec(
            num_scalar_prefetch=1,
            grid=(2 * halves,),
            in_specs=[
                pl.BlockSpec(attn.shape, lambda i, o: (0, 0, 0)),
                pl.BlockSpec((depth, tile), lambda i, o: (0, o[last - i // halves] * halves + i % halves)),
            ]
            + [pl.BlockSpec(memory_space=pltpu.HBM)] * len(after),
            out_specs=[pl.BlockSpec((rows, width), lambda i, o: (0, 0))] * 2,
            scratch_shapes=[pltpu.VMEM((rows, depth), bf16)],
        ),
        compiler_params=pltpu.CompilerParams(vmem_limit_bytes=62 * 1024 * 1024),
    )(order, attn, weight, *after)


def swap(x, axis):
    return lax.ppermute(x, axis, [(0, 1), (1, 0)])


def planes_up(x, by):
    return lax.ppermute(x, "z", [(i, i + by) for i in range(PLANES) if 0 <= i + by < PLANES])


def in_plane(x):
    return lax.all_to_all(x, PLANE, 0, 0, tiled=True)


def column_blocks():
    xl, core = lax.axis_index("xl"), lax.axis_index("c")
    own, other = 2 * xl, 2 * (1 - xl)
    return jnp.stack([own + core, own + 1 - core, other + core, other + 1 - core]).astype(jnp.int32)


def gathered_grad(out_grad, out_weight, q_proj, blocks):
    far = swap(out_grad, "xl")
    near = swap(out_grad, "c")
    start = grad_part((out_grad, near), blocks, out_weight)
    far, start = lax.optimization_barrier((far, start))
    both = swap(far, "c")
    return start, grad_part((far, both), blocks, out_weight, (start, q_proj))


def projected(attn, out_weight, width, blocks, after):
    def share(last, attn):
        send, keep = project(attn, blocks, last, out_weight, width, after)
        return keep.astype(f32) + swap(send, "c").astype(f32)

    part = share(3, attn).astype(bf16)
    part, attn = lax.optimization_barrier((part, attn))
    far = swap(part, "xl")
    return (share(1, attn) + far.astype(f32)).astype(bf16)


def shards(q_proj, k_proj, v_proj, out_weight, out_grad):
    tokens, cols = q_proj.shape
    rows = tokens * PLANE_DEVS
    coarse = rows // SHORT
    total = PLANES * coarse
    z = lax.axis_index("z").astype(jnp.int32).reshape(1)

    def array(*shape, dtype=bf16):
        return jax.ShapeDtypeStruct(shape, dtype)

    in_place = pl.BlockSpec(memory_space=pltpu.HBM)
    whole = pl.BlockSpec(memory_space=pltpu.VMEM)
    packed = call(
        pack_kernel,
        array(PLANE_DEVS, tokens + TAIL, 2 * HEAD_DIM),
        62,
        in_specs=[in_place] * 3,
        out_specs=whole,
        scratch_shapes=[pltpu.SemaphoreType.DMA((PLANE_DEVS, 4))],
    )(q_proj, k_proj, v_proj)
    own = in_plane(packed)
    blocks = column_blocks()
    early, pair_packed = gathered_grad(out_grad, out_weight, q_proj, blocks)
    near_rows = WINDOW + 2 * TAIL + WINDOW // SHORT
    near, far = call(
        pool_kernel,
        (array(near_rows, 256), array(coarse + TAIL, 256)),
        16,
        in_specs=[whole, in_place],
    )(own, early)
    near_in = planes_up(near, 1)
    far2_in = planes_up(far, 2)
    far3_in = planes_up(far, 3)
    pair = in_plane(pair_packed).reshape(rows, 2 * HEAD_DIM)

    part, sums = call(
        own_kernel,
        (array(rows - WINDOW, 256, dtype=f32), array(rows, 256, dtype=f32)),
        56,
        in_specs=[whole] * 2,
        out_specs=[whole] * 2,
        scratch_shapes=[pltpu.VMEM((rows, HEAD_DIM), bf16)] * 2
        + [pltpu.VMEM((HEAD_DIM, rows), bf16)] * 2
        + [pltpu.VMEM((rows, HEAD_DIM), f32)] * 2,
    )(own, pair)
    attn, fine, short, back1, back2, back3 = call(
        attention_kernel,
        (
            array(rows, 256),
            array(rows - WINDOW, 256, dtype=f32),
            array(coarse, 256, dtype=f32),
            array(near_rows, 256),
            array(coarse + TAIL, 256),
            array(coarse + TAIL, 256),
        ),
        62,
        in_specs=[pl.BlockSpec(memory_space=pltpu.SMEM)] + [whole] * 7,
        out_specs=[whole] * 6,
        scratch_shapes=[
            pltpu.VMEM((rows, HEAD_DIM), bf16),
            pltpu.VMEM((rows, HEAD_DIM), bf16),
            pltpu.VMEM((HEAD_DIM, rows), bf16),
            pltpu.VMEM((HEAD_DIM, rows), bf16),
            pltpu.VMEM((total, HEAD_DIM), bf16),
            pltpu.VMEM((total, HEAD_DIM), bf16),
            pltpu.VMEM((HEAD_DIM, total), bf16),
            pltpu.VMEM((HEAD_DIM, total), bf16),
            pltpu.VMEM((coarse, HEAD_DIM), bf16),
            pltpu.VMEM((coarse, HEAD_DIM), bf16),
            pltpu.VMEM((rows, HEAD_DIM), f32),
            pltpu.VMEM((rows, HEAD_DIM), f32),
            pltpu.VMEM((total, HEAD_DIM), f32),
            pltpu.VMEM((total, HEAD_DIM), f32),
            pltpu.VMEM((HEAD_DIM, coarse), bf16),
            pltpu.VMEM((HEAD_DIM, coarse), bf16),
            pltpu.VMEM((WINDOW // SHORT + TAIL, 256), bf16),
            pltpu.VMEM((WINDOW // SHORT + TAIL, 256), bf16),
            pltpu.VMEM((coarse + TAIL, HEAD_DIM), bf16),
            pltpu.VMEM((coarse + TAIL, HEAD_DIM), bf16),
        ],
    )(z, own, far, near_in, far2_in, far3_in, pair, part)

    back1_in = planes_up(back1, -1)
    halfway = lax.ppermute(back2, "z", [(3, 0)])
    back3_in = planes_up(back3, -3)
    back2_in = lax.ppermute(back2, "z", [(2, 0)])
    round_in = lax.ppermute(halfway, "z", [(0, 1)])
    attn_in = in_plane(attn.reshape(PLANE_DEVS, tokens, 256))
    finished = call(
        finish_kernel,
        array(PLANE_DEVS, tokens + TAIL, 256),
        32,
        scratch_shapes=[
            pltpu.VMEM((coarse + 2 * TAIL, 256), bf16),
            pltpu.VMEM((coarse + 2 * TAIL, 256), bf16),
        ],
    )(sums, fine, short, back1_in, back2_in, back3_in, round_in)
    mixed_out = projected(
        attn_in, out_weight, out_grad.shape[1], blocks, (finished,)
    )
    returned = in_plane(finished)
    grads = call(unpack_kernel, (array(tokens, cols),) * 3, 16)(attn_in, returned)
    return (mixed_out, *grads)


def solution(mesh):
    fine_mesh = Mesh(np.asarray(mesh.devices).reshape(4, 4, 2, 2, 2), ("z", "y", "xh", "xl", "c"))
    both = P(("z", "y", "xh"), ("xl", "c"))
    in_specs = (both, both, both, P(("xl", "c"), None), both)
    return jax.shard_map(
        shards, mesh=fine_mesh, in_specs=in_specs, out_specs=(both,) * 4, check_vma=False
    )
```

```python
import functools
import math

import jax
import jax.numpy as jnp
import numpy as np
from jax import lax
from jax.experimental import pallas as pl
from jax.experimental.pallas import tpu as pltpu
from jax.sharding import Mesh, PartitionSpec as P

HEAD_DIM = 128
SHORT = 4
WINDOW = 1024
PLANES = 4
PLANE_DEVS = 8
BLOCK = 256
TAIL = 16
LOG2E = math.log2(math.e)
SCALE = 1.0 / math.sqrt(HEAD_DIM)
COARSE_SCALE = 2.0 * SCALE
FAR = -1e30
PLANE = ("y", "xh")
bf16 = jnp.bfloat16
f32 = jnp.float32


def call(kernel, out_shape, vmem_mib, **rest):
    return pl.pallas_call(
        kernel,
        out_shape=out_shape,
        compiler_params=pltpu.CompilerParams(vmem_limit_bytes=vmem_mib * 1024 * 1024),
        **rest,
    )


def dot(a, b):
    return jnp.dot(a, b, preferred_element_type=f32)


def dot_nt(a, b):
    return lax.dot_general(a, b, (((1,), (1,)), ((), ())), preferred_element_type=f32)


def iota(shape, dim):
    return lax.broadcasted_iota(jnp.int32, shape, dim)


def split(x):
    high = x.astype(bf16)
    return high, (x - high.astype(f32)).astype(bf16)


def ones_where(mask):
    return jnp.where(mask, 1.0, 0.0).astype(bf16)


def pack_kernel(q_ref, k_ref, v_ref, out_ref, sems):
    tokens = q_ref.shape[0]
    last = q_ref.shape[1] // HEAD_DIM - 1
    copies = []
    for slot in range(PLANE_DEVS):
        cols = pl.ds(min(slot, last) * HEAD_DIM, HEAD_DIM)
        tail = q_ref.at[tokens - TAIL :, cols]
        pieces = (
            (k_ref.at[:, cols], out_ref.at[slot, 0:tokens, 0:128]),
            (v_ref.at[:, cols], out_ref.at[slot, 0:tokens, 128:256]),
            (tail, out_ref.at[slot, tokens:, 0:128]),
            (tail, out_ref.at[slot, tokens:, 128:256]),
        )
        for at, (source, target) in enumerate(pieces):
            copies.append(pltpu.make_async_copy(source, target, sems.at[slot, at]))
    for copy in copies:
        copy.start()
    for copy in copies:
        copy.wait()


def pooling(lead):
    shape = (BLOCK // SHORT, BLOCK + lead)
    back = iota(shape, 1) - lead - SHORT * iota(shape, 0)
    return ones_where((back <= 0) & (back > -SHORT))


def spreading():
    shape = (BLOCK, BLOCK // SHORT + TAIL)
    return ones_where((iota(shape, 0) + (SHORT - 1)) // SHORT == iota(shape, 1))


def pooled_rows(block, lead=None):
    rows = block if lead is None else jnp.concatenate([lead, block], 0)
    taken = pooling(0 if lead is None else TAIL)
    return (dot(taken, rows) * (1.0 / SHORT)).astype(bf16)


def pool_kernel(x_ref, after_ref, near_ref, far_ref):
    del after_ref
    devs, tokens = x_ref.shape[0], x_ref.shape[1] - TAIL
    step = tokens // SHORT
    half = WINDOW // SHORT
    coarse = devs * step
    for slot in range(devs):
        block = x_ref[slot, 0:tokens, :]
        lead = x_ref[slot - 1, tokens - TAIL : tokens, :] if slot else None
        far_ref[slot * step : (slot + 1) * step, :] = pooled_rows(block, lead)
        late = slot * tokens - (devs * tokens - WINDOW)
        if late >= 0:
            near_ref[late : late + tokens, :] = block
    far_ref[coarse : coarse + TAIL, :] = x_ref[devs - 1, tokens - TAIL : tokens, :]
    near_ref[WINDOW : WINDOW + TAIL, :] = x_ref[devs - 1, tokens:, :]
    near_ref[WINDOW + TAIL :, :] = far_ref[0 : half + TAIL, :]


def first_row_fixed(pooled, tail):
    kept = jnp.where(iota(tail.shape, 0) > TAIL - SHORT, tail.astype(f32), 0.0)
    lacking = jnp.sum(kept, 0, keepdims=True) * (1.0 / SHORT)
    head = pooled[0:TAIL, :].astype(f32)
    return jnp.where(iota(head.shape, 0) == 0, head + lacking, head).astype(bf16)


def transposed(ref, out, count):
    def body(i, carry):
        at = pl.multiple_of(i * BLOCK, BLOCK)
        out[:, pl.ds(at, BLOCK)] = ref[pl.ds(at, BLOCK), :].T
        return carry

    lax.fori_loop(0, count, body, 0)


def weights(scores, biases, factor):
    tops = [jnp.max(s, 0, keepdims=True) + b for s, b in zip(scores, biases)]
    top = functools.reduce(jnp.maximum, tops)
    exps = [jnp.exp2((s - (top - b)) * factor) for s, b in zip(scores, biases)]
    total = functools.reduce(jnp.add, [jnp.sum(e, 0, keepdims=True) for e in exps])
    inverse = 1.0 / total
    return jnp.concatenate([e * inverse for e in exps], 0)


def window_block(at, query, grad, biases, kx, vx, kxt, vxt, dk, dv):
    span = WINDOW + BLOCK
    reach = WINDOW // BLOCK
    row_at, col_at = iota((BLOCK, BLOCK), 0), iota((BLOCK, BLOCK), 1)
    scores = []
    for piece in range(reach + 1):
        s = dot_nt(kx[pl.ds(pl.multiple_of(at + piece * BLOCK, BLOCK), BLOCK), :], query)
        if piece == 0:
            s = jnp.where(row_at > col_at, s, FAR)
        if piece == reach:
            s = jnp.where(row_at <= col_at, s, FAR)
        scores.append(s)
    probs = weights(scores, biases, SCALE * LOG2E)
    rounded = probs.astype(bf16)
    out_t = dot(vxt[:, pl.ds(at, span)], rounded)
    delta = jnp.sum(grad.astype(f32).T * out_t, 0, keepdims=True)
    grad_probs = dot_nt(vx[pl.ds(at, span), :], grad)
    grad_scores = (probs * (grad_probs - delta)).astype(bf16)
    dk[pl.ds(at, span), :] += dot(grad_scores, query)
    dv[pl.ds(at, span), :] += dot(rounded, grad)
    return out_t, dot(kxt[:, pl.ds(at, span)], grad_scores).T * SCALE


def own_kernel(x_ref, pair_ref, part_ref, sums_ref, kx, vx, kxt, vxt, dk, dv):
    rows = pair_ref.shape[0]
    tokens = rows // PLANE_DEVS
    for slot in range(PLANE_DEVS):
        at = slot * tokens
        kx[at : at + tokens, :] = x_ref[slot, 0:tokens, 0:128]
        vx[at : at + tokens, :] = x_ref[slot, 0:tokens, 128:256]
    transposed(kx, kxt, rows // BLOCK)
    transposed(vx, vxt, rows // BLOCK)
    dk[...] = jnp.zeros_like(dk)
    dv[...] = jnp.zeros_like(dv)

    def body(block, carry):
        at = pl.multiple_of(block * BLOCK, BLOCK)
        own = pl.ds(pl.multiple_of(WINDOW + at, BLOCK), BLOCK)
        biases = [0.0] * (WINDOW // BLOCK + 1)
        out_t, query_grad = window_block(
            at, pair_ref[own, 0:128], pair_ref[own, 128:256], biases, kx, vx, kxt, vxt, dk, dv
        )
        part_ref[pl.ds(at, BLOCK), 0:128] = out_t.T
        part_ref[pl.ds(at, BLOCK), 128:256] = query_grad
        return carry

    lax.fori_loop(0, (rows - WINDOW) // BLOCK, body, 0, unroll=4)
    sums_ref[:, 0:128] = dk[...] * SCALE
    sums_ref[:, 128:256] = dv[...]


def short_kernel(
    z_ref,
    own_ref,
    near_ref,
    far2_ref,
    far3_ref,
    pair_ref,
    after_ref,
    coarse_ref,
    back2_ref,
    back3_ref,
    slot1_ref,
    high,
    low,
    high_t,
    low_t,
    query_high,
    query_low,
    kc,
    vc,
    kct,
    vct,
    pq,
    gp,
    dkc,
    dvc,
):
    del after_ref
    z = z_ref[0]
    rows = pair_ref.shape[0]
    coarse = rows // SHORT
    half = WINDOW // SHORT
    step = BLOCK // SHORT
    reach = WINDOW // BLOCK

    tails = [
        near_ref[WINDOW - TAIL : WINDOW, :],
        far2_ref[coarse : coarse + TAIL, :],
        far3_ref[coarse : coarse + TAIL, :],
    ]
    base = WINDOW + TAIL
    for piece in range(reach):
        at = coarse + half + piece * step
        block = near_ref[piece * BLOCK : (piece + 1) * BLOCK, :]
        lead = near_ref[piece * BLOCK - TAIL : piece * BLOCK, :] if piece else None
        rest = pooled_rows(block, lead)
        kc[at : at + step, :] = rest[:, 0:128]
        vc[at : at + step, :] = rest[:, 128:256]
    sources = ((own_ref, coarse), (near_ref.at[base:], half + TAIL), (far2_ref, coarse), (far3_ref, coarse))
    for slot, (source, count) in enumerate(sources):
        at = slot * coarse
        kc[at : at + count, :] = source[0:count, 0:128]
        vc[at : at + count, :] = source[0:count, 128:256]
        if slot + 1 < PLANES:
            fixed = first_row_fixed(source[0:TAIL, :], tails[slot])
            kc[at : at + TAIL, :] = fixed[:, 0:128]
            vc[at : at + TAIL, :] = fixed[:, 128:256]
    transposed(kc, kct, PLANES * coarse // BLOCK)
    transposed(vc, vct, PLANES * coarse // BLOCK)

    shape = (step, BLOCK)
    offset = iota(shape, 1) - SHORT * iota(shape, 0)
    taken = ones_where((offset >= 0) & (offset < SHORT))
    for block in range(rows // BLOCK):
        at = block * BLOCK
        lead = pair_ref[at - TAIL : at, 0:128] if block else near_ref[WINDOW : WINDOW + TAIL, 0:128]
        pq[block * step : (block + 1) * step, :] = pooled_rows(pair_ref[at : at + BLOCK, 0:128], lead)
        gp[block * step : (block + 1) * step, :] = dot(
            taken, pair_ref[at : at + BLOCK, 128:256]
        ).astype(bf16)

    row_at, col_at = iota((BLOCK, BLOCK), 0), iota((BLOCK, BLOCK), 1)
    diagonal = row_at <= col_at
    for block in range(coarse // BLOCK):
        at = block * BLOCK
        query = pq[at : at + BLOCK, :]
        grad = gp[at : at + BLOCK, :]
        scores, biases, keys, values = [], [], [], []
        for piece in range(block + 1):
            s = dot_nt(kc[piece * BLOCK : (piece + 1) * BLOCK, :], query)
            scores.append(jnp.where(diagonal, s, FAR) if piece == block else s)
            biases.append(0.0)
        for slot in range(1, PLANES):
            s = dot_nt(kc[slot * coarse : (slot + 1) * coarse, :], query)
            scores.append(s)
            biases.append(jnp.where(z >= slot, 0.0, FAR))
        probs = weights(scores, biases, COARSE_SCALE * LOG2E)
        rounded = probs.astype(bf16)
        own = at + BLOCK
        parts = ((0, own, 0), (coarse, PLANES * coarse, own))
        out_t = functools.reduce(
            jnp.add, [dot(vct[:, a:b], rounded[c : c + b - a]) for a, b, c in parts]
        )
        grad_t = grad.astype(f32).T
        delta = jnp.sum(grad_t * out_t, 0, keepdims=True)
        high_t[:, at : at + BLOCK], low_t[:, at : at + BLOCK] = split(out_t)
        query_grad_t = jnp.zeros((HEAD_DIM, BLOCK), f32)
        for a, b, c in parts:
            grad_probs = dot_nt(vc[a:b, :], grad)
            grad_scores = (probs[c : c + b - a] * (grad_probs - delta)).astype(bf16)
            query_grad_t += dot(kct[:, a:b], grad_scores)
            dk = dot(grad_scores, query) * COARSE_SCALE
            dv = dot(rounded[c : c + b - a], grad)
            if block == 0:
                dkc[a:b, :] = dk
                dvc[a:b, :] = dv
                if a == 0:
                    dkc[b:coarse, :] = jnp.zeros((coarse - b, HEAD_DIM), f32)
                    dvc[b:coarse, :] = jnp.zeros((coarse - b, HEAD_DIM), f32)
            else:
                dkc[a:b, :] += dk
                dvc[a:b, :] += dv
        query_grad = query_grad_t.T * COARSE_SCALE
        query_high[at : at + BLOCK, :], query_low[at : at + BLOCK, :] = split(query_grad)
    query_high[coarse:, :] = jnp.zeros((TAIL, HEAD_DIM), bf16)
    query_low[coarse:, :] = jnp.zeros((TAIL, HEAD_DIM), bf16)
    coarse_ref[:, 0:128] = dkc[0:coarse, :]
    coarse_ref[:, 128:256] = dvc[0:coarse, :]

    first = iota((TAIL, HEAD_DIM), 0) == 0
    for cols, short in ((slice(0, 128), dkc), (slice(128, 256), dvc)):
        high[0:half, cols], low[0:half, cols] = split(short[2 * coarse - half : 2 * coarse, :])
        above = jnp.where(first, short[0:TAIL, :], 0.0)
        high[half:, cols], low[half:, cols] = split(above)
    slot1_ref[:, 0:128] = dkc[coarse : coarse + half + TAIL, :].astype(bf16)
    slot1_ref[:, 128:256] = dvc[coarse : coarse + half + TAIL, :].astype(bf16)
    for slot, ref in ((2, back2_ref), (3, back3_ref)):
        at = slot * coarse
        above = at - coarse
        for cols, short in ((slice(0, 128), dkc), (slice(128, 256), dvc)):
            ref[0:coarse, cols] = short[at : at + coarse, :].astype(bf16)
            row = jnp.where(first, short[above : above + TAIL, :], 0.0)
            ref[coarse : coarse + TAIL, cols] = row.astype(bf16)


def attention_kernel(
    z_ref,
    x_ref,
    near_ref,
    pair_ref,
    slot1_ref,
    high,
    low,
    high_t,
    low_t,
    query_high,
    query_low,
    attn_ref,
    fine_ref,
    back1_ref,
    kx,
    vx,
    kxt,
    vxt,
    dkx,
    dvx,
):
    z = z_ref[0]
    rows = pair_ref.shape[0]
    tokens = rows // PLANE_DEVS
    step = BLOCK // SHORT
    reach = WINDOW // BLOCK
    base = WINDOW + TAIL

    kx[0:WINDOW, :] = near_ref[0:WINDOW, 0:128]
    vx[0:WINDOW, :] = near_ref[0:WINDOW, 128:256]
    for slot in range((rows - WINDOW) // tokens):
        at = WINDOW + slot * tokens
        kx[at : at + tokens, :] = x_ref[slot, 0:tokens, 0:128]
        vx[at : at + tokens, :] = x_ref[slot, 0:tokens, 128:256]

    transposed(kx, kxt, rows // BLOCK)
    transposed(vx, vxt, rows // BLOCK)

    dkx[...] = jnp.zeros_like(dkx)
    dvx[...] = jnp.zeros_like(dvx)

    def window(block, carry):
        at = pl.multiple_of(block * BLOCK, BLOCK)
        here = pl.ds(at, BLOCK)
        biases = [jnp.where((z == 0) & (block + piece < reach), FAR, 0.0) for piece in range(reach + 1)]
        out_t, query_grad = window_block(
            at, pair_ref[here, 0:128], pair_ref[here, 128:256], biases, kx, vx, kxt, vxt, dkx, dvx
        )
        attn_ref[here, 0:128] = (out_t + short_out(block, high_t, low_t)).T.astype(bf16)
        attn_ref[here, 128:256] = (
            query_grad + short_query_grad(block, query_high, query_low)
        ).astype(bf16)
        return carry

    lax.fori_loop(0, reach, window, 0, unroll=4)
    fine_ref[:, 0:128] = dkx[WINDOW:, :] * SCALE
    fine_ref[:, 128:256] = dvx[WINDOW:, :]

    taken = spreading()
    for piece in range(reach):
        at = piece * BLOCK
        below = piece * step
        spread = dot(taken, high[below : below + step + TAIL, :])
        spread += dot(taken, low[below : below + step + TAIL, :])
        spread = spread * (1.0 / SHORT)
        back1_ref[at : at + BLOCK, 0:128] = (
            dkx[at : at + BLOCK, :] * SCALE + spread[:, 0:128]
        ).astype(bf16)
        back1_ref[at : at + BLOCK, 128:256] = (
            dvx[at : at + BLOCK, :] + spread[:, 128:256]
        ).astype(bf16)
    first = iota((TAIL, HEAD_DIM), 0) == 0
    query_row = jnp.where(first, query_high[0:TAIL, :].astype(f32), 0.0).astype(bf16)
    back1_ref[WINDOW:base, 0:128] = query_row
    back1_ref[WINDOW:base, 128:256] = query_row
    back1_ref[base:, :] = slot1_ref[...]


def short_out(block, high_t, low_t):
    step = BLOCK // SHORT
    pair = pl.multiple_of(block // 2 * (2 * step), 2 * step)
    shape = (2 * step, BLOCK)
    spread = ones_where(iota(shape, 0) == block % 2 * step + iota(shape, 1) // SHORT)
    short_t = dot(high_t[:, pl.ds(pair, 2 * step)], spread)
    return short_t + dot(low_t[:, pl.ds(pair, 2 * step)], spread)


def short_query_grad(block, high, low):
    step = BLOCK // SHORT
    below = pl.ds(pl.multiple_of(block * step, step), step + TAIL)
    spread = dot(spreading(), high[below, :]) + dot(spreading(), low[below, :])
    return spread * (1.0 / SHORT)


def late_kernel(early_ref, part_ref, high_t, low_t, high, low, after2_ref, after3_ref, attn_ref):
    del after2_ref, after3_ref
    count = early_ref.shape[0]
    attn_ref[0:count, :] = early_ref[...]
    for block in range(part_ref.shape[0] // BLOCK):
        here = slice(block * BLOCK, (block + 1) * BLOCK)
        late = slice(count + block * BLOCK, count + (block + 1) * BLOCK)
        place = block + count // BLOCK
        attn_ref[late, 0:128] = (part_ref[here, 0:128] + short_out(place, high_t, low_t).T).astype(bf16)
        attn_ref[late, 128:256] = (
            part_ref[here, 128:256] + short_query_grad(place, high, low)
        ).astype(bf16)


def finish_kernel(
    sums_ref, fine_ref, coarse_ref, back1_ref, back2_ref, back3_ref, out_ref, high, low
):
    rows = sums_ref.shape[0]
    tokens = rows // PLANE_DEVS
    coarse = rows // SHORT
    half = coarse - WINDOW // SHORT
    step = BLOCK // SHORT
    base = WINDOW + TAIL
    part = half + TAIL
    ups = (back2_ref, back3_ref)
    total = coarse_ref[...]
    for up in ups:
        total += up[0:coarse, :].astype(f32)
    near = total[0:part, :] + back1_ref[base:, :].astype(f32)
    high[0:part, :], low[0:part, :] = split(near)
    high[part : part + half, :], low[part : part + half, :] = split(total[half:, :])
    extra = functools.reduce(jnp.add, [up[coarse : coarse + TAIL, :].astype(f32) for up in ups])
    high[part + half :, :], low[part + half :, :] = split(extra)
    taken = spreading()
    for block in range(rows // BLOCK):
        at = block * BLOCK
        late = at - (rows - WINDOW)
        below = block * step if late < 0 else part + late // SHORT
        spread = dot(taken, high[below : below + step + TAIL, :])
        spread += dot(taken, low[below : below + step + TAIL, :])
        result = sums_ref[at : at + BLOCK, :] + spread * (1.0 / SHORT)
        if late < 0:
            result = result + fine_ref[at : at + BLOCK, :]
        else:
            result = result + back1_ref[late : late + BLOCK, :].astype(f32)
        out_ref[block, 0:tokens, :] = result.astype(bf16)
        out_ref[block, tokens:, :] = jnp.zeros((TAIL, 256), bf16)
    out_ref[PLANE_DEVS - 1, tokens:, :] = back1_ref[WINDOW:base, :]


def unpack_kernel(pair_ref, x_ref, q_ref, k_ref, v_ref):
    tokens = q_ref.shape[0]
    last = iota((TAIL, HEAD_DIM), 0) > TAIL - SHORT
    for slot in range(q_ref.shape[1] // HEAD_DIM):
        cols = pl.ds(slot * HEAD_DIM, HEAD_DIM)
        k_ref[:, cols] = x_ref[slot, 0:tokens, 0:128]
        v_ref[:, cols] = x_ref[slot, 0:tokens, 128:256]
        q_ref[0 : tokens - TAIL, cols] = pair_ref[slot, 0 : tokens - TAIL, 128:256]
        above = jnp.sum(x_ref[slot, tokens:, 0:128].astype(f32), 0, keepdims=True) * (1.0 / SHORT)
        rest = pair_ref[slot, tokens - TAIL :, 128:256].astype(f32)
        q_ref[tokens - TAIL :, cols] = (rest + jnp.where(last, above, 0.0)).astype(bf16)


def grad_product(halves, a_ref, b_ref, w_ref, total, start):
    at = pl.program_id(0)
    depth = w_ref.shape[1]
    for piece, ref in enumerate((a_ref, b_ref)):
        for half in range(halves):

            @pl.when(at == piece * halves + half)
            def _():
                product = dot_nt(w_ref[...], ref[:, half * depth : (half + 1) * depth])
                if piece + half > 0:
                    total[...] += product
                elif start is None:
                    total[...] = product
                else:
                    total[...] = start[...] + product


def grad_near_kernel(halves, order_ref, a_ref, b_ref, w_ref, total):
    grad_product(halves, a_ref, b_ref, w_ref, total, None)


def grad_far_kernel(halves, order_ref, a_ref, b_ref, w_ref, start, q_ref, out_ref, total):
    grad_product(halves, a_ref, b_ref, w_ref, total, start)

    @pl.when(pl.program_id(0) == pl.num_programs(0) - 1)
    def _():
        last = total.shape[0] // HEAD_DIM - 1
        for slot in range(PLANE_DEVS):
            head = slice(min(slot, last) * HEAD_DIM, (min(slot, last) + 1) * HEAD_DIM)
            out_ref[slot, :, 0:128] = q_ref[:, head]
            out_ref[slot, :, 128:256] = total[head, :].T.astype(bf16)


def grad_part(pieces, order, weight, rest=()):
    rows, width = pieces[0].shape
    depth = weight.shape[0]
    halves = 1
    tile = width // halves

    first = 2 if rest else 0

    def whole(shape):
        return pl.BlockSpec(shape, lambda i, o: (0,) * len(shape))

    packed = (PLANE_DEVS, rows, 2 * HEAD_DIM)
    return pl.pallas_call(
        functools.partial(grad_far_kernel if rest else grad_near_kernel, halves),
        out_shape=jax.ShapeDtypeStruct(packed, bf16) if rest else jax.ShapeDtypeStruct((depth, rows), f32),
        grid_spec=pltpu.PrefetchScalarGridSpec(
            num_scalar_prefetch=1,
            grid=(2 * halves,),
            in_specs=[whole((rows, width))] * 2
            + [pl.BlockSpec((depth, tile), lambda i, o: (0, o[first + i // halves] * halves + i % halves))]
            + [whole(x.shape) for x in rest],
            out_specs=whole(packed if rest else (depth, rows)),
            scratch_shapes=[pltpu.VMEM((depth, rows), f32)] if rest else [],
        ),
        compiler_params=pltpu.CompilerParams(vmem_limit_bytes=62 * 1024 * 1024),
    )(order, *pieces, weight, *rest)


def project_kernel(halves, order_ref, attn_ref, w_ref, *refs):
    send_ref, keep_ref, rows_ref = refs[-3:]
    at = pl.program_id(0)
    heads = w_ref.shape[0] // HEAD_DIM
    tile = w_ref.shape[1]

    @pl.when(at == 0)
    def _():
        for slot in range(heads):
            rows_ref[:, slot * HEAD_DIM : (slot + 1) * HEAD_DIM] = attn_ref[slot, :, 0:128]

    product = dot(rows_ref[...], w_ref[...]).astype(bf16)
    for half in range(halves):

        @pl.when(at == half)
        def _():
            send_ref[:, half * tile : (half + 1) * tile] = product

        @pl.when(at == halves + half)
        def _():
            keep_ref[:, half * tile : (half + 1) * tile] = product


def project(attn, order, last, weight, width, after):
    rows = attn.shape[1]
    depth = weight.shape[0]
    halves = 1
    tile = width // halves
    out = jax.ShapeDtypeStruct((rows, width), bf16)
    return pl.pallas_call(
        functools.partial(project_kernel, halves),
        out_shape=(out, out),
        grid_spec=pltpu.PrefetchScalarGridSpec(
            num_scalar_prefetch=1,
            grid=(2 * halves,),
            in_specs=[
                pl.BlockSpec(attn.shape, lambda i, o: (0, 0, 0)),
                pl.BlockSpec((depth, tile), lambda i, o: (0, o[last - i // halves] * halves + i % halves)),
            ]
            + [pl.BlockSpec(memory_space=pltpu.HBM)] * len(after),
            out_specs=[pl.BlockSpec((rows, width), lambda i, o: (0, 0))] * 2,
            scratch_shapes=[pltpu.VMEM((rows, depth), bf16)],
        ),
        compiler_params=pltpu.CompilerParams(vmem_limit_bytes=62 * 1024 * 1024),
    )(order, attn, weight, *after)


def swap(x, axis):
    return lax.ppermute(x, axis, [(0, 1), (1, 0)])


def planes_up(x, by):
    return lax.ppermute(x, "z", [(i, i + by) for i in range(PLANES) if 0 <= i + by < PLANES])


def in_plane(x):
    return lax.all_to_all(x, PLANE, 0, 0, tiled=True)


def column_blocks():
    xl, core = lax.axis_index("xl"), lax.axis_index("c")
    own, other = 2 * xl, 2 * (1 - xl)
    return jnp.stack([own + core, own + 1 - core, other + core, other + 1 - core]).astype(jnp.int32)


def gathered_grad(out_grad, out_weight, q_proj, blocks):
    far = swap(out_grad, "xl")
    near = swap(out_grad, "c")
    start = grad_part((out_grad, near), blocks, out_weight)
    far, start = lax.optimization_barrier((far, start))
    both = swap(far, "c")
    return start, grad_part((far, both), blocks, out_weight, (start, q_proj))


def projected(attn, out_weight, width, blocks, after):
    def share(last, attn):
        send, keep = project(attn, blocks, last, out_weight, width, after)
        return keep.astype(f32) + swap(send, "c").astype(f32)

    part = share(3, attn).astype(bf16)
    part, attn = lax.optimization_barrier((part, attn))
    far = swap(part, "xl")
    return (share(1, attn) + far.astype(f32)).astype(bf16)


def shards(q_proj, k_proj, v_proj, out_weight, out_grad):
    tokens, cols = q_proj.shape
    rows = tokens * PLANE_DEVS
    coarse = rows // SHORT
    total = PLANES * coarse
    z = lax.axis_index("z").astype(jnp.int32).reshape(1)

    def array(*shape, dtype=bf16):
        return jax.ShapeDtypeStruct(shape, dtype)

    in_place = pl.BlockSpec(memory_space=pltpu.HBM)
    whole = pl.BlockSpec(memory_space=pltpu.VMEM)
    packed = call(
        pack_kernel,
        array(PLANE_DEVS, tokens + TAIL, 2 * HEAD_DIM),
        62,
        in_specs=[in_place] * 3,
        out_specs=whole,
        scratch_shapes=[pltpu.SemaphoreType.DMA((PLANE_DEVS, 4))],
    )(q_proj, k_proj, v_proj)
    own = in_plane(packed)
    blocks = column_blocks()
    early, pair_packed = gathered_grad(out_grad, out_weight, q_proj, blocks)
    near_rows = WINDOW + 2 * TAIL + WINDOW // SHORT
    near, far = call(
        pool_kernel,
        (array(near_rows, 256), array(coarse + TAIL, 256)),
        16,
        in_specs=[whole, in_place],
    )(own, early)
    near_in = planes_up(near, 1)
    far2_in = planes_up(far, 2)
    far3_in = planes_up(far, 3)
    pair = in_plane(pair_packed).reshape(rows, 2 * HEAD_DIM)

    part, sums = call(
        own_kernel,
        (array(rows - WINDOW, 256, dtype=f32), array(rows, 256, dtype=f32)),
        56,
        in_specs=[whole] * 2,
        out_specs=[whole] * 2,
        scratch_shapes=[pltpu.VMEM((rows, HEAD_DIM), bf16)] * 2
        + [pltpu.VMEM((HEAD_DIM, rows), bf16)] * 2
        + [pltpu.VMEM((rows, HEAD_DIM), f32)] * 2,
    )(own, pair)
    scalar = pl.BlockSpec(memory_space=pltpu.SMEM)
    half = WINDOW // SHORT + TAIL
    short, back2, back3, *tables = call(
        short_kernel,
        (
            array(coarse, 256, dtype=f32),
            array(coarse + TAIL, 256),
            array(coarse + TAIL, 256),
            array(half, 256),
            array(half, 256),
            array(half, 256),
            array(HEAD_DIM, coarse),
            array(HEAD_DIM, coarse),
            array(coarse + TAIL, HEAD_DIM),
            array(coarse + TAIL, HEAD_DIM),
        ),
        56,
        in_specs=[scalar] + [whole] * 5 + [in_place],
        out_specs=[whole] * 10,
        scratch_shapes=[pltpu.VMEM((total, HEAD_DIM), bf16)] * 2
        + [pltpu.VMEM((HEAD_DIM, total), bf16)] * 2
        + [pltpu.VMEM((coarse, HEAD_DIM), bf16)] * 2
        + [pltpu.VMEM((total, HEAD_DIM), f32)] * 2,
    )(z, far, near_in, far2_in, far3_in, pair, part)
    back2_in = planes_up(back2, -2)
    back3_in = planes_up(back3, -3)
    early, fine, back1 = call(
        attention_kernel,
        (array(rows - WINDOW, 256), array(rows - WINDOW, 256, dtype=f32), array(near_rows, 256)),
        56,
        in_specs=[scalar] + [whole] * 10,
        out_specs=[whole] * 3,
        scratch_shapes=[pltpu.VMEM((rows, HEAD_DIM), bf16)] * 2
        + [pltpu.VMEM((HEAD_DIM, rows), bf16)] * 2
        + [pltpu.VMEM((rows, HEAD_DIM), f32)] * 2,
    )(z, own, near_in, pair, *tables)
    back1_in = planes_up(back1, -1)
    attn = call(
        late_kernel,
        array(rows, 256),
        56,
        in_specs=[whole] * 6 + [in_place] * 2,
    )(early, part, *tables[3:], back2_in, back3_in)
    attn_in = in_plane(attn.reshape(PLANE_DEVS, tokens, 256))
    finished = call(
        finish_kernel,
        array(PLANE_DEVS, tokens + TAIL, 256),
        32,
        scratch_shapes=[
            pltpu.VMEM((coarse + 2 * TAIL, 256), bf16),
            pltpu.VMEM((coarse + 2 * TAIL, 256), bf16),
        ],
    )(sums, fine, short, back1_in, back2_in, back3_in)
    mixed_out = projected(
        attn_in, out_weight, out_grad.shape[1], blocks, (finished,)
    )
    returned = in_plane(finished)
    grads = call(unpack_kernel, (array(tokens, cols),) * 3, 16)(attn_in, returned)
    return (mixed_out, *grads)


def solution(mesh):
    fine_mesh = Mesh(np.asarray(mesh.devices).reshape(4, 4, 2, 2, 2), ("z", "y", "xh", "xl", "c"))
    both = P(("z", "y", "xh"), ("xl", "c"))
    in_specs = (both, both, both, P(("xl", "c"), None), both)
    return jax.shard_map(
        shards, mesh=fine_mesh, in_specs=in_specs, out_specs=(both,) * 4, check_vma=False
    )
```

```python
import functools
import math

import jax
import jax.numpy as jnp
import numpy as np
from jax import lax
from jax.experimental import pallas as pl
from jax.experimental.pallas import tpu as pltpu
from jax.sharding import Mesh, PartitionSpec as P

HEAD_DIM = 128
SHORT = 4
WINDOW = 1024
PLANES = 4
PLANE_DEVS = 8
BLOCK = 256
TAIL = 16
LOG2E = math.log2(math.e)
SCALE = 1.0 / math.sqrt(HEAD_DIM)
COARSE_SCALE = 2.0 * SCALE
FAR = -1e30
PLANE = ("y", "xh")
bf16 = jnp.bfloat16
f32 = jnp.float32


def call(kernel, out_shape, vmem_mib, **rest):
    return pl.pallas_call(
        kernel,
        out_shape=out_shape,
        compiler_params=pltpu.CompilerParams(vmem_limit_bytes=vmem_mib * 1024 * 1024),
        **rest,
    )


def dot(a, b):
    return jnp.dot(a, b, preferred_element_type=f32)


def dot_nt(a, b):
    return lax.dot_general(a, b, (((1,), (1,)), ((), ())), preferred_element_type=f32)


def iota(shape, dim):
    return lax.broadcasted_iota(jnp.int32, shape, dim)


def split(x):
    high = x.astype(bf16)
    return high, (x - high.astype(f32)).astype(bf16)


def ones_where(mask):
    return jnp.where(mask, 1.0, 0.0).astype(bf16)


def pack_kernel(q_ref, k_ref, v_ref, out_ref, sems):
    tokens = q_ref.shape[0]
    last = q_ref.shape[1] // HEAD_DIM - 1
    copies = []
    for slot in range(PLANE_DEVS):
        cols = pl.ds(min(slot, last) * HEAD_DIM, HEAD_DIM)
        tail = q_ref.at[tokens - TAIL :, cols]
        pieces = (
            (k_ref.at[:, cols], out_ref.at[slot, 0:tokens, 0:128]),
            (v_ref.at[:, cols], out_ref.at[slot, 0:tokens, 128:256]),
            (tail, out_ref.at[slot, tokens:, 0:128]),
            (tail, out_ref.at[slot, tokens:, 128:256]),
        )
        for at, (source, target) in enumerate(pieces):
            copies.append(pltpu.make_async_copy(source, target, sems.at[slot, at]))
    for copy in copies:
        copy.start()
    for copy in copies:
        copy.wait()


def pooling(lead):
    shape = (BLOCK // SHORT, BLOCK + lead)
    back = iota(shape, 1) - lead - SHORT * iota(shape, 0)
    return ones_where((back <= 0) & (back > -SHORT))


def spreading():
    shape = (BLOCK, BLOCK // SHORT + TAIL)
    return ones_where((iota(shape, 0) + (SHORT - 1)) // SHORT == iota(shape, 1))


def pooled_rows(block, lead=None):
    rows = block if lead is None else jnp.concatenate([lead, block], 0)
    taken = pooling(0 if lead is None else TAIL)
    return (dot(taken, rows) * (1.0 / SHORT)).astype(bf16)


def pool_kernel(x_ref, after_ref, near_ref, far_ref):
    del after_ref
    devs, tokens = x_ref.shape[0], x_ref.shape[1] - TAIL
    step = tokens // SHORT
    half = WINDOW // SHORT
    coarse = devs * step
    for slot in range(devs):
        block = x_ref[slot, 0:tokens, :]
        lead = x_ref[slot - 1, tokens - TAIL : tokens, :] if slot else None
        far_ref[slot * step : (slot + 1) * step, :] = pooled_rows(block, lead)
        late = slot * tokens - (devs * tokens - WINDOW)
        if late >= 0:
            near_ref[late : late + tokens, :] = block
    far_ref[coarse : coarse + TAIL, :] = x_ref[devs - 1, tokens - TAIL : tokens, :]
    near_ref[WINDOW : WINDOW + TAIL, :] = x_ref[devs - 1, tokens:, :]
    near_ref[WINDOW + TAIL :, :] = far_ref[0 : half + TAIL, :]


def first_row_fixed(pooled, tail):
    kept = jnp.where(iota(tail.shape, 0) > TAIL - SHORT, tail.astype(f32), 0.0)
    lacking = jnp.sum(kept, 0, keepdims=True) * (1.0 / SHORT)
    head = pooled[0:TAIL, :].astype(f32)
    return jnp.where(iota(head.shape, 0) == 0, head + lacking, head).astype(bf16)


def transposed(ref, out, count):
    def body(i, carry):
        at = pl.multiple_of(i * BLOCK, BLOCK)
        out[:, pl.ds(at, BLOCK)] = ref[pl.ds(at, BLOCK), :].T
        return carry

    lax.fori_loop(0, count, body, 0)


def weights(scores, biases, factor):
    tops = [jnp.max(s, 0, keepdims=True) + b for s, b in zip(scores, biases)]
    top = functools.reduce(jnp.maximum, tops)
    exps = [jnp.exp2((s - (top - b)) * factor) for s, b in zip(scores, biases)]
    total = functools.reduce(jnp.add, [jnp.sum(e, 0, keepdims=True) for e in exps])
    inverse = 1.0 / total
    return jnp.concatenate([e * inverse for e in exps], 0)


def window_block(at, query, grad, biases, kx, vx, kxt, vxt, dk, dv):
    span = WINDOW + BLOCK
    reach = WINDOW // BLOCK
    row_at, col_at = iota((BLOCK, BLOCK), 0), iota((BLOCK, BLOCK), 1)
    scores = []
    for piece in range(reach + 1):
        s = dot_nt(kx[pl.ds(pl.multiple_of(at + piece * BLOCK, BLOCK), BLOCK), :], query)
        if piece == 0:
            s = jnp.where(row_at > col_at, s, FAR)
        if piece == reach:
            s = jnp.where(row_at <= col_at, s, FAR)
        scores.append(s)
    probs = weights(scores, biases, SCALE * LOG2E)
    rounded = probs.astype(bf16)
    out_t = dot(vxt[:, pl.ds(at, span)], rounded)
    delta = jnp.sum(grad.astype(f32).T * out_t, 0, keepdims=True)
    grad_probs = dot_nt(vx[pl.ds(at, span), :], grad)
    grad_scores = (probs * (grad_probs - delta)).astype(bf16)
    dk[pl.ds(at, span), :] += dot(grad_scores, query)
    dv[pl.ds(at, span), :] += dot(rounded, grad)
    return out_t, dot(kxt[:, pl.ds(at, span)], grad_scores).T * SCALE


def own_kernel(x_ref, pair_ref, part_ref, sums_ref, kx, vx, kxt, vxt, dk, dv):
    rows = pair_ref.shape[0]
    tokens = rows // PLANE_DEVS
    for slot in range(PLANE_DEVS):
        at = slot * tokens
        kx[at : at + tokens, :] = x_ref[slot, 0:tokens, 0:128]
        vx[at : at + tokens, :] = x_ref[slot, 0:tokens, 128:256]
    transposed(kx, kxt, rows // BLOCK)
    transposed(vx, vxt, rows // BLOCK)
    dk[...] = jnp.zeros_like(dk)
    dv[...] = jnp.zeros_like(dv)

    def body(block, carry):
        at = pl.multiple_of(block * BLOCK, BLOCK)
        own = pl.ds(pl.multiple_of(WINDOW + at, BLOCK), BLOCK)
        biases = [0.0] * (WINDOW // BLOCK + 1)
        out_t, query_grad = window_block(
            at, pair_ref[own, 0:128], pair_ref[own, 128:256], biases, kx, vx, kxt, vxt, dk, dv
        )
        part_ref[pl.ds(at, BLOCK), 0:128] = out_t.T
        part_ref[pl.ds(at, BLOCK), 128:256] = query_grad
        return carry

    lax.fori_loop(0, (rows - WINDOW) // BLOCK, body, 0, unroll=4)
    sums_ref[:, 0:128] = dk[...] * SCALE
    sums_ref[:, 128:256] = dv[...]


def attention_kernel(
    z_ref,
    x_ref,
    own_ref,
    near_ref,
    far2_ref,
    far3_ref,
    pair_ref,
    part_ref,
    attn_ref,
    fine_ref,
    coarse_ref,
    back1_ref,
    back2_ref,
    back3_ref,
    kx,
    vx,
    kxt,
    vxt,
    kc,
    vc,
    kct,
    vct,
    pq,
    gp,
    dkx,
    dvx,
    dkc,
    dvc,
    high_t,
    low_t,
    high,
    low,
    query_high,
    query_low,
):
    z = z_ref[0]
    rows = pair_ref.shape[0]
    tokens = rows // PLANE_DEVS
    coarse = rows // SHORT
    half = WINDOW // SHORT
    step = BLOCK // SHORT
    reach = WINDOW // BLOCK

    kx[0:WINDOW, :] = near_ref[0:WINDOW, 0:128]
    vx[0:WINDOW, :] = near_ref[0:WINDOW, 128:256]
    for slot in range((rows - WINDOW) // tokens):
        at = WINDOW + slot * tokens
        kx[at : at + tokens, :] = x_ref[slot, 0:tokens, 0:128]
        vx[at : at + tokens, :] = x_ref[slot, 0:tokens, 128:256]

    transposed(kx, kxt, rows // BLOCK)
    transposed(vx, vxt, rows // BLOCK)

    tails = [
        near_ref[WINDOW - TAIL : WINDOW, :],
        far2_ref[coarse : coarse + TAIL, :],
        far3_ref[coarse : coarse + TAIL, :],
    ]
    base = WINDOW + TAIL
    for piece in range(reach):
        at = coarse + half + piece * step
        block = near_ref[piece * BLOCK : (piece + 1) * BLOCK, :]
        lead = near_ref[piece * BLOCK - TAIL : piece * BLOCK, :] if piece else None
        rest = pooled_rows(block, lead)
        kc[at : at + step, :] = rest[:, 0:128]
        vc[at : at + step, :] = rest[:, 128:256]
    sources = ((own_ref, coarse), (near_ref.at[base:], half + TAIL), (far2_ref, coarse), (far3_ref, coarse))
    for slot, (source, count) in enumerate(sources):
        at = slot * coarse
        kc[at : at + count, :] = source[0:count, 0:128]
        vc[at : at + count, :] = source[0:count, 128:256]
        if slot + 1 < PLANES:
            fixed = first_row_fixed(source[0:TAIL, :], tails[slot])
            kc[at : at + TAIL, :] = fixed[:, 0:128]
            vc[at : at + TAIL, :] = fixed[:, 128:256]
    transposed(kc, kct, PLANES * coarse // BLOCK)
    transposed(vc, vct, PLANES * coarse // BLOCK)

    shape = (step, BLOCK)
    offset = iota(shape, 1) - SHORT * iota(shape, 0)
    taken = ones_where((offset >= 0) & (offset < SHORT))
    for block in range(rows // BLOCK):
        at = block * BLOCK
        lead = pair_ref[at - TAIL : at, 0:128] if block else near_ref[WINDOW : WINDOW + TAIL, 0:128]
        pq[block * step : (block + 1) * step, :] = pooled_rows(pair_ref[at : at + BLOCK, 0:128], lead)
        gp[block * step : (block + 1) * step, :] = dot(
            taken, pair_ref[at : at + BLOCK, 128:256]
        ).astype(bf16)

    row_at, col_at = iota((BLOCK, BLOCK), 0), iota((BLOCK, BLOCK), 1)
    diagonal = row_at <= col_at
    for block in range(coarse // BLOCK):
        at = block * BLOCK
        query = pq[at : at + BLOCK, :]
        grad = gp[at : at + BLOCK, :]
        scores, biases, keys, values = [], [], [], []
        for piece in range(block + 1):
            s = dot_nt(kc[piece * BLOCK : (piece + 1) * BLOCK, :], query)
            scores.append(jnp.where(diagonal, s, FAR) if piece == block else s)
            biases.append(0.0)
        for slot in range(1, PLANES):
            s = dot_nt(kc[slot * coarse : (slot + 1) * coarse, :], query)
            scores.append(s)
            biases.append(jnp.where(z >= slot, 0.0, FAR))
        probs = weights(scores, biases, COARSE_SCALE * LOG2E)
        rounded = probs.astype(bf16)
        own = at + BLOCK
        parts = ((0, own, 0), (coarse, PLANES * coarse, own))
        out_t = functools.reduce(
            jnp.add, [dot(vct[:, a:b], rounded[c : c + b - a]) for a, b, c in parts]
        )
        grad_t = grad.astype(f32).T
        delta = jnp.sum(grad_t * out_t, 0, keepdims=True)
        high_t[:, at : at + BLOCK], low_t[:, at : at + BLOCK] = split(out_t)
        query_grad_t = jnp.zeros((HEAD_DIM, BLOCK), f32)
        for a, b, c in parts:
            grad_probs = dot_nt(vc[a:b, :], grad)
            grad_scores = (probs[c : c + b - a] * (grad_probs - delta)).astype(bf16)
            query_grad_t += dot(kct[:, a:b], grad_scores)
            dk = dot(grad_scores, query) * COARSE_SCALE
            dv = dot(rounded[c : c + b - a], grad)
            if block == 0:
                dkc[a:b, :] = dk
                dvc[a:b, :] = dv
                if a == 0:
                    dkc[b:coarse, :] = jnp.zeros((coarse - b, HEAD_DIM), f32)
                    dvc[b:coarse, :] = jnp.zeros((coarse - b, HEAD_DIM), f32)
            else:
                dkc[a:b, :] += dk
                dvc[a:b, :] += dv
        query_grad = query_grad_t.T * COARSE_SCALE
        query_high[at : at + BLOCK, :], query_low[at : at + BLOCK, :] = split(query_grad)
    query_high[coarse:, :] = jnp.zeros((TAIL, HEAD_DIM), bf16)
    query_low[coarse:, :] = jnp.zeros((TAIL, HEAD_DIM), bf16)
    coarse_ref[:, 0:128] = dkc[0:coarse, :]
    coarse_ref[:, 128:256] = dvc[0:coarse, :]

    dkx[...] = jnp.zeros_like(dkx)
    dvx[...] = jnp.zeros_like(dvx)

    def short_out(block):
        pair = pl.multiple_of(block // 2 * (2 * step), 2 * step)
        shape = (2 * step, BLOCK)
        spread = ones_where(iota(shape, 0) == block % 2 * step + iota(shape, 1) // SHORT)
        short_t = dot(high_t[:, pl.ds(pair, 2 * step)], spread)
        return short_t + dot(low_t[:, pl.ds(pair, 2 * step)], spread)

    def short_query_grad(block):
        below = pl.ds(pl.multiple_of(block * step, step), step + TAIL)
        spread = dot(spreading(), query_high[below, :]) + dot(spreading(), query_low[below, :])
        return spread * (1.0 / SHORT)

    def window(block, carry):
        at = pl.multiple_of(block * BLOCK, BLOCK)
        here = pl.ds(at, BLOCK)
        biases = [jnp.where((z == 0) & (block + piece < reach), FAR, 0.0) for piece in range(reach + 1)]
        out_t, query_grad = window_block(
            at, pair_ref[here, 0:128], pair_ref[here, 128:256], biases, kx, vx, kxt, vxt, dkx, dvx
        )
        attn_ref[here, 0:128] = (out_t + short_out(block)).T.astype(bf16)
        attn_ref[here, 128:256] = (query_grad + short_query_grad(block)).astype(bf16)
        late = pl.ds(pl.multiple_of(WINDOW + at, BLOCK), BLOCK)
        attn_ref[late, 0:128] = (part_ref[here, 0:128] + short_out(block + reach).T).astype(bf16)
        attn_ref[late, 128:256] = (part_ref[here, 128:256] + short_query_grad(block + reach)).astype(bf16)
        return carry

    lax.fori_loop(0, reach, window, 0, unroll=4)
    fine_ref[:, 0:128] = dkx[WINDOW:, :] * SCALE
    fine_ref[:, 128:256] = dvx[WINDOW:, :]

    first = iota((TAIL, HEAD_DIM), 0) == 0
    for cols, short in ((slice(0, 128), dkc), (slice(128, 256), dvc)):
        high[0:half, cols], low[0:half, cols] = split(short[2 * coarse - half : 2 * coarse, :])
        above = jnp.where(first, short[0:TAIL, :], 0.0)
        high[half:, cols], low[half:, cols] = split(above)
    taken = spreading()
    for piece in range(reach):
        at = piece * BLOCK
        below = piece * step
        spread = dot(taken, high[below : below + step + TAIL, :])
        spread += dot(taken, low[below : below + step + TAIL, :])
        spread = spread * (1.0 / SHORT)
        back1_ref[at : at + BLOCK, 0:128] = (
            dkx[at : at + BLOCK, :] * SCALE + spread[:, 0:128]
        ).astype(bf16)
        back1_ref[at : at + BLOCK, 128:256] = (
            dvx[at : at + BLOCK, :] + spread[:, 128:256]
        ).astype(bf16)
    query_row = jnp.where(first, query_high[0:TAIL, :].astype(f32), 0.0).astype(bf16)
    back1_ref[WINDOW:base, 0:128] = query_row
    back1_ref[WINDOW:base, 128:256] = query_row
    back1_ref[base:, 0:128] = dkc[coarse : coarse + half + TAIL, :].astype(bf16)
    back1_ref[base:, 128:256] = dvc[coarse : coarse + half + TAIL, :].astype(bf16)
    for slot, ref in ((2, back2_ref), (3, back3_ref)):
        at = slot * coarse
        above = at - coarse
        for cols, short in ((slice(0, 128), dkc), (slice(128, 256), dvc)):
            ref[0:coarse, cols] = short[at : at + coarse, :].astype(bf16)
            row = jnp.where(first, short[above : above + TAIL, :], 0.0)
            ref[coarse : coarse + TAIL, cols] = row.astype(bf16)


def finish_kernel(
    sums_ref, fine_ref, coarse_ref, back1_ref, back2_ref, back3_ref, after_ref, out_ref, high, low
):
    del after_ref
    rows = sums_ref.shape[0]
    tokens = rows // PLANE_DEVS
    coarse = rows // SHORT
    half = coarse - WINDOW // SHORT
    step = BLOCK // SHORT
    base = WINDOW + TAIL
    part = half + TAIL
    ups = (back2_ref, back3_ref)
    total = coarse_ref[...]
    for up in ups:
        total += up[0:coarse, :].astype(f32)
    near = total[0:part, :] + back1_ref[base:, :].astype(f32)
    high[0:part, :], low[0:part, :] = split(near)
    high[part : part + half, :], low[part : part + half, :] = split(total[half:, :])
    extra = functools.reduce(jnp.add, [up[coarse : coarse + TAIL, :].astype(f32) for up in ups])
    high[part + half :, :], low[part + half :, :] = split(extra)
    taken = spreading()
    for block in range(rows // BLOCK):
        at = block * BLOCK
        late = at - (rows - WINDOW)
        below = block * step if late < 0 else part + late // SHORT
        spread = dot(taken, high[below : below + step + TAIL, :])
        spread += dot(taken, low[below : below + step + TAIL, :])
        result = sums_ref[at : at + BLOCK, :] + spread * (1.0 / SHORT)
        if late < 0:
            result = result + fine_ref[at : at + BLOCK, :]
        else:
            result = result + back1_ref[late : late + BLOCK, :].astype(f32)
        out_ref[block, 0:tokens, :] = result.astype(bf16)
        out_ref[block, tokens:, :] = jnp.zeros((TAIL, 256), bf16)
    out_ref[PLANE_DEVS - 1, tokens:, :] = back1_ref[WINDOW:base, :]


def unpack_kernel(pair_ref, x_ref, q_ref, k_ref, v_ref):
    tokens = q_ref.shape[0]
    last = iota((TAIL, HEAD_DIM), 0) > TAIL - SHORT
    for slot in range(q_ref.shape[1] // HEAD_DIM):
        cols = pl.ds(slot * HEAD_DIM, HEAD_DIM)
        k_ref[:, cols] = x_ref[slot, 0:tokens, 0:128]
        v_ref[:, cols] = x_ref[slot, 0:tokens, 128:256]
        q_ref[0 : tokens - TAIL, cols] = pair_ref[slot, 0 : tokens - TAIL, 128:256]
        above = jnp.sum(x_ref[slot, tokens:, 0:128].astype(f32), 0, keepdims=True) * (1.0 / SHORT)
        rest = pair_ref[slot, tokens - TAIL :, 128:256].astype(f32)
        q_ref[tokens - TAIL :, cols] = (rest + jnp.where(last, above, 0.0)).astype(bf16)


def grad_product(halves, a_ref, b_ref, w_ref, total, start):
    at = pl.program_id(0)
    depth = w_ref.shape[1]
    for piece, ref in enumerate((a_ref, b_ref)):
        for half in range(halves):

            @pl.when(at == piece * halves + half)
            def _():
                product = dot_nt(w_ref[...], ref[:, half * depth : (half + 1) * depth])
                if piece + half > 0:
                    total[...] += product
                elif start is None:
                    total[...] = product
                else:
                    total[...] = start[...] + product


def grad_near_kernel(halves, order_ref, a_ref, b_ref, w_ref, total):
    grad_product(halves, a_ref, b_ref, w_ref, total, None)


def grad_far_kernel(halves, order_ref, a_ref, b_ref, w_ref, start, q_ref, out_ref, total):
    grad_product(halves, a_ref, b_ref, w_ref, total, start)

    @pl.when(pl.program_id(0) == pl.num_programs(0) - 1)
    def _():
        last = total.shape[0] // HEAD_DIM - 1
        for slot in range(PLANE_DEVS):
            head = slice(min(slot, last) * HEAD_DIM, (min(slot, last) + 1) * HEAD_DIM)
            out_ref[slot, :, 0:128] = q_ref[:, head]
            out_ref[slot, :, 128:256] = total[head, :].T.astype(bf16)


def grad_part(pieces, order, weight, rest=()):
    rows, width = pieces[0].shape
    depth = weight.shape[0]
    halves = 1
    tile = width // halves

    first = 2 if rest else 0

    def whole(shape):
        return pl.BlockSpec(shape, lambda i, o: (0,) * len(shape))

    packed = (PLANE_DEVS, rows, 2 * HEAD_DIM)
    return pl.pallas_call(
        functools.partial(grad_far_kernel if rest else grad_near_kernel, halves),
        out_shape=jax.ShapeDtypeStruct(packed, bf16) if rest else jax.ShapeDtypeStruct((depth, rows), f32),
        grid_spec=pltpu.PrefetchScalarGridSpec(
            num_scalar_prefetch=1,
            grid=(2 * halves,),
            in_specs=[whole((rows, width))] * 2
            + [pl.BlockSpec((depth, tile), lambda i, o: (0, o[first + i // halves] * halves + i % halves))]
            + [whole(x.shape) for x in rest],
            out_specs=whole(packed if rest else (depth, rows)),
            scratch_shapes=[pltpu.VMEM((depth, rows), f32)] if rest else [],
        ),
        compiler_params=pltpu.CompilerParams(vmem_limit_bytes=62 * 1024 * 1024),
    )(order, *pieces, weight, *rest)


def project_kernel(halves, order_ref, attn_ref, w_ref, *refs):
    send_ref, keep_ref, rows_ref = refs[-3:]
    at = pl.program_id(0)
    heads = w_ref.shape[0] // HEAD_DIM
    tile = w_ref.shape[1]

    @pl.when(at == 0)
    def _():
        for slot in range(heads):
            rows_ref[:, slot * HEAD_DIM : (slot + 1) * HEAD_DIM] = attn_ref[slot, :, 0:128]

    product = dot(rows_ref[...], w_ref[...]).astype(bf16)
    for half in range(halves):

        @pl.when(at == half)
        def _():
            send_ref[:, half * tile : (half + 1) * tile] = product

        @pl.when(at == halves + half)
        def _():
            keep_ref[:, half * tile : (half + 1) * tile] = product


def project(attn, order, last, weight, width, after):
    rows = attn.shape[1]
    depth = weight.shape[0]
    halves = 1
    tile = width // halves
    out = jax.ShapeDtypeStruct((rows, width), bf16)
    return pl.pallas_call(
        functools.partial(project_kernel, halves),
        out_shape=(out, out),
        grid_spec=pltpu.PrefetchScalarGridSpec(
            num_scalar_prefetch=1,
            grid=(2 * halves,),
            in_specs=[
                pl.BlockSpec(attn.shape, lambda i, o: (0, 0, 0)),
                pl.BlockSpec((depth, tile), lambda i, o: (0, o[last - i // halves] * halves + i % halves)),
            ]
            + [pl.BlockSpec(memory_space=pltpu.HBM)] * len(after),
            out_specs=[pl.BlockSpec((rows, width), lambda i, o: (0, 0))] * 2,
            scratch_shapes=[pltpu.VMEM((rows, depth), bf16)],
        ),
        compiler_params=pltpu.CompilerParams(vmem_limit_bytes=62 * 1024 * 1024),
    )(order, attn, weight, *after)


def swap(x, axis):
    return lax.ppermute(x, axis, [(0, 1), (1, 0)])


def planes_up(x, by):
    return lax.ppermute(x, "z", [(i, i + by) for i in range(PLANES) if 0 <= i + by < PLANES])


def in_plane(x):
    return lax.all_to_all(x, PLANE, 0, 0, tiled=True)


def column_blocks():
    xl, core = lax.axis_index("xl"), lax.axis_index("c")
    own, other = 2 * xl, 2 * (1 - xl)
    return jnp.stack([own + core, own + 1 - core, other + core, other + 1 - core]).astype(jnp.int32)


def gathered_grad(out_grad, out_weight, q_proj, blocks):
    far = swap(out_grad, "xl")
    near = swap(out_grad, "c")
    start = grad_part((out_grad, near), blocks, out_weight)
    far, start = lax.optimization_barrier((far, start))
    both = swap(far, "c")
    return start, grad_part((far, both), blocks, out_weight, (start, q_proj))


def projected(attn, out_weight, width, blocks, last, after):
    send, keep = project(attn, blocks, last, out_weight, width, after)
    return keep.astype(f32) + swap(send, "c").astype(f32), keep


def shards(q_proj, k_proj, v_proj, out_weight, out_grad):
    tokens, cols = q_proj.shape
    rows = tokens * PLANE_DEVS
    coarse = rows // SHORT
    total = PLANES * coarse
    z = lax.axis_index("z").astype(jnp.int32).reshape(1)

    def array(*shape, dtype=bf16):
        return jax.ShapeDtypeStruct(shape, dtype)

    in_place = pl.BlockSpec(memory_space=pltpu.HBM)
    whole = pl.BlockSpec(memory_space=pltpu.VMEM)
    packed = call(
        pack_kernel,
        array(PLANE_DEVS, tokens + TAIL, 2 * HEAD_DIM),
        62,
        in_specs=[in_place] * 3,
        out_specs=whole,
        scratch_shapes=[pltpu.SemaphoreType.DMA((PLANE_DEVS, 4))],
    )(q_proj, k_proj, v_proj)
    own = in_plane(packed)
    blocks = column_blocks()
    early, pair_packed = gathered_grad(out_grad, out_weight, q_proj, blocks)
    near_rows = WINDOW + 2 * TAIL + WINDOW // SHORT
    near, far = call(
        pool_kernel,
        (array(near_rows, 256), array(coarse + TAIL, 256)),
        16,
        in_specs=[whole, in_place],
    )(own, early)
    near_in = planes_up(near, 1)
    far2_in = planes_up(far, 2)
    far3_in = planes_up(far, 3)
    pair = in_plane(pair_packed).reshape(rows, 2 * HEAD_DIM)

    part, sums = call(
        own_kernel,
        (array(rows - WINDOW, 256, dtype=f32), array(rows, 256, dtype=f32)),
        56,
        in_specs=[whole] * 2,
        out_specs=[whole] * 2,
        scratch_shapes=[pltpu.VMEM((rows, HEAD_DIM), bf16)] * 2
        + [pltpu.VMEM((HEAD_DIM, rows), bf16)] * 2
        + [pltpu.VMEM((rows, HEAD_DIM), f32)] * 2,
    )(own, pair)
    attn, fine, short, back1, back2, back3 = call(
        attention_kernel,
        (
            array(rows, 256),
            array(rows - WINDOW, 256, dtype=f32),
            array(coarse, 256, dtype=f32),
            array(near_rows, 256),
            array(coarse + TAIL, 256),
            array(coarse + TAIL, 256),
        ),
        62,
        in_specs=[pl.BlockSpec(memory_space=pltpu.SMEM)] + [whole] * 7,
        out_specs=[whole] * 6,
        scratch_shapes=[
            pltpu.VMEM((rows, HEAD_DIM), bf16),
            pltpu.VMEM((rows, HEAD_DIM), bf16),
            pltpu.VMEM((HEAD_DIM, rows), bf16),
            pltpu.VMEM((HEAD_DIM, rows), bf16),
            pltpu.VMEM((total, HEAD_DIM), bf16),
            pltpu.VMEM((total, HEAD_DIM), bf16),
            pltpu.VMEM((HEAD_DIM, total), bf16),
            pltpu.VMEM((HEAD_DIM, total), bf16),
            pltpu.VMEM((coarse, HEAD_DIM), bf16),
            pltpu.VMEM((coarse, HEAD_DIM), bf16),
            pltpu.VMEM((rows, HEAD_DIM), f32),
            pltpu.VMEM((rows, HEAD_DIM), f32),
            pltpu.VMEM((total, HEAD_DIM), f32),
            pltpu.VMEM((total, HEAD_DIM), f32),
            pltpu.VMEM((HEAD_DIM, coarse), bf16),
            pltpu.VMEM((HEAD_DIM, coarse), bf16),
            pltpu.VMEM((WINDOW // SHORT + TAIL, 256), bf16),
            pltpu.VMEM((WINDOW // SHORT + TAIL, 256), bf16),
            pltpu.VMEM((coarse + TAIL, HEAD_DIM), bf16),
            pltpu.VMEM((coarse + TAIL, HEAD_DIM), bf16),
        ],
    )(z, own, far, near_in, far2_in, far3_in, pair, part)

    back1_in = planes_up(back1, -1)
    back2_in = planes_up(back2, -2)
    back3_in = planes_up(back3, -3)
    attn_in = in_plane(attn.reshape(PLANE_DEVS, tokens, 256))
    width = out_grad.shape[1]
    part, kept = projected(attn_in, out_weight, width, blocks, 1, ())
    finished = call(
        finish_kernel,
        array(PLANE_DEVS, tokens + TAIL, 256),
        32,
        in_specs=[whole] * 6 + [in_place],
        scratch_shapes=[
            pltpu.VMEM((coarse + 2 * TAIL, 256), bf16),
            pltpu.VMEM((coarse + 2 * TAIL, 256), bf16),
        ],
    )(sums, fine, short, back1_in, back2_in, back3_in, kept)
    other, _ = projected(attn_in, out_weight, width, blocks, 3, (finished,))
    mixed_out = (part + swap(other.astype(bf16), "xl").astype(f32)).astype(bf16)
    returned = in_plane(finished)
    grads = call(unpack_kernel, (array(tokens, cols),) * 3, 16)(attn_in, returned)
    return (mixed_out, *grads)


def solution(mesh):
    fine_mesh = Mesh(np.asarray(mesh.devices).reshape(4, 4, 2, 2, 2), ("z", "y", "xh", "xl", "c"))
    both = P(("z", "y", "xh"), ("xl", "c"))
    in_specs = (both, both, both, P(("xl", "c"), None), both)
    return jax.shard_map(
        shards, mesh=fine_mesh, in_specs=in_specs, out_specs=(both,) * 4, check_vma=False
    )
```

```python
import functools
import math

import jax
import jax.numpy as jnp
import numpy as np
from jax import lax
from jax.experimental import pallas as pl
from jax.experimental.pallas import tpu as pltpu
from jax.sharding import Mesh, PartitionSpec as P

HEAD_DIM = 128
SHORT = 4
WINDOW = 1024
PLANES = 4
PLANE_DEVS = 8
BLOCK = 256
TAIL = 16
LOG2E = math.log2(math.e)
SCALE = 1.0 / math.sqrt(HEAD_DIM)
COARSE_SCALE = 2.0 * SCALE
FAR = -1e30
PLANE = ("y", "xh")
bf16 = jnp.bfloat16
f32 = jnp.float32


def call(kernel, out_shape, vmem_mib, **rest):
    return pl.pallas_call(
        kernel,
        out_shape=out_shape,
        compiler_params=pltpu.CompilerParams(vmem_limit_bytes=vmem_mib * 1024 * 1024),
        **rest,
    )


def dot(a, b):
    return jnp.dot(a, b, preferred_element_type=f32)


def dot_nt(a, b):
    return lax.dot_general(a, b, (((1,), (1,)), ((), ())), preferred_element_type=f32)


def iota(shape, dim):
    return lax.broadcasted_iota(jnp.int32, shape, dim)


def split(x):
    high = x.astype(bf16)
    return high, (x - high.astype(f32)).astype(bf16)


def ones_where(mask):
    return jnp.where(mask, 1.0, 0.0).astype(bf16)


def pack_kernel(q_ref, k_ref, v_ref, out_ref, sems):
    tokens = q_ref.shape[0]
    last = q_ref.shape[1] // HEAD_DIM - 1
    copies = []
    for slot in range(PLANE_DEVS):
        cols = pl.ds(min(slot, last) * HEAD_DIM, HEAD_DIM)
        tail = q_ref.at[tokens - TAIL :, cols]
        pieces = (
            (k_ref.at[:, cols], out_ref.at[slot, 0:tokens, 0:128]),
            (v_ref.at[:, cols], out_ref.at[slot, 0:tokens, 128:256]),
            (tail, out_ref.at[slot, tokens:, 0:128]),
            (tail, out_ref.at[slot, tokens:, 128:256]),
        )
        for at, (source, target) in enumerate(pieces):
            copies.append(pltpu.make_async_copy(source, target, sems.at[slot, at]))
    for copy in copies:
        copy.start()
    for copy in copies:
        copy.wait()


def pooling(lead):
    shape = (BLOCK // SHORT, BLOCK + lead)
    back = iota(shape, 1) - lead - SHORT * iota(shape, 0)
    return ones_where((back <= 0) & (back > -SHORT))


def spreading():
    shape = (BLOCK, BLOCK // SHORT + TAIL)
    return ones_where((iota(shape, 0) + (SHORT - 1)) // SHORT == iota(shape, 1))


def pooled_rows(block, lead=None):
    rows = block if lead is None else jnp.concatenate([lead, block], 0)
    taken = pooling(0 if lead is None else TAIL)
    return (dot(taken, rows) * (1.0 / SHORT)).astype(bf16)


def pool_kernel(x_ref, after_ref, near_ref, far_ref):
    del after_ref
    devs, tokens = x_ref.shape[0], x_ref.shape[1] - TAIL
    step = tokens // SHORT
    half = WINDOW // SHORT
    coarse = devs * step
    for slot in range(devs):
        block = x_ref[slot, 0:tokens, :]
        lead = x_ref[slot - 1, tokens - TAIL : tokens, :] if slot else None
        far_ref[slot * step : (slot + 1) * step, :] = pooled_rows(block, lead)
        late = slot * tokens - (devs * tokens - WINDOW)
        if late >= 0:
            near_ref[late : late + tokens, :] = block
    far_ref[coarse : coarse + TAIL, :] = x_ref[devs - 1, tokens - TAIL : tokens, :]
    near_ref[WINDOW : WINDOW + TAIL, :] = x_ref[devs - 1, tokens:, :]
    near_ref[WINDOW + TAIL :, :] = far_ref[0 : half + TAIL, :]


def first_row_fixed(pooled, tail):
    kept = jnp.where(iota(tail.shape, 0) > TAIL - SHORT, tail.astype(f32), 0.0)
    lacking = jnp.sum(kept, 0, keepdims=True) * (1.0 / SHORT)
    head = pooled[0:TAIL, :].astype(f32)
    return jnp.where(iota(head.shape, 0) == 0, head + lacking, head).astype(bf16)


def transposed(ref, out, count):
    def body(i, carry):
        at = pl.multiple_of(i * BLOCK, BLOCK)
        out[:, pl.ds(at, BLOCK)] = ref[pl.ds(at, BLOCK), :].T
        return carry

    lax.fori_loop(0, count, body, 0)


def weights(scores, biases, factor):
    tops = [jnp.max(s, 0, keepdims=True) + b for s, b in zip(scores, biases)]
    top = functools.reduce(jnp.maximum, tops)
    exps = [jnp.exp2((s - (top - b)) * factor) for s, b in zip(scores, biases)]
    total = functools.reduce(jnp.add, [jnp.sum(e, 0, keepdims=True) for e in exps])
    inverse = 1.0 / total
    return jnp.concatenate([e * inverse for e in exps], 0)


def window_block(at, query, grad, biases, kx, vx, kxt, vxt, dk, dv):
    span = WINDOW + BLOCK
    reach = WINDOW // BLOCK
    row_at, col_at = iota((BLOCK, BLOCK), 0), iota((BLOCK, BLOCK), 1)
    scores = []
    for piece in range(reach + 1):
        s = dot_nt(kx[pl.ds(pl.multiple_of(at + piece * BLOCK, BLOCK), BLOCK), :], query)
        if piece == 0:
            s = jnp.where(row_at > col_at, s, FAR)
        if piece == reach:
            s = jnp.where(row_at <= col_at, s, FAR)
        scores.append(s)
    probs = weights(scores, biases, SCALE * LOG2E)
    rounded = probs.astype(bf16)
    out_t = dot(vxt[:, pl.ds(at, span)], rounded)
    delta = jnp.sum(grad.astype(f32).T * out_t, 0, keepdims=True)
    grad_probs = dot_nt(vx[pl.ds(at, span), :], grad)
    grad_scores = (probs * (grad_probs - delta)).astype(bf16)
    dk[pl.ds(at, span), :] += dot(grad_scores, query)
    dv[pl.ds(at, span), :] += dot(rounded, grad)
    return out_t, dot(kxt[:, pl.ds(at, span)], grad_scores).T * SCALE


def own_kernel(x_ref, pair_ref, part_ref, sums_ref, kx, vx, kxt, vxt, dk, dv):
    rows = pair_ref.shape[0]
    tokens = rows // PLANE_DEVS
    for slot in range(PLANE_DEVS):
        at = slot * tokens
        kx[at : at + tokens, :] = x_ref[slot, 0:tokens, 0:128]
        vx[at : at + tokens, :] = x_ref[slot, 0:tokens, 128:256]
    transposed(kx, kxt, rows // BLOCK)
    transposed(vx, vxt, rows // BLOCK)
    dk[...] = jnp.zeros_like(dk)
    dv[...] = jnp.zeros_like(dv)

    def body(block, carry):
        at = pl.multiple_of(block * BLOCK, BLOCK)
        own = pl.ds(pl.multiple_of(WINDOW + at, BLOCK), BLOCK)
        biases = [0.0] * (WINDOW // BLOCK + 1)
        out_t, query_grad = window_block(
            at, pair_ref[own, 0:128], pair_ref[own, 128:256], biases, kx, vx, kxt, vxt, dk, dv
        )
        part_ref[pl.ds(at, BLOCK), 0:128] = out_t.T
        part_ref[pl.ds(at, BLOCK), 128:256] = query_grad
        return carry

    lax.fori_loop(0, (rows - WINDOW) // BLOCK, body, 0, unroll=4)
    sums_ref[:, 0:128] = dk[...] * SCALE
    sums_ref[:, 128:256] = dv[...]


def attention_kernel(
    z_ref,
    x_ref,
    own_ref,
    near_ref,
    far2_ref,
    far3_ref,
    pair_ref,
    part_ref,
    attn_ref,
    fine_ref,
    coarse_ref,
    back1_ref,
    back2_ref,
    back3_ref,
    kx,
    vx,
    kxt,
    vxt,
    kc,
    vc,
    kct,
    vct,
    pq,
    gp,
    dkx,
    dvx,
    dkc,
    dvc,
    high_t,
    low_t,
    high,
    low,
    query_high,
    query_low,
):
    z = z_ref[0]
    rows = pair_ref.shape[0]
    tokens = rows // PLANE_DEVS
    coarse = rows // SHORT
    half = WINDOW // SHORT
    step = BLOCK // SHORT
    reach = WINDOW // BLOCK

    kx[0:WINDOW, :] = near_ref[0:WINDOW, 0:128]
    vx[0:WINDOW, :] = near_ref[0:WINDOW, 128:256]
    for slot in range((rows - WINDOW) // tokens):
        at = WINDOW + slot * tokens
        kx[at : at + tokens, :] = x_ref[slot, 0:tokens, 0:128]
        vx[at : at + tokens, :] = x_ref[slot, 0:tokens, 128:256]

    transposed(kx, kxt, rows // BLOCK)
    transposed(vx, vxt, rows // BLOCK)

    tails = [
        near_ref[WINDOW - TAIL : WINDOW, :],
        far2_ref[coarse : coarse + TAIL, :],
        far3_ref[coarse : coarse + TAIL, :],
    ]
    base = WINDOW + TAIL
    for piece in range(reach):
        at = coarse + half + piece * step
        block = near_ref[piece * BLOCK : (piece + 1) * BLOCK, :]
        lead = near_ref[piece * BLOCK - TAIL : piece * BLOCK, :] if piece else None
        rest = pooled_rows(block, lead)
        kc[at : at + step, :] = rest[:, 0:128]
        vc[at : at + step, :] = rest[:, 128:256]
    sources = ((own_ref, coarse), (near_ref.at[base:], half + TAIL), (far2_ref, coarse), (far3_ref, coarse))
    for slot, (source, count) in enumerate(sources):
        at = slot * coarse
        kc[at : at + count, :] = source[0:count, 0:128]
        vc[at : at + count, :] = source[0:count, 128:256]
        if slot + 1 < PLANES:
            fixed = first_row_fixed(source[0:TAIL, :], tails[slot])
            kc[at : at + TAIL, :] = fixed[:, 0:128]
            vc[at : at + TAIL, :] = fixed[:, 128:256]
    transposed(kc, kct, PLANES * coarse // BLOCK)
    transposed(vc, vct, PLANES * coarse // BLOCK)

    shape = (step, BLOCK)
    offset = iota(shape, 1) - SHORT * iota(shape, 0)
    taken = ones_where((offset >= 0) & (offset < SHORT))
    for block in range(rows // BLOCK):
        at = block * BLOCK
        lead = pair_ref[at - TAIL : at, 0:128] if block else near_ref[WINDOW : WINDOW + TAIL, 0:128]
        pq[block * step : (block + 1) * step, :] = pooled_rows(pair_ref[at : at + BLOCK, 0:128], lead)
        gp[block * step : (block + 1) * step, :] = dot(
            taken, pair_ref[at : at + BLOCK, 128:256]
        ).astype(bf16)

    row_at, col_at = iota((BLOCK, BLOCK), 0), iota((BLOCK, BLOCK), 1)
    diagonal = row_at <= col_at
    for block in range(coarse // BLOCK):
        at = block * BLOCK
        query = pq[at : at + BLOCK, :]
        grad = gp[at : at + BLOCK, :]
        scores, biases, keys, values = [], [], [], []
        for piece in range(block + 1):
            s = dot_nt(kc[piece * BLOCK : (piece + 1) * BLOCK, :], query)
            scores.append(jnp.where(diagonal, s, FAR) if piece == block else s)
            biases.append(0.0)
        for slot in range(1, PLANES):
            s = dot_nt(kc[slot * coarse : (slot + 1) * coarse, :], query)
            scores.append(s)
            biases.append(jnp.where(z >= slot, 0.0, FAR))
        probs = weights(scores, biases, COARSE_SCALE * LOG2E)
        rounded = probs.astype(bf16)
        own = at + BLOCK
        parts = ((0, own, 0), (coarse, PLANES * coarse, own))
        out_t = functools.reduce(
            jnp.add, [dot(vct[:, a:b], rounded[c : c + b - a]) for a, b, c in parts]
        )
        grad_t = grad.astype(f32).T
        delta = jnp.sum(grad_t * out_t, 0, keepdims=True)
        high_t[:, at : at + BLOCK], low_t[:, at : at + BLOCK] = split(out_t)
        query_grad_t = jnp.zeros((HEAD_DIM, BLOCK), f32)
        for a, b, c in parts:
            grad_probs = dot_nt(vc[a:b, :], grad)
            grad_scores = (probs[c : c + b - a] * (grad_probs - delta)).astype(bf16)
            query_grad_t += dot(kct[:, a:b], grad_scores)
            dk = dot(grad_scores, query) * COARSE_SCALE
            dv = dot(rounded[c : c + b - a], grad)
            if block == 0:
                dkc[a:b, :] = dk
                dvc[a:b, :] = dv
                if a == 0:
                    dkc[b:coarse, :] = jnp.zeros((coarse - b, HEAD_DIM), f32)
                    dvc[b:coarse, :] = jnp.zeros((coarse - b, HEAD_DIM), f32)
            else:
                dkc[a:b, :] += dk
                dvc[a:b, :] += dv
        query_grad = query_grad_t.T * COARSE_SCALE
        query_high[at : at + BLOCK, :], query_low[at : at + BLOCK, :] = split(query_grad)
    query_high[coarse:, :] = jnp.zeros((TAIL, HEAD_DIM), bf16)
    query_low[coarse:, :] = jnp.zeros((TAIL, HEAD_DIM), bf16)
    coarse_ref[:, 0:128] = dkc[0:coarse, :]
    coarse_ref[:, 128:256] = dvc[0:coarse, :]

    dkx[...] = jnp.zeros_like(dkx)
    dvx[...] = jnp.zeros_like(dvx)

    def short_out(block):
        pair = pl.multiple_of(block // 2 * (2 * step), 2 * step)
        shape = (2 * step, BLOCK)
        spread = ones_where(iota(shape, 0) == block % 2 * step + iota(shape, 1) // SHORT)
        short_t = dot(high_t[:, pl.ds(pair, 2 * step)], spread)
        return short_t + dot(low_t[:, pl.ds(pair, 2 * step)], spread)

    def short_query_grad(block):
        below = pl.ds(pl.multiple_of(block * step, step), step + TAIL)
        spread = dot(spreading(), query_high[below, :]) + dot(spreading(), query_low[below, :])
        return spread * (1.0 / SHORT)

    def window(block, carry):
        at = pl.multiple_of(block * BLOCK, BLOCK)
        here = pl.ds(at, BLOCK)
        biases = [jnp.where((z == 0) & (block + piece < reach), FAR, 0.0) for piece in range(reach + 1)]
        out_t, query_grad = window_block(
            at, pair_ref[here, 0:128], pair_ref[here, 128:256], biases, kx, vx, kxt, vxt, dkx, dvx
        )
        attn_ref[here, 0:128] = (out_t + short_out(block)).T.astype(bf16)
        attn_ref[here, 128:256] = (query_grad + short_query_grad(block)).astype(bf16)
        late = pl.ds(pl.multiple_of(WINDOW + at, BLOCK), BLOCK)
        attn_ref[late, 0:128] = (part_ref[here, 0:128] + short_out(block + reach).T).astype(bf16)
        attn_ref[late, 128:256] = (part_ref[here, 128:256] + short_query_grad(block + reach)).astype(bf16)
        return carry

    lax.fori_loop(0, reach, window, 0, unroll=4)
    fine_ref[:, 0:128] = dkx[WINDOW:, :] * SCALE
    fine_ref[:, 128:256] = dvx[WINDOW:, :]

    first = iota((TAIL, HEAD_DIM), 0) == 0
    for cols, short in ((slice(0, 128), dkc), (slice(128, 256), dvc)):
        high[0:half, cols], low[0:half, cols] = split(short[2 * coarse - half : 2 * coarse, :])
        above = jnp.where(first, short[0:TAIL, :], 0.0)
        high[half:, cols], low[half:, cols] = split(above)
    taken = spreading()
    for piece in range(reach):
        at = piece * BLOCK
        below = piece * step
        spread = dot(taken, high[below : below + step + TAIL, :])
        spread += dot(taken, low[below : below + step + TAIL, :])
        spread = spread * (1.0 / SHORT)
        back1_ref[at : at + BLOCK, 0:128] = (
            dkx[at : at + BLOCK, :] * SCALE + spread[:, 0:128]
        ).astype(bf16)
        back1_ref[at : at + BLOCK, 128:256] = (
            dvx[at : at + BLOCK, :] + spread[:, 128:256]
        ).astype(bf16)
    query_row = jnp.where(first, query_high[0:TAIL, :].astype(f32), 0.0).astype(bf16)
    back1_ref[WINDOW:base, 0:128] = query_row
    back1_ref[WINDOW:base, 128:256] = query_row
    back1_ref[base:, 0:128] = dkc[coarse : coarse + half + TAIL, :].astype(bf16)
    back1_ref[base:, 128:256] = dvc[coarse : coarse + half + TAIL, :].astype(bf16)
    for slot, ref in ((2, back2_ref), (3, back3_ref)):
        at = slot * coarse
        above = at - coarse
        for cols, short in ((slice(0, 128), dkc), (slice(128, 256), dvc)):
            ref[0:coarse, cols] = short[at : at + coarse, :].astype(bf16)
            row = jnp.where(first, short[above : above + TAIL, :], 0.0)
            ref[coarse : coarse + TAIL, cols] = row.astype(bf16)


def finish_kernel(
    sums_ref, fine_ref, coarse_ref, back1_ref, back2_ref, back3_ref, after_ref, out_ref, high, low
):
    del after_ref
    rows = sums_ref.shape[0]
    tokens = rows // PLANE_DEVS
    coarse = rows // SHORT
    half = coarse - WINDOW // SHORT
    step = BLOCK // SHORT
    base = WINDOW + TAIL
    part = half + TAIL
    ups = (back2_ref, back3_ref)
    total = coarse_ref[...]
    for up in ups:
        total += up[0:coarse, :].astype(f32)
    near = total[0:part, :] + back1_ref[base:, :].astype(f32)
    high[0:part, :], low[0:part, :] = split(near)
    high[part : part + half, :], low[part : part + half, :] = split(total[half:, :])
    extra = functools.reduce(jnp.add, [up[coarse : coarse + TAIL, :].astype(f32) for up in ups])
    high[part + half :, :], low[part + half :, :] = split(extra)
    taken = spreading()
    for block in range(rows // BLOCK):
        at = block * BLOCK
        late = at - (rows - WINDOW)
        below = block * step if late < 0 else part + late // SHORT
        spread = dot(taken, high[below : below + step + TAIL, :])
        spread += dot(taken, low[below : below + step + TAIL, :])
        result = sums_ref[at : at + BLOCK, :] + spread * (1.0 / SHORT)
        if late < 0:
            result = result + fine_ref[at : at + BLOCK, :]
        else:
            result = result + back1_ref[late : late + BLOCK, :].astype(f32)
        out_ref[block, 0:tokens, :] = result.astype(bf16)
        out_ref[block, tokens:, :] = jnp.zeros((TAIL, 256), bf16)
    out_ref[PLANE_DEVS - 1, tokens:, :] = back1_ref[WINDOW:base, :]


def unpack_kernel(pair_ref, x_ref, q_ref, k_ref, v_ref):
    tokens = q_ref.shape[0]
    last = iota((TAIL, HEAD_DIM), 0) > TAIL - SHORT
    for slot in range(q_ref.shape[1] // HEAD_DIM):
        cols = pl.ds(slot * HEAD_DIM, HEAD_DIM)
        k_ref[:, cols] = x_ref[slot, 0:tokens, 0:128]
        v_ref[:, cols] = x_ref[slot, 0:tokens, 128:256]
        q_ref[0 : tokens - TAIL, cols] = pair_ref[slot, 0 : tokens - TAIL, 128:256]
        above = jnp.sum(x_ref[slot, tokens:, 0:128].astype(f32), 0, keepdims=True) * (1.0 / SHORT)
        rest = pair_ref[slot, tokens - TAIL :, 128:256].astype(f32)
        q_ref[tokens - TAIL :, cols] = (rest + jnp.where(last, above, 0.0)).astype(bf16)


def grad_product(halves, a_ref, b_ref, w_ref, total, start):
    at = pl.program_id(0)
    depth = w_ref.shape[1]
    for piece, ref in enumerate((a_ref, b_ref)):
        for half in range(halves):

            @pl.when(at == piece * halves + half)
            def _():
                product = dot_nt(w_ref[...], ref[:, half * depth : (half + 1) * depth])
                if piece + half > 0:
                    total[...] += product
                elif start is None:
                    total[...] = product
                else:
                    total[...] = start[...] + product


def grad_near_kernel(halves, order_ref, a_ref, b_ref, w_ref, total):
    grad_product(halves, a_ref, b_ref, w_ref, total, None)


def grad_far_kernel(halves, order_ref, a_ref, b_ref, w_ref, start, q_ref, out_ref, total):
    grad_product(halves, a_ref, b_ref, w_ref, total, start)

    @pl.when(pl.program_id(0) == pl.num_programs(0) - 1)
    def _():
        last = total.shape[0] // HEAD_DIM - 1
        for slot in range(PLANE_DEVS):
            head = slice(min(slot, last) * HEAD_DIM, (min(slot, last) + 1) * HEAD_DIM)
            out_ref[slot, :, 0:128] = q_ref[:, head]
            out_ref[slot, :, 128:256] = total[head, :].T.astype(bf16)


def grad_part(pieces, order, weight, rest=()):
    rows, width = pieces[0].shape
    depth = weight.shape[0]
    halves = 1
    tile = width // halves

    first = 2 if rest else 0

    def whole(shape):
        return pl.BlockSpec(shape, lambda i, o: (0,) * len(shape))

    packed = (PLANE_DEVS, rows, 2 * HEAD_DIM)
    return pl.pallas_call(
        functools.partial(grad_far_kernel if rest else grad_near_kernel, halves),
        out_shape=jax.ShapeDtypeStruct(packed, bf16) if rest else jax.ShapeDtypeStruct((depth, rows), f32),
        grid_spec=pltpu.PrefetchScalarGridSpec(
            num_scalar_prefetch=1,
            grid=(2 * halves,),
            in_specs=[whole((rows, width))] * 2
            + [pl.BlockSpec((depth, tile), lambda i, o: (0, o[first + i // halves] * halves + i % halves))]
            + [whole(x.shape) for x in rest],
            out_specs=whole(packed if rest else (depth, rows)),
            scratch_shapes=[pltpu.VMEM((depth, rows), f32)] if rest else [],
        ),
        compiler_params=pltpu.CompilerParams(vmem_limit_bytes=62 * 1024 * 1024),
    )(order, *pieces, weight, *rest)


def project_kernel(halves, order_ref, attn_ref, w_ref, *refs):
    send_ref, keep_ref, rows_ref = refs[-3:]
    at = pl.program_id(0)
    heads = w_ref.shape[0] // HEAD_DIM
    tile = w_ref.shape[1]

    @pl.when(at == 0)
    def _():
        for slot in range(heads):
            rows_ref[:, slot * HEAD_DIM : (slot + 1) * HEAD_DIM] = attn_ref[slot, :, 0:128]

    product = dot(rows_ref[...], w_ref[...]).astype(bf16)
    for half in range(halves):

        @pl.when(at == half)
        def _():
            send_ref[:, half * tile : (half + 1) * tile] = product

        @pl.when(at == halves + half)
        def _():
            keep_ref[:, half * tile : (half + 1) * tile] = product


def project(attn, order, last, weight, width, after):
    rows = attn.shape[1]
    depth = weight.shape[0]
    halves = 1
    tile = width // halves
    out = jax.ShapeDtypeStruct((rows, width), bf16)
    return pl.pallas_call(
        functools.partial(project_kernel, halves),
        out_shape=(out, out),
        grid_spec=pltpu.PrefetchScalarGridSpec(
            num_scalar_prefetch=1,
            grid=(2 * halves,),
            in_specs=[
                pl.BlockSpec(attn.shape, lambda i, o: (0, 0, 0)),
                pl.BlockSpec((depth, tile), lambda i, o: (0, o[last - i // halves] * halves + i % halves)),
            ]
            + [pl.BlockSpec(memory_space=pltpu.HBM)] * len(after),
            out_specs=[pl.BlockSpec((rows, width), lambda i, o: (0, 0))] * 2,
            scratch_shapes=[pltpu.VMEM((rows, depth), bf16)],
        ),
        compiler_params=pltpu.CompilerParams(vmem_limit_bytes=64 * 1024 * 1024),
    )(order, attn, weight, *after)


def swap(x, axis):
    return lax.ppermute(x, axis, [(0, 1), (1, 0)])


def planes_up(x, by):
    return lax.ppermute(x, "z", [(i, i + by) for i in range(PLANES) if 0 <= i + by < PLANES])


def in_plane(x):
    return lax.all_to_all(x, PLANE, 0, 0, tiled=True)


def column_blocks():
    xl, core = lax.axis_index("xl"), lax.axis_index("c")
    own, other = 2 * xl, 2 * (1 - xl)
    return jnp.stack([own + core, own + 1 - core, other + core, other + 1 - core]).astype(jnp.int32)


def gathered_grad(out_grad, out_weight, q_proj, blocks):
    far = swap(out_grad, "xl")
    near = swap(out_grad, "c")
    start = grad_part((out_grad, near), blocks, out_weight)
    far, start = lax.optimization_barrier((far, start))
    both = swap(far, "c")
    return start, grad_part((far, both), blocks, out_weight, (start, q_proj))


def projected(attn, out_weight, width, blocks, last, after):
    send, keep = project(attn, blocks, last, out_weight, width, after)
    return keep.astype(f32) + swap(send, "c").astype(f32), keep


def shards(q_proj, k_proj, v_proj, out_weight, out_grad):
    tokens, cols = q_proj.shape
    rows = tokens * PLANE_DEVS
    coarse = rows // SHORT
    total = PLANES * coarse
    z = lax.axis_index("z").astype(jnp.int32).reshape(1)

    def array(*shape, dtype=bf16):
        return jax.ShapeDtypeStruct(shape, dtype)

    in_place = pl.BlockSpec(memory_space=pltpu.HBM)
    whole = pl.BlockSpec(memory_space=pltpu.VMEM)
    packed = call(
        pack_kernel,
        array(PLANE_DEVS, tokens + TAIL, 2 * HEAD_DIM),
        62,
        in_specs=[in_place] * 3,
        out_specs=whole,
        scratch_shapes=[pltpu.SemaphoreType.DMA((PLANE_DEVS, 4))],
    )(q_proj, k_proj, v_proj)
    own = in_plane(packed)
    blocks = column_blocks()
    early, pair_packed = gathered_grad(out_grad, out_weight, q_proj, blocks)
    near_rows = WINDOW + 2 * TAIL + WINDOW // SHORT
    near, far = call(
        pool_kernel,
        (array(near_rows, 256), array(coarse + TAIL, 256)),
        16,
        in_specs=[whole, in_place],
    )(own, early)
    near_in = planes_up(near, 1)
    far2_in = planes_up(far, 2)
    far3_in = planes_up(far, 3)
    pair = in_plane(pair_packed).reshape(rows, 2 * HEAD_DIM)

    part, sums = call(
        own_kernel,
        (array(rows - WINDOW, 256, dtype=f32), array(rows, 256, dtype=f32)),
        56,
        in_specs=[whole] * 2,
        out_specs=[whole] * 2,
        scratch_shapes=[pltpu.VMEM((rows, HEAD_DIM), bf16)] * 2
        + [pltpu.VMEM((HEAD_DIM, rows), bf16)] * 2
        + [pltpu.VMEM((rows, HEAD_DIM), f32)] * 2,
    )(own, pair)
    attn, fine, short, back1, back2, back3 = call(
        attention_kernel,
        (
            array(rows, 256),
            array(rows - WINDOW, 256, dtype=f32),
            array(coarse, 256, dtype=f32),
            array(near_rows, 256),
            array(coarse + TAIL, 256),
            array(coarse + TAIL, 256),
        ),
        62,
        in_specs=[pl.BlockSpec(memory_space=pltpu.SMEM)] + [whole] * 7,
        out_specs=[whole] * 6,
        scratch_shapes=[
            pltpu.VMEM((rows, HEAD_DIM), bf16),
            pltpu.VMEM((rows, HEAD_DIM), bf16),
            pltpu.VMEM((HEAD_DIM, rows), bf16),
            pltpu.VMEM((HEAD_DIM, rows), bf16),
            pltpu.VMEM((total, HEAD_DIM), bf16),
            pltpu.VMEM((total, HEAD_DIM), bf16),
            pltpu.VMEM((HEAD_DIM, total), bf16),
            pltpu.VMEM((HEAD_DIM, total), bf16),
            pltpu.VMEM((coarse, HEAD_DIM), bf16),
            pltpu.VMEM((coarse, HEAD_DIM), bf16),
            pltpu.VMEM((rows, HEAD_DIM), f32),
            pltpu.VMEM((rows, HEAD_DIM), f32),
            pltpu.VMEM((total, HEAD_DIM), f32),
            pltpu.VMEM((total, HEAD_DIM), f32),
            pltpu.VMEM((HEAD_DIM, coarse), bf16),
            pltpu.VMEM((HEAD_DIM, coarse), bf16),
            pltpu.VMEM((WINDOW // SHORT + TAIL, 256), bf16),
            pltpu.VMEM((WINDOW // SHORT + TAIL, 256), bf16),
            pltpu.VMEM((coarse + TAIL, HEAD_DIM), bf16),
            pltpu.VMEM((coarse + TAIL, HEAD_DIM), bf16),
        ],
    )(z, own, far, near_in, far2_in, far3_in, pair, part)

    back1_in = planes_up(back1, -1)
    back2_in = planes_up(back2, -2)
    back3_in = planes_up(back3, -3)
    attn_in = in_plane(attn.reshape(PLANE_DEVS, tokens, 256))
    width = out_grad.shape[1]
    part, kept = projected(attn_in, out_weight, width, blocks, 1, ())
    finished = call(
        finish_kernel,
        array(PLANE_DEVS, tokens + TAIL, 256),
        64,
        in_specs=[whole] * 6 + [in_place],
        scratch_shapes=[
            pltpu.VMEM((coarse + 2 * TAIL, 256), bf16),
            pltpu.VMEM((coarse + 2 * TAIL, 256), bf16),
        ],
    )(sums, fine, short, back1_in, back2_in, back3_in, kept)
    other, _ = projected(attn_in, out_weight, width, blocks, 3, (finished,))
    mixed_out = (part + swap(other.astype(bf16), "xl").astype(f32)).astype(bf16)
    returned = in_plane(finished)
    grads = call(unpack_kernel, (array(tokens, cols),) * 3, 16)(attn_in, returned)
    return (mixed_out, *grads)


def solution(mesh):
    fine_mesh = Mesh(np.asarray(mesh.devices).reshape(4, 4, 2, 2, 2), ("z", "y", "xh", "xl", "c"))
    both = P(("z", "y", "xh"), ("xl", "c"))
    in_specs = (both, both, both, P(("xl", "c"), None), both)
    return jax.shard_map(
        shards, mesh=fine_mesh, in_specs=in_specs, out_specs=(both,) * 4, check_vma=False
    )
```

```python
import functools
import math

import jax
import jax.numpy as jnp
import numpy as np
from jax import lax
from jax.experimental import pallas as pl
from jax.experimental.pallas import tpu as pltpu
from jax.sharding import Mesh, PartitionSpec as P

HEAD_DIM = 128
SHORT = 4
WINDOW = 1024
PLANES = 4
PLANE_DEVS = 8
BLOCK = 256
TAIL = 16
LOG2E = math.log2(math.e)
SCALE = 1.0 / math.sqrt(HEAD_DIM)
COARSE_SCALE = 2.0 * SCALE
FAR = -1e30
PLANE = ("y", "xh")
bf16 = jnp.bfloat16
f32 = jnp.float32


def call(kernel, out_shape, vmem_mib, **rest):
    return pl.pallas_call(
        kernel,
        out_shape=out_shape,
        compiler_params=pltpu.CompilerParams(vmem_limit_bytes=vmem_mib * 1024 * 1024),
        **rest,
    )


def dot(a, b):
    return jnp.dot(a, b, preferred_element_type=f32)


def dot_nt(a, b):
    return lax.dot_general(a, b, (((1,), (1,)), ((), ())), preferred_element_type=f32)


def iota(shape, dim):
    return lax.broadcasted_iota(jnp.int32, shape, dim)


def split(x):
    high = x.astype(bf16)
    return high, (x - high.astype(f32)).astype(bf16)


def ones_where(mask):
    return jnp.where(mask, 1.0, 0.0).astype(bf16)


def pack_kernel(q_ref, k_ref, v_ref, out_ref, sems):
    tokens = q_ref.shape[0]
    last = q_ref.shape[1] // HEAD_DIM - 1
    copies = []
    for slot in range(PLANE_DEVS):
        cols = pl.ds(min(slot, last) * HEAD_DIM, HEAD_DIM)
        tail = q_ref.at[tokens - TAIL :, cols]
        pieces = (
            (k_ref.at[:, cols], out_ref.at[slot, 0:tokens, 0:128]),
            (v_ref.at[:, cols], out_ref.at[slot, 0:tokens, 128:256]),
            (tail, out_ref.at[slot, tokens:, 0:128]),
            (tail, out_ref.at[slot, tokens:, 128:256]),
        )
        for at, (source, target) in enumerate(pieces):
            copies.append(pltpu.make_async_copy(source, target, sems.at[slot, at]))
    for copy in copies:
        copy.start()
    for copy in copies:
        copy.wait()


def pooling(lead):
    shape = (BLOCK // SHORT, BLOCK + lead)
    back = iota(shape, 1) - lead - SHORT * iota(shape, 0)
    return ones_where((back <= 0) & (back > -SHORT))


def spreading():
    shape = (BLOCK, BLOCK // SHORT + TAIL)
    return ones_where((iota(shape, 0) + (SHORT - 1)) // SHORT == iota(shape, 1))


def pooled_rows(block, lead=None):
    rows = block if lead is None else jnp.concatenate([lead, block], 0)
    taken = pooling(0 if lead is None else TAIL)
    return (dot(taken, rows) * (1.0 / SHORT)).astype(bf16)


def pool_kernel(x_ref, after_ref, near_ref, far_ref):
    del after_ref
    devs, tokens = x_ref.shape[0], x_ref.shape[1] - TAIL
    step = tokens // SHORT
    half = WINDOW // SHORT
    coarse = devs * step
    for slot in range(devs):
        block = x_ref[slot, 0:tokens, :]
        lead = x_ref[slot - 1, tokens - TAIL : tokens, :] if slot else None
        far_ref[slot * step : (slot + 1) * step, :] = pooled_rows(block, lead)
        late = slot * tokens - (devs * tokens - WINDOW)
        if late >= 0:
            near_ref[late : late + tokens, :] = block
    far_ref[coarse : coarse + TAIL, :] = x_ref[devs - 1, tokens - TAIL : tokens, :]
    near_ref[WINDOW : WINDOW + TAIL, :] = x_ref[devs - 1, tokens:, :]
    near_ref[WINDOW + TAIL :, :] = far_ref[0 : half + TAIL, :]


def first_row_fixed(pooled, tail):
    kept = jnp.where(iota(tail.shape, 0) > TAIL - SHORT, tail.astype(f32), 0.0)
    lacking = jnp.sum(kept, 0, keepdims=True) * (1.0 / SHORT)
    head = pooled[0:TAIL, :].astype(f32)
    return jnp.where(iota(head.shape, 0) == 0, head + lacking, head).astype(bf16)


def transposed(ref, out, count):
    def body(i, carry):
        at = pl.multiple_of(i * BLOCK, BLOCK)
        out[:, pl.ds(at, BLOCK)] = ref[pl.ds(at, BLOCK), :].T
        return carry

    lax.fori_loop(0, count, body, 0)


def weights(scores, biases, factor):
    tops = [jnp.max(s, 0, keepdims=True) + b for s, b in zip(scores, biases)]
    top = functools.reduce(jnp.maximum, tops)
    exps = [jnp.exp2((s - (top - b)) * factor) for s, b in zip(scores, biases)]
    total = functools.reduce(jnp.add, [jnp.sum(e, 0, keepdims=True) for e in exps])
    inverse = 1.0 / total
    return jnp.concatenate([e * inverse for e in exps], 0)


def window_block(at, query, grad, biases, kx, vx, kxt, vxt, dk, dv):
    span = WINDOW + BLOCK
    reach = WINDOW // BLOCK
    row_at, col_at = iota((BLOCK, BLOCK), 0), iota((BLOCK, BLOCK), 1)
    scores = []
    for piece in range(reach + 1):
        s = dot_nt(kx[pl.ds(pl.multiple_of(at + piece * BLOCK, BLOCK), BLOCK), :], query)
        if piece == 0:
            s = jnp.where(row_at > col_at, s, FAR)
        if piece == reach:
            s = jnp.where(row_at <= col_at, s, FAR)
        scores.append(s)
    probs = weights(scores, biases, SCALE * LOG2E)
    rounded = probs.astype(bf16)
    out_t = dot(vxt[:, pl.ds(at, span)], rounded)
    delta = jnp.sum(grad.astype(f32).T * out_t, 0, keepdims=True)
    grad_probs = dot_nt(vx[pl.ds(at, span), :], grad)
    grad_scores = (probs * (grad_probs - delta)).astype(bf16)
    dk[pl.ds(at, span), :] += dot(grad_scores, query)
    dv[pl.ds(at, span), :] += dot(rounded, grad)
    return out_t, dot(kxt[:, pl.ds(at, span)], grad_scores).T * SCALE


def own_kernel(x_ref, pair_ref, part_ref, sums_ref, kx, vx, kxt, vxt, dk, dv):
    rows = pair_ref.shape[0]
    tokens = rows // PLANE_DEVS
    for slot in range(PLANE_DEVS):
        at = slot * tokens
        kx[at : at + tokens, :] = x_ref[slot, 0:tokens, 0:128]
        vx[at : at + tokens, :] = x_ref[slot, 0:tokens, 128:256]
    transposed(kx, kxt, rows // BLOCK)
    transposed(vx, vxt, rows // BLOCK)
    dk[...] = jnp.zeros_like(dk)
    dv[...] = jnp.zeros_like(dv)

    def body(block, carry):
        at = pl.multiple_of(block * BLOCK, BLOCK)
        own = pl.ds(pl.multiple_of(WINDOW + at, BLOCK), BLOCK)
        biases = [0.0] * (WINDOW // BLOCK + 1)
        out_t, query_grad = window_block(
            at, pair_ref[own, 0:128], pair_ref[own, 128:256], biases, kx, vx, kxt, vxt, dk, dv
        )
        part_ref[pl.ds(at, BLOCK), 0:128] = out_t.T
        part_ref[pl.ds(at, BLOCK), 128:256] = query_grad
        return carry

    lax.fori_loop(0, (rows - WINDOW) // BLOCK, body, 0, unroll=4)
    sums_ref[:, 0:128] = dk[...] * SCALE
    sums_ref[:, 128:256] = dv[...]


def attention_kernel(
    z_ref,
    x_ref,
    own_ref,
    near_ref,
    far2_ref,
    far3_ref,
    pair_ref,
    part_ref,
    attn_ref,
    fine_ref,
    coarse_ref,
    back1_ref,
    back2_ref,
    back3_ref,
    kx,
    vx,
    kxt,
    vxt,
    kc,
    vc,
    kct,
    vct,
    pq,
    gp,
    dkx,
    dvx,
    dkc,
    dvc,
    high_t,
    low_t,
    high,
    low,
    query_high,
    query_low,
):
    z = z_ref[0]
    rows = pair_ref.shape[0]
    tokens = rows // PLANE_DEVS
    coarse = rows // SHORT
    half = WINDOW // SHORT
    step = BLOCK // SHORT
    reach = WINDOW // BLOCK

    kx[0:WINDOW, :] = near_ref[0:WINDOW, 0:128]
    vx[0:WINDOW, :] = near_ref[0:WINDOW, 128:256]
    for slot in range((rows - WINDOW) // tokens):
        at = WINDOW + slot * tokens
        kx[at : at + tokens, :] = x_ref[slot, 0:tokens, 0:128]
        vx[at : at + tokens, :] = x_ref[slot, 0:tokens, 128:256]

    transposed(kx, kxt, rows // BLOCK)
    transposed(vx, vxt, rows // BLOCK)

    tails = [
        near_ref[WINDOW - TAIL : WINDOW, :],
        far2_ref[coarse : coarse + TAIL, :],
        far3_ref[coarse : coarse + TAIL, :],
    ]
    base = WINDOW + TAIL
    for piece in range(reach):
        at = coarse + half + piece * step
        block = near_ref[piece * BLOCK : (piece + 1) * BLOCK, :]
        lead = near_ref[piece * BLOCK - TAIL : piece * BLOCK, :] if piece else None
        rest = pooled_rows(block, lead)
        kc[at : at + step, :] = rest[:, 0:128]
        vc[at : at + step, :] = rest[:, 128:256]
    sources = ((own_ref, coarse), (near_ref.at[base:], half + TAIL), (far2_ref, coarse), (far3_ref, coarse))
    for slot, (source, count) in enumerate(sources):
        at = slot * coarse
        kc[at : at + count, :] = source[0:count, 0:128]
        vc[at : at + count, :] = source[0:count, 128:256]
        if slot + 1 < PLANES:
            fixed = first_row_fixed(source[0:TAIL, :], tails[slot])
            kc[at : at + TAIL, :] = fixed[:, 0:128]
            vc[at : at + TAIL, :] = fixed[:, 128:256]
    transposed(kc, kct, PLANES * coarse // BLOCK)
    transposed(vc, vct, PLANES * coarse // BLOCK)

    shape = (step, BLOCK)
    offset = iota(shape, 1) - SHORT * iota(shape, 0)
    taken = ones_where((offset >= 0) & (offset < SHORT))
    for block in range(rows // BLOCK):
        at = block * BLOCK
        lead = pair_ref[at - TAIL : at, 0:128] if block else near_ref[WINDOW : WINDOW + TAIL, 0:128]
        pq[block * step : (block + 1) * step, :] = pooled_rows(pair_ref[at : at + BLOCK, 0:128], lead)
        gp[block * step : (block + 1) * step, :] = dot(
            taken, pair_ref[at : at + BLOCK, 128:256]
        ).astype(bf16)

    row_at, col_at = iota((BLOCK, BLOCK), 0), iota((BLOCK, BLOCK), 1)
    diagonal = row_at <= col_at
    for block in range(coarse // BLOCK):
        at = block * BLOCK
        query = pq[at : at + BLOCK, :]
        grad = gp[at : at + BLOCK, :]
        scores, biases, keys, values = [], [], [], []
        for piece in range(block + 1):
            s = dot_nt(kc[piece * BLOCK : (piece + 1) * BLOCK, :], query)
            scores.append(jnp.where(diagonal, s, FAR) if piece == block else s)
            biases.append(0.0)
        for slot in range(1, PLANES):
            s = dot_nt(kc[slot * coarse : (slot + 1) * coarse, :], query)
            scores.append(s)
            biases.append(jnp.where(z >= slot, 0.0, FAR))
        probs = weights(scores, biases, COARSE_SCALE * LOG2E)
        rounded = probs.astype(bf16)
        own = at + BLOCK
        parts = ((0, own, 0), (coarse, PLANES * coarse, own))
        out_t = functools.reduce(
            jnp.add, [dot(vct[:, a:b], rounded[c : c + b - a]) for a, b, c in parts]
        )
        grad_t = grad.astype(f32).T
        delta = jnp.sum(grad_t * out_t, 0, keepdims=True)
        high_t[:, at : at + BLOCK], low_t[:, at : at + BLOCK] = split(out_t)
        query_grad_t = jnp.zeros((HEAD_DIM, BLOCK), f32)
        for a, b, c in parts:
            grad_probs = dot_nt(vc[a:b, :], grad)
            grad_scores = (probs[c : c + b - a] * (grad_probs - delta)).astype(bf16)
            query_grad_t += dot(kct[:, a:b], grad_scores)
            dk = dot(grad_scores, query) * COARSE_SCALE
            dv = dot(rounded[c : c + b - a], grad)
            if block == 0:
                dkc[a:b, :] = dk
                dvc[a:b, :] = dv
                if a == 0:
                    dkc[b:coarse, :] = jnp.zeros((coarse - b, HEAD_DIM), f32)
                    dvc[b:coarse, :] = jnp.zeros((coarse - b, HEAD_DIM), f32)
            else:
                dkc[a:b, :] += dk
                dvc[a:b, :] += dv
        query_grad = query_grad_t.T * COARSE_SCALE
        query_high[at : at + BLOCK, :], query_low[at : at + BLOCK, :] = split(query_grad)
    query_high[coarse:, :] = jnp.zeros((TAIL, HEAD_DIM), bf16)
    query_low[coarse:, :] = jnp.zeros((TAIL, HEAD_DIM), bf16)
    coarse_ref[:, 0:128] = dkc[0:coarse, :]
    coarse_ref[:, 128:256] = dvc[0:coarse, :]

    dkx[...] = jnp.zeros_like(dkx)
    dvx[...] = jnp.zeros_like(dvx)

    def short_out(block):
        pair = pl.multiple_of(block // 2 * (2 * step), 2 * step)
        shape = (2 * step, BLOCK)
        spread = ones_where(iota(shape, 0) == block % 2 * step + iota(shape, 1) // SHORT)
        short_t = dot(high_t[:, pl.ds(pair, 2 * step)], spread)
        return short_t + dot(low_t[:, pl.ds(pair, 2 * step)], spread)

    def short_query_grad(block):
        below = pl.ds(pl.multiple_of(block * step, step), step + TAIL)
        spread = dot(spreading(), query_high[below, :]) + dot(spreading(), query_low[below, :])
        return spread * (1.0 / SHORT)

    def window(block, carry):
        at = pl.multiple_of(block * BLOCK, BLOCK)
        here = pl.ds(at, BLOCK)
        biases = [jnp.where((z == 0) & (block + piece < reach), FAR, 0.0) for piece in range(reach + 1)]
        out_t, query_grad = window_block(
            at, pair_ref[here, 0:128], pair_ref[here, 128:256], biases, kx, vx, kxt, vxt, dkx, dvx
        )
        attn_ref[here, 0:128] = (out_t + short_out(block)).T.astype(bf16)
        attn_ref[here, 128:256] = (query_grad + short_query_grad(block)).astype(bf16)
        late = pl.ds(pl.multiple_of(WINDOW + at, BLOCK), BLOCK)
        attn_ref[late, 0:128] = (part_ref[here, 0:128] + short_out(block + reach).T).astype(bf16)
        attn_ref[late, 128:256] = (part_ref[here, 128:256] + short_query_grad(block + reach)).astype(bf16)
        return carry

    lax.fori_loop(0, reach, window, 0, unroll=4)
    fine_ref[:, 0:128] = dkx[WINDOW:, :] * SCALE
    fine_ref[:, 128:256] = dvx[WINDOW:, :]

    first = iota((TAIL, HEAD_DIM), 0) == 0
    for cols, short in ((slice(0, 128), dkc), (slice(128, 256), dvc)):
        high[0:half, cols], low[0:half, cols] = split(short[2 * coarse - half : 2 * coarse, :])
        above = jnp.where(first, short[0:TAIL, :], 0.0)
        high[half:, cols], low[half:, cols] = split(above)
    taken = spreading()
    for piece in range(reach):
        at = piece * BLOCK
        below = piece * step
        spread = dot(taken, high[below : below + step + TAIL, :])
        spread += dot(taken, low[below : below + step + TAIL, :])
        spread = spread * (1.0 / SHORT)
        back1_ref[at : at + BLOCK, 0:128] = (
            dkx[at : at + BLOCK, :] * SCALE + spread[:, 0:128]
        ).astype(bf16)
        back1_ref[at : at + BLOCK, 128:256] = (
            dvx[at : at + BLOCK, :] + spread[:, 128:256]
        ).astype(bf16)
    query_row = jnp.where(first, query_high[0:TAIL, :].astype(f32), 0.0).astype(bf16)
    back1_ref[WINDOW:base, 0:128] = query_row
    back1_ref[WINDOW:base, 128:256] = query_row
    back1_ref[base:, 0:128] = dkc[coarse : coarse + half + TAIL, :].astype(bf16)
    back1_ref[base:, 128:256] = dvc[coarse : coarse + half + TAIL, :].astype(bf16)
    for slot, ref in ((2, back2_ref), (3, back3_ref)):
        at = slot * coarse
        above = at - coarse
        for cols, short in ((slice(0, 128), dkc), (slice(128, 256), dvc)):
            ref[0:coarse, cols] = short[at : at + coarse, :].astype(bf16)
            row = jnp.where(first, short[above : above + TAIL, :], 0.0)
            ref[coarse : coarse + TAIL, cols] = row.astype(bf16)


def finish_kernel(
    sums_ref, fine_ref, coarse_ref, back1_ref, back2_ref, back3_ref, after_ref, out_ref, high, low
):
    del after_ref
    rows = sums_ref.shape[0]
    tokens = rows // PLANE_DEVS
    coarse = rows // SHORT
    half = coarse - WINDOW // SHORT
    step = BLOCK // SHORT
    base = WINDOW + TAIL
    part = half + TAIL
    ups = (back2_ref, back3_ref)
    total = coarse_ref[...]
    for up in ups:
        total += up[0:coarse, :].astype(f32)
    near = total[0:part, :] + back1_ref[base:, :].astype(f32)
    high[0:part, :], low[0:part, :] = split(near)
    high[part : part + half, :], low[part : part + half, :] = split(total[half:, :])
    extra = functools.reduce(jnp.add, [up[coarse : coarse + TAIL, :].astype(f32) for up in ups])
    high[part + half :, :], low[part + half :, :] = split(extra)
    taken = spreading()
    for block in range(rows // BLOCK):
        at = block * BLOCK
        late = at - (rows - WINDOW)
        below = block * step if late < 0 else part + late // SHORT
        spread = dot(taken, high[below : below + step + TAIL, :])
        spread += dot(taken, low[below : below + step + TAIL, :])
        result = sums_ref[at : at + BLOCK, :] + spread * (1.0 / SHORT)
        if late < 0:
            result = result + fine_ref[at : at + BLOCK, :]
        else:
            result = result + back1_ref[late : late + BLOCK, :].astype(f32)
        out_ref[block, 0:tokens, :] = result.astype(bf16)
        out_ref[block, tokens:, :] = jnp.zeros((TAIL, 256), bf16)
    out_ref[PLANE_DEVS - 1, tokens:, :] = back1_ref[WINDOW:base, :]


def unpack_kernel(pair_ref, x_ref, q_ref, k_ref, v_ref):
    tokens = q_ref.shape[0]
    last = iota((TAIL, HEAD_DIM), 0) > TAIL - SHORT
    for slot in range(q_ref.shape[1] // HEAD_DIM):
        cols = pl.ds(slot * HEAD_DIM, HEAD_DIM)
        k_ref[:, cols] = x_ref[slot, 0:tokens, 0:128]
        v_ref[:, cols] = x_ref[slot, 0:tokens, 128:256]
        q_ref[0 : tokens - TAIL, cols] = pair_ref[slot, 0 : tokens - TAIL, 128:256]
        above = jnp.sum(x_ref[slot, tokens:, 0:128].astype(f32), 0, keepdims=True) * (1.0 / SHORT)
        rest = pair_ref[slot, tokens - TAIL :, 128:256].astype(f32)
        q_ref[tokens - TAIL :, cols] = (rest + jnp.where(last, above, 0.0)).astype(bf16)


def grad_product(halves, a_ref, b_ref, w_ref, total, start):
    at = pl.program_id(0)
    depth = w_ref.shape[1]
    for piece, ref in enumerate((a_ref, b_ref)):
        for half in range(halves):

            @pl.when(at == piece * halves + half)
            def _():
                product = dot_nt(w_ref[...], ref[:, half * depth : (half + 1) * depth])
                if piece + half > 0:
                    total[...] += product
                elif start is None:
                    total[...] = product
                else:
                    total[...] = start[...] + product


def grad_near_kernel(halves, order_ref, a_ref, b_ref, w_ref, total):
    grad_product(halves, a_ref, b_ref, w_ref, total, None)


def grad_far_kernel(halves, order_ref, a_ref, b_ref, w_ref, start, q_ref, out_ref, total):
    grad_product(halves, a_ref, b_ref, w_ref, total, start)

    @pl.when(pl.program_id(0) == pl.num_programs(0) - 1)
    def _():
        last = total.shape[0] // HEAD_DIM - 1
        for slot in range(PLANE_DEVS):
            head = slice(min(slot, last) * HEAD_DIM, (min(slot, last) + 1) * HEAD_DIM)
            out_ref[slot, :, 0:128] = q_ref[:, head]
            out_ref[slot, :, 128:256] = total[head, :].T.astype(bf16)


def grad_part(pieces, order, weight, rest=()):
    rows, width = pieces[0].shape
    depth = weight.shape[0]
    halves = 1
    tile = width // halves

    first = 2 if rest else 0

    def whole(shape):
        return pl.BlockSpec(shape, lambda i, o: (0,) * len(shape))

    packed = (PLANE_DEVS, rows, 2 * HEAD_DIM)
    return pl.pallas_call(
        functools.partial(grad_far_kernel if rest else grad_near_kernel, halves),
        out_shape=jax.ShapeDtypeStruct(packed, bf16) if rest else jax.ShapeDtypeStruct((depth, rows), f32),
        grid_spec=pltpu.PrefetchScalarGridSpec(
            num_scalar_prefetch=1,
            grid=(2 * halves,),
            in_specs=[whole((rows, width))] * 2
            + [pl.BlockSpec((depth, tile), lambda i, o: (0, o[first + i // halves] * halves + i % halves))]
            + [whole(x.shape) for x in rest],
            out_specs=whole(packed if rest else (depth, rows)),
            scratch_shapes=[pltpu.VMEM((depth, rows), f32)] if rest else [],
        ),
        compiler_params=pltpu.CompilerParams(vmem_limit_bytes=64 * 1024 * 1024),
    )(order, *pieces, weight, *rest)


def project_kernel(halves, order_ref, attn_ref, w_ref, *refs):
    send_ref, keep_ref, rows_ref = refs[-3:]
    at = pl.program_id(0)
    heads = w_ref.shape[0] // HEAD_DIM
    tile = w_ref.shape[1]

    @pl.when(at == 0)
    def _():
        for slot in range(heads):
            rows_ref[:, slot * HEAD_DIM : (slot + 1) * HEAD_DIM] = attn_ref[slot, :, 0:128]

    product = dot(rows_ref[...], w_ref[...]).astype(bf16)
    for half in range(halves):

        @pl.when(at == half)
        def _():
            send_ref[:, half * tile : (half + 1) * tile] = product

        @pl.when(at == halves + half)
        def _():
            keep_ref[:, half * tile : (half + 1) * tile] = product


def project(attn, order, last, weight, width, after):
    rows = attn.shape[1]
    depth = weight.shape[0]
    halves = 1
    tile = width // halves
    out = jax.ShapeDtypeStruct((rows, width), bf16)
    return pl.pallas_call(
        functools.partial(project_kernel, halves),
        out_shape=(out, out),
        grid_spec=pltpu.PrefetchScalarGridSpec(
            num_scalar_prefetch=1,
            grid=(2 * halves,),
            in_specs=[
                pl.BlockSpec(attn.shape, lambda i, o: (0, 0, 0)),
                pl.BlockSpec((depth, tile), lambda i, o: (0, o[last - i // halves] * halves + i % halves)),
            ]
            + [pl.BlockSpec(memory_space=pltpu.HBM)] * len(after),
            out_specs=[pl.BlockSpec((rows, width), lambda i, o: (0, 0))] * 2,
            scratch_shapes=[pltpu.VMEM((rows, depth), bf16)],
        ),
        compiler_params=pltpu.CompilerParams(vmem_limit_bytes=64 * 1024 * 1024),
    )(order, attn, weight, *after)


def swap(x, axis):
    return lax.ppermute(x, axis, [(0, 1), (1, 0)])


def planes_up(x, by):
    return lax.ppermute(x, "z", [(i, i + by) for i in range(PLANES) if 0 <= i + by < PLANES])


def in_plane(x):
    return lax.all_to_all(x, PLANE, 0, 0, tiled=True)


def column_blocks():
    xl, core = lax.axis_index("xl"), lax.axis_index("c")
    own, other = 2 * xl, 2 * (1 - xl)
    return jnp.stack([own + core, own + 1 - core, other + core, other + 1 - core]).astype(jnp.int32)


def gathered_grad(out_grad, out_weight, q_proj, blocks):
    far = swap(out_grad, "xl")
    near = swap(out_grad, "c")
    start = grad_part((out_grad, near), blocks, out_weight)
    far, start = lax.optimization_barrier((far, start))
    both = swap(far, "c")
    return start, grad_part((far, both), blocks, out_weight, (start, q_proj))


def projected(attn, out_weight, width, blocks, last, after):
    send, keep = project(attn, blocks, last, out_weight, width, after)
    return keep.astype(f32) + swap(send, "c").astype(f32), keep


def shards(q_proj, k_proj, v_proj, out_weight, out_grad):
    tokens, cols = q_proj.shape
    rows = tokens * PLANE_DEVS
    coarse = rows // SHORT
    total = PLANES * coarse
    z = lax.axis_index("z").astype(jnp.int32).reshape(1)

    def array(*shape, dtype=bf16):
        return jax.ShapeDtypeStruct(shape, dtype)

    in_place = pl.BlockSpec(memory_space=pltpu.HBM)
    whole = pl.BlockSpec(memory_space=pltpu.VMEM)
    packed = call(
        pack_kernel,
        array(PLANE_DEVS, tokens + TAIL, 2 * HEAD_DIM),
        62,
        in_specs=[in_place] * 3,
        out_specs=whole,
        scratch_shapes=[pltpu.SemaphoreType.DMA((PLANE_DEVS, 4))],
    )(q_proj, k_proj, v_proj)
    own = in_plane(packed)
    blocks = column_blocks()
    early, pair_packed = gathered_grad(out_grad, out_weight, q_proj, blocks)
    near_rows = WINDOW + 2 * TAIL + WINDOW // SHORT
    near, far = call(
        pool_kernel,
        (array(near_rows, 256), array(coarse + TAIL, 256)),
        16,
        in_specs=[whole, in_place],
    )(own, early)
    near_in = planes_up(near, 1)
    far2_in = planes_up(far, 2)
    far3_in = planes_up(far, 3)
    pair = in_plane(pair_packed).reshape(rows, 2 * HEAD_DIM)

    part, sums = call(
        own_kernel,
        (array(rows - WINDOW, 256, dtype=f32), array(rows, 256, dtype=f32)),
        64,
        in_specs=[whole] * 2,
        out_specs=[whole] * 2,
        scratch_shapes=[pltpu.VMEM((rows, HEAD_DIM), bf16)] * 2
        + [pltpu.VMEM((HEAD_DIM, rows), bf16)] * 2
        + [pltpu.VMEM((rows, HEAD_DIM), f32)] * 2,
    )(own, pair)
    attn, fine, short, back1, back2, back3 = call(
        attention_kernel,
        (
            array(rows, 256),
            array(rows - WINDOW, 256, dtype=f32),
            array(coarse, 256, dtype=f32),
            array(near_rows, 256),
            array(coarse + TAIL, 256),
            array(coarse + TAIL, 256),
        ),
        64,
        in_specs=[pl.BlockSpec(memory_space=pltpu.SMEM)] + [whole] * 7,
        out_specs=[whole] * 6,
        scratch_shapes=[
            pltpu.VMEM((rows, HEAD_DIM), bf16),
            pltpu.VMEM((rows, HEAD_DIM), bf16),
            pltpu.VMEM((HEAD_DIM, rows), bf16),
            pltpu.VMEM((HEAD_DIM, rows), bf16),
            pltpu.VMEM((total, HEAD_DIM), bf16),
            pltpu.VMEM((total, HEAD_DIM), bf16),
            pltpu.VMEM((HEAD_DIM, total), bf16),
            pltpu.VMEM((HEAD_DIM, total), bf16),
            pltpu.VMEM((coarse, HEAD_DIM), bf16),
            pltpu.VMEM((coarse, HEAD_DIM), bf16),
            pltpu.VMEM((rows, HEAD_DIM), f32),
            pltpu.VMEM((rows, HEAD_DIM), f32),
            pltpu.VMEM((total, HEAD_DIM), f32),
            pltpu.VMEM((total, HEAD_DIM), f32),
            pltpu.VMEM((HEAD_DIM, coarse), bf16),
            pltpu.VMEM((HEAD_DIM, coarse), bf16),
            pltpu.VMEM((WINDOW // SHORT + TAIL, 256), bf16),
            pltpu.VMEM((WINDOW // SHORT + TAIL, 256), bf16),
            pltpu.VMEM((coarse + TAIL, HEAD_DIM), bf16),
            pltpu.VMEM((coarse + TAIL, HEAD_DIM), bf16),
        ],
    )(z, own, far, near_in, far2_in, far3_in, pair, part)

    back1_in = planes_up(back1, -1)
    back2_in = planes_up(back2, -2)
    back3_in = planes_up(back3, -3)
    attn_in = in_plane(attn.reshape(PLANE_DEVS, tokens, 256))
    width = out_grad.shape[1]
    part, kept = projected(attn_in, out_weight, width, blocks, 1, ())
    finished = call(
        finish_kernel,
        array(PLANE_DEVS, tokens + TAIL, 256),
        64,
        in_specs=[whole] * 6 + [in_place],
        scratch_shapes=[
            pltpu.VMEM((coarse + 2 * TAIL, 256), bf16),
            pltpu.VMEM((coarse + 2 * TAIL, 256), bf16),
        ],
    )(sums, fine, short, back1_in, back2_in, back3_in, kept)
    other, _ = projected(attn_in, out_weight, width, blocks, 3, (finished,))
    mixed_out = (part + swap(other.astype(bf16), "xl").astype(f32)).astype(bf16)
    returned = in_plane(finished)
    grads = call(unpack_kernel, (array(tokens, cols),) * 3, 16)(attn_in, returned)
    return (mixed_out, *grads)


def solution(mesh):
    fine_mesh = Mesh(np.asarray(mesh.devices).reshape(4, 4, 2, 2, 2), ("z", "y", "xh", "xl", "c"))
    both = P(("z", "y", "xh"), ("xl", "c"))
    in_specs = (both, both, both, P(("xl", "c"), None), both)
    return jax.shard_map(
        shards, mesh=fine_mesh, in_specs=in_specs, out_specs=(both,) * 4, check_vma=False
    )
```
